256 devices in a mesh: ctx: 32 (over y, z_lo, core), tp: 8 (over x, z_hi).
Axes of the slice: x: 4, y: 4, z: 8 (z_hi: 2, z_lo: 4; z = z_hi * 4 + z_lo), core: 2. Of those that a mesh axis runs over, the one named last changes fastest.
Arguments:
- inputs: bfloat16 [16384, 1024], P('ctx', 'tp'), may hold values from -0.09375 to 0.09375
- grad_out: bfloat16 [16384, 1024], P('ctx', 'tp'), may hold values from -6 to 6
- filters: bfloat16 [12, 4096], replicated, may hold values from -0.09375 to 0.09375
- projection: bfloat16 [1024, 12, 1024], P(None, None, 'tp'), may hold values from -0.078125 to 0.078125
Outputs:
- grad_input: bfloat16 [16384, 1024], P('ctx', 'tp')
- grad_proj: float32 [1024, 12, 1024], P('ctx', None, 'tp')
The draws below stay inside these ranges and needn't reach their ends.
All inputs are finite; a program needn't handle non-finite values.
Results may differ from the reference program's by a relative error of at most 0.0049.
Values may be sent and summed in bfloat16 or wider, within the bound.
No kernel may reach another device: no remote copies, remote signals or barrier semaphores. Data moves between devices by JAX's collectives and lax.ppermute only.
A program may use at most 128 MiB of HBM per device.

```python
import jax
import jax.numpy as jnp
from jax import lax

D = 1024
K = 12
FILT = 4096
TOK_DEV = 512
TOKENS = 16384


def spiked(values, rng, source, target, blocks, factor):
    def block_of(dim):
        return (jnp.arange(values.shape[dim]) // (values.shape[dim] // blocks)).reshape((-1,) + (1,) * (values.ndim - 1 - dim))

    first = jax.random.permutation(rng, blocks)[block_of(target)]
    second = (block_of(target) + blocks // 2) % blocks
    return jnp.where((block_of(source) == first) | (block_of(source) == second), factor * values, values)


def level_of(rng, shape, shards, low, largest):
    gain, own = 1.0, jax.random.fold_in(rng, 6)
    for axis_at, parts in shards:
        heights = jnp.exp(jax.random.uniform(jax.random.fold_in(own, axis_at), (parts,), jnp.float32, low / len(shards), largest / len(shards)))
        gain = gain * jnp.repeat(heights, shape[axis_at] // parts).reshape([-1 if axis == axis_at else 1 for axis in range(len(shape))])
    return gain


def centred(rng, dims, deviation, bound, cuts=(), kind=jnp.bfloat16):
    level = level_of(rng, dims, cuts, -0.22, 0.18) if cuts else 1.0
    result = jax.random.normal(rng, dims, jnp.float32) * deviation * level
    return jnp.minimum(jnp.maximum(result, -bound), bound).astype(kind)


def heavy_noise(key, shape, width, limit, pieces, heavy, kind=jnp.bfloat16):
    drawn = width * jax.random.normal(key, shape, jnp.float32)
    if pieces:
        drawn = drawn * level_of(key, shape, pieces, -0.22, 0.18)
    return jnp.clip(spiked(drawn, jax.random.fold_in(key, 3), *heavy), -limit, limit).astype(kind)


def setup_inputs(seed: int = 0) -> dict:
    streams_of = jax.random.split(jax.random.key(seed), 5)
    inputs = heavy_noise(streams_of[0], (TOKENS, D), (TOKENS ** -0.5), 0.09375, ((0, 32), (1, 8)), (0, 1, 32, 2.75))
    grad_out = centred(streams_of[1], (TOKENS, D), 1.0, 6.0, ((0, 32), (1, 8)))
    filters = centred(streams_of[2], (K, FILT), FILT ** -0.5, 0.09375)
    projection = heavy_noise(streams_of[3], (D, K, D), (K * D) ** -0.5, 0.078125, ((2, 8),), (2, 0, 8, 2.0))
    return dict(inputs=inputs, grad_out=grad_out, filters=filters, projection=projection)


def reference(inputs, grad_out, filters, projection):
    tok_rows = TOK_DEV
    lag_reach = FILT // tok_rows
    block_count = TOKENS // tok_rows
    wide_filters = filters.astype(jnp.float32)
    zero_edge = jnp.zeros((K, tok_rows), jnp.float32)
    padded_filters = jnp.concatenate([zero_edge, wide_filters, zero_edge], axis=1)
    rows_index = jnp.arange(tok_rows, dtype=jnp.int32)
    offsets = rows_index[None, :] - rows_index[:, None] + tok_rows
    tables = []
    for lag_index in range(lag_reach + 1):
        tables.append(jnp.take(padded_filters, offsets + lag_index * tok_rows, axis=1))
    tables = jnp.stack(tables, axis=0)
    wide_grad = grad_out.astype(jnp.float32)
    grad_padded = jnp.concatenate([wide_grad, jnp.zeros((FILT, D), jnp.float32)], axis=0)
    wide_inputs = inputs.astype(jnp.float32)
    wide_proj = projection.astype(jnp.float32)

    def per_block(grad_proj, block_index):
        running = jnp.zeros((K, tok_rows, D), jnp.float32)
        for lag_index in range(lag_reach + 1):
            start = ((block_index + lag_index) * tok_rows).astype(jnp.int32)
            grad_block = lax.dynamic_slice_in_dim(grad_padded, start, tok_rows, 0)
            running = running + jnp.einsum("kab,bc->kac", tables[lag_index], grad_block, precision=lax.Precision.HIGHEST, preferred_element_type=jnp.float32)
        correlated = running.astype(jnp.bfloat16).astype(jnp.float32)
        grad_block_in = jnp.einsum("ikc,ktc->ti", wide_proj, correlated, precision=lax.Precision.HIGHEST, preferred_element_type=jnp.float32)
        in_block = lax.dynamic_slice_in_dim(wide_inputs, (block_index * tok_rows).astype(jnp.int32), tok_rows, 0)
        grad_proj = grad_proj + jnp.einsum("ti,ktc->ikc", in_block, correlated, precision=lax.Precision.HIGHEST, preferred_element_type=jnp.float32)
        return grad_proj, grad_block_in.astype(jnp.bfloat16)

    grad_proj, grad_blocks = lax.scan(per_block, jnp.zeros((D, K, D), jnp.float32), jnp.arange(block_count, dtype=jnp.int32))
    return grad_blocks.reshape(TOKENS, D), grad_proj
```

```python
import functools

import jax
import jax.numpy as jnp
from jax import lax
from jax.experimental import pallas as pl
from jax.experimental.pallas import tpu as pltpu
from jax.sharding import PartitionSpec as P

BF16, F32 = jnp.bfloat16, jnp.float32
ROWS = 64
LANE = 128
NX, NZ_HI, NY, NZ_LO, NCORE = 4, 2, 4, 4, 2
CHIPS = NY * NZ_LO
VMEM_LIMIT = 48 * 1024 * 1024


def ctx_of(y, z, core):
    return (y * NZ_LO + z) * NCORE + core


CTX = [(y, z, core) for y in range(NY) for z in range(NZ_LO) for core in range(NCORE)]
TP = [(x, z) for x in range(NX) for z in range(NZ_HI)]
CORE_SWAP = [(ctx_of(y, z, c), ctx_of(y, z, 1 - c)) for y, z, c in CTX]
Z_HI_SWAP = [(x * NZ_HI + z, x * NZ_HI + 1 - z) for x, z in TP]


def along_y(steps):
    return [(ctx_of(y, z, c), ctx_of((y + steps) % NY, z, c)) for y, z, c in CTX]


def along_z(steps):
    return [(ctx_of(y, z, c), ctx_of(y, (z + steps) % NZ_LO, c)) for y, z, c in CTX]


def along_x(steps):
    return [(x * NZ_HI + z, (x + steps) % NX * NZ_HI + z) for x, z in TP]


def from_later_chip(steps):
    return [
        (NCORE * (chip + steps) + core, NCORE * chip + core)
        for chip in range(CHIPS - steps)
        for core in range(NCORE)
    ]


def table_kernel(filters_ref, table_ref):
    filt_count, rows, width = table_ref.shape
    taps = filters_ref.shape[1]
    for k in range(filt_count):
        line = filters_ref[k : k + 1, :].astype(F32)
        line = jnp.concatenate([line, jnp.zeros((1, width - taps), F32)], axis=1)
        block = jnp.broadcast_to(line, (rows, width))
        table_ref[k] = pltpu.roll(block, 0, 1, stride=1, stride_axis=0).astype(BF16)


def toeplitz_tables(filters):
    filt_count, taps = filters.shape
    width = taps + LANE
    return pl.pallas_call(
        table_kernel,
        out_shape=jax.ShapeDtypeStruct((filt_count, ROWS, width), BF16),
        in_specs=[pl.BlockSpec(memory_space=pltpu.VMEM)],
        out_specs=pl.BlockSpec(memory_space=pltpu.VMEM),
        compiler_params=pltpu.CompilerParams(vmem_limit_bytes=VMEM_LIMIT),
        cost_estimate=pl.CostEstimate(flops=30_000_000, bytes_accessed=7_000_000, transcendentals=0),
        name="tables",
    )(filters)


def conv_kernel(
    pos_ref, table_ref, own_ref, r1_ref, r2_ref, r3_ref, r4_ref, swapped_ref,
    x0_ref, x1_ref, x2_ref, x3_ref,
    corr_ref, keep_ref, send_ref, grad_ref, full_ref,
):
    filt_count, rows, width = table_ref.shape
    tok = own_ref.shape[0]
    x, z_hi, y, z_lo, core = (pos_ref[i] for i in range(5))
    received = (own_ref, r1_ref, r2_ref, r3_ref, r4_ref)
    for s, part in enumerate(received):
        grad_ref[2 * s * tok : (2 * s + 1) * tok, :] = part[...]
    for s in range(4):
        grad_ref[(2 * s + 1) * tok : (2 * s + 2) * tok, :] = swapped_ref[s]
    grad_ref[9 * tok :, :] = jnp.zeros((grad_ref.shape[0] - 9 * tok, LANE), BF16)

    table = table_ref[...].reshape(filt_count * rows, width)

    @pl.loop(0, tok // (2 * rows))
    def _(pair):
        start = pl.multiple_of(pair * (2 * rows), 2 * rows)
        first = grad_ref[pl.ds(start, width), :]
        second = grad_ref[pl.ds(start + rows, width), :]
        both = jnp.concatenate([first, second], axis=1)
        result = jnp.dot(table, both, preferred_element_type=F32).astype(BF16)
        for k in range(filt_count):
            for half in range(2):
                corr_ref[pl.ds(start + half * rows, rows), k * LANE : (k + 1) * LANE] = result[
                    k * rows : (k + 1) * rows, half * LANE : (half + 1) * LANE
                ]

    for s, part in enumerate((x0_ref, x1_ref, x2_ref, x3_ref)):
        for h in range(NZ_HI):
            at = lax.rem(x + NX - s, NX) * NZ_HI + lax.rem(z_hi + h, NZ_HI)
            full_ref[:, pl.ds(pl.multiple_of(at * LANE, LANE), LANE)] = part[h]

    deep = NZ_LO * NCORE * 32

    @pl.loop(0, NY)
    def _(s):
        at = lax.rem(y + s, NY)
        part = full_ref[:, pl.ds(pl.multiple_of(at * deep, deep), deep)]
        result = lax.dot_general(
            part, corr_ref[...], (((0,), (0,)), ((), ())), preferred_element_type=F32
        ).astype(BF16)
        for z in range(NZ_LO):
            slot = lax.rem(z + NZ_LO - z_lo, NZ_LO)
            for k in range(filt_count):
                columns = slice(k * LANE, (k + 1) * LANE)
                even = result[z * 64 : z * 64 + 32, columns]
                odd = result[z * 64 + 32 : z * 64 + 64, columns]
                keep_ref[s, slot, k] = jnp.where(core == 0, even, odd)
                send_ref[s, slot, k] = jnp.where(core == 0, odd, even)


def conv_and_product(pos, table, halo, swapped, gathered):
    filt_count, rows, width = table.shape
    tok = halo[0].shape[0]
    part = jax.ShapeDtypeStruct((NY, NZ_LO, filt_count, 32, LANE), BF16)
    vmem = pl.BlockSpec(memory_space=pltpu.VMEM)
    flops = 2 * filt_count * (rows * width * (tok // rows) * LANE + tok * LANE * 1024)
    return pl.pallas_call(
        conv_kernel,
        out_shape=(jax.ShapeDtypeStruct((tok, filt_count * LANE), BF16), part, part),
        in_specs=[pl.BlockSpec(memory_space=pltpu.SMEM)] + [vmem] * 11,
        out_specs=(vmem,) * 3,
        scratch_shapes=[
            pltpu.VMEM((9 * tok + rows, LANE), BF16),
            pltpu.VMEM((tok, 1024), BF16),
        ],
        compiler_params=pltpu.CompilerParams(vmem_limit_bytes=VMEM_LIMIT),
        cost_estimate=pl.CostEstimate(flops=flops, bytes_accessed=8_000_000, transcendentals=0),
        name="conv_product",
    )(pos, table, *halo, swapped, *gathered)


def share_kernel(pos_ref, *refs):
    corr_refs, proj_ref, slot_refs, all_ref = refs[:-6], refs[-6], refs[-5:-1], refs[-1]
    filt_count = proj_ref.shape[0]
    x, z_hi = pos_ref[0], pos_ref[1]
    at = 0
    for part in corr_refs:
        all_ref[:, at : at + part.shape[1]] = part[...]
        at += part.shape[1]
    wide = NZ_HI * LANE
    for s, slot_ref in enumerate(slot_refs):
        base = pl.multiple_of(lax.rem(x + s, NX) * wide, wide)
        weights = jnp.concatenate(
            [proj_ref[k, pl.ds(base, wide), :] for k in range(filt_count)], axis=1
        )
        result = lax.dot_general(
            all_ref[...], weights, (((1,), (1,)), ((), ())), preferred_element_type=F32
        ).astype(BF16)
        low, high = result[:, :LANE], result[:, LANE:]
        slot_ref[0] = jnp.where(z_hi == 0, low, high)
        slot_ref[1] = jnp.where(z_hi == 0, high, low)


def input_shares(pos, corrs, projection):
    tok = corrs[0].shape[0]
    filt_count, channels, _ = projection.shape
    vmem = pl.BlockSpec(memory_space=pltpu.VMEM)
    return pl.pallas_call(
        share_kernel,
        out_shape=(jax.ShapeDtypeStruct((NZ_HI, tok, LANE), BF16),) * NX,
        in_specs=[pl.BlockSpec(memory_space=pltpu.SMEM)] + [vmem] * (len(corrs) + 1),
        out_specs=(vmem,) * NX,
        scratch_shapes=[pltpu.VMEM((tok, filt_count * LANE), BF16)],
        compiler_params=pltpu.CompilerParams(vmem_limit_bytes=VMEM_LIMIT),
        cost_estimate=pl.CostEstimate(
            flops=2 * tok * filt_count * LANE * channels, bytes_accessed=6_000_000, transcendentals=0
        ),
        name="input_shares",
    )(pos, *corrs, projection)


GROUPS = 2


def per_device(inputs, grad_out, filters, projection):
    filt_count = filters.shape[0]
    tp, ctx = lax.axis_index("tp"), lax.axis_index("ctx")
    core = ctx % NCORE
    pos = jnp.stack(
        [tp // NZ_HI, tp % NZ_HI, ctx // (NCORE * NZ_LO), ctx // NCORE % NZ_LO, core]
    ).astype(jnp.int32)

    later = [lax.ppermute(grad_out, "ctx", from_later_chip(s)) for s in range(1, 5)]
    pair = jnp.stack([inputs, lax.ppermute(inputs, "tp", Z_HI_SWAP)])
    gathered = [pair] + [lax.ppermute(pair, "tp", along_x(s)) for s in range(1, NX)]
    tables = toeplitz_tables(filters)
    halo = [grad_out] + later
    sent = jnp.stack([jnp.where(core == 0, halo[s + 1], halo[s]) for s in range(4)])
    swapped = lax.ppermute(sent, "ctx", CORE_SWAP)

    per_group = filt_count // GROUPS
    corrs, gradients = [], []
    for group in range(GROUPS):
        table = tables[group * per_group : (group + 1) * per_group]
        corr, keep, send = conv_and_product(pos, table, halo, swapped, gathered)
        corrs.append(corr)
        other = lax.ppermute(send, "ctx", CORE_SWAP)
        chip_sum = [keep[s].astype(F32) + other[s].astype(F32) for s in range(NY)]
        column = chip_sum[0]
        for s in range(1, NY):
            column += lax.ppermute(chip_sum[s].astype(BF16), "ctx", along_y(s)).astype(F32)
        total = column[0]
        for s in range(1, NZ_LO):
            total += lax.ppermute(column[s].astype(BF16), "ctx", along_z(s)).astype(F32)
        gradients.append(total)
    grad_proj = jnp.concatenate(gradients, axis=0).transpose(1, 0, 2)

    shares = input_shares(pos, corrs, projection.transpose(1, 0, 2))
    both = shares[0].astype(F32)
    for s in range(1, NX):
        both += lax.ppermute(shares[s], "tp", along_x(s)).astype(F32)
    far = lax.ppermute(both[1].astype(BF16), "tp", Z_HI_SWAP)
    grad_input = (both[0] + far.astype(F32)).astype(BF16)
    return grad_input, grad_proj


def solution(mesh):
    return jax.shard_map(
        per_device,
        mesh=mesh,
        in_specs=(P("ctx", "tp"), P("ctx", "tp"), P(), P(None, None, "tp")),
        out_specs=(P("ctx", "tp"), P("ctx", None, "tp")),
        check_vma=False,
    )
```

```python
import functools

import jax
import jax.numpy as jnp
from jax import lax
from jax.experimental import pallas as pl
from jax.experimental.pallas import tpu as pltpu
from jax.sharding import PartitionSpec as P

BF16, F32 = jnp.bfloat16, jnp.float32
ROWS = 64
LANE = 128
NX, NZ_HI, NY, NZ_LO, NCORE = 4, 2, 4, 4, 2
CHIPS = NY * NZ_LO
VMEM_LIMIT = 20 * 1024 * 1024
LARGE_COST = pl.CostEstimate(flops=4_000_000_000, bytes_accessed=8_000_000, transcendentals=0)
SMALL_COST = pl.CostEstimate(flops=1000, bytes_accessed=1000, transcendentals=0)


def ctx_of(y, z, core):
    return (y * NZ_LO + z) * NCORE + core


CTX = [(y, z, core) for y in range(NY) for z in range(NZ_LO) for core in range(NCORE)]
TP = [(x, z) for x in range(NX) for z in range(NZ_HI)]
CORE_SWAP = [(ctx_of(y, z, c), ctx_of(y, z, 1 - c)) for y, z, c in CTX]
Z_HI_SWAP = [(x * NZ_HI + z, x * NZ_HI + 1 - z) for x, z in TP]


def ring_partner(at, crossed):
    return NX - 1 - at if crossed else at ^ 1


def ring_slots(at, crossed):
    near, far = ring_partner(at, crossed), ring_partner(at, not crossed)
    return at, far, near, ring_partner(near, not crossed)


def y_swap(crossed):
    return [(ctx_of(y, z, c), ctx_of(ring_partner(y, crossed), z, c)) for y, z, c in CTX]


def x_swap(crossed):
    return [(x * NZ_HI + z, ring_partner(x, crossed) * NZ_HI + z) for x, z in TP]


def z_swap(bit):
    return [(ctx_of(y, z, c), ctx_of(y, z ^ bit, c)) for y, z, c in CTX]


def along_x(steps):
    return [(x * NZ_HI + z, (x + steps) % NX * NZ_HI + z) for x, z in TP]


def from_later_chip(steps):
    return [
        (NCORE * (chip + steps) + core, NCORE * chip + core)
        for chip in range(CHIPS - steps)
        for core in range(NCORE)
    ]


def table_kernel(filters_ref, near_ref, *far_refs):
    filt_count, rows, near = near_ref.shape
    per_group, _, far = far_refs[0].shape
    taps = filters_ref.shape[1]
    width = near + far
    for k in range(filt_count):
        line = filters_ref[k : k + 1, :].astype(F32)
        line = jnp.concatenate([line, jnp.zeros((1, width - taps), F32)], axis=1)
        block = jnp.broadcast_to(line, (rows, width))
        block = pltpu.roll(block, 0, 1, stride=1, stride_axis=0).astype(BF16)
        near_ref[k] = block[:, :near]
        far_refs[k // per_group][k % per_group] = block[:, near:]


def toeplitz_tables(filters, groups):
    filt_count, taps = filters.shape
    near, far = taps // 2, taps // 2 + LANE
    vmem = pl.BlockSpec(memory_space=pltpu.VMEM)
    outs = [jax.ShapeDtypeStruct((filt_count, ROWS, near), BF16)]
    outs += [jax.ShapeDtypeStruct((filt_count // groups, ROWS, far), BF16)] * groups
    return pl.pallas_call(
        table_kernel,
        out_shape=outs,
        in_specs=[vmem],
        out_specs=[vmem] * (1 + groups),
        compiler_params=pltpu.CompilerParams(vmem_limit_bytes=VMEM_LIMIT),
        cost_estimate=LARGE_COST,
        name="tables",
    )(filters)


def pair_of_blocks(grad_ref, start, rows, width):
    first = grad_ref[pl.ds(start, width), :]
    second = grad_ref[pl.ds(start + rows, width), :]
    return jnp.concatenate([first, second], axis=1)


def near_kernel(table_ref, own_ref, r1_ref, r2_ref, swapped_ref, *refs):
    acc_refs, grad_ref = refs[:-1], refs[-1]
    filt_count, rows, width = table_ref.shape
    tok = own_ref.shape[0]
    for s, part in enumerate((own_ref, r1_ref, r2_ref)):
        grad_ref[2 * s * tok : (2 * s + 1) * tok, :] = part[...]
    for s in range(2):
        grad_ref[(2 * s + 1) * tok : (2 * s + 2) * tok, :] = swapped_ref[s]
    table = table_ref[...].reshape(filt_count * rows, width)

    @pl.loop(0, tok // (2 * rows))
    def _(pair):
        start = pl.multiple_of(pair * (2 * rows), 2 * rows)
        both = pair_of_blocks(grad_ref, start, rows, width)
        result = jnp.dot(table, both, preferred_element_type=F32)
        part = acc_refs[0].shape[1]
        for group, acc_ref in enumerate(acc_refs):
            acc_ref[pair] = result[group * part : (group + 1) * part]


def near_conv(table, near_halo, swapped, groups):
    filt_count, rows, width = table.shape
    tok = near_halo[0].shape[0]
    vmem = pl.BlockSpec(memory_space=pltpu.VMEM)
    acc = jax.ShapeDtypeStruct((tok // (2 * rows), filt_count // groups * rows, 2 * LANE), F32)
    return pl.pallas_call(
        near_kernel,
        out_shape=[acc] * groups,
        in_specs=[vmem] * 5,
        out_specs=[vmem] * groups,
        scratch_shapes=[pltpu.VMEM((5 * tok, LANE), BF16)],
        compiler_params=pltpu.CompilerParams(vmem_limit_bytes=VMEM_LIMIT),
        cost_estimate=LARGE_COST,
        name="near_conv",
    )(table, *near_halo, swapped)


def conv_kernel(
    crossed, pos_ref, table_ref, acc_ref, r2_ref, r3_ref, r4_ref, swapped_ref,
    x0_ref, x1_ref, x2_ref, x3_ref,
    corr_ref, keep_ref, send_ref, grad_ref, full_ref,
):
    filt_count, rows, width = table_ref.shape
    tok = r2_ref.shape[0]
    x, z_hi = pos_ref[0] // NZ_HI, lax.rem(pos_ref[0], NZ_HI)
    y, z_lo, core = pos_ref[1] // (NZ_LO * NCORE), lax.rem(pos_ref[1] // NCORE, NZ_LO), lax.rem(pos_ref[1], NCORE)
    for s, part in enumerate((r2_ref, r3_ref, r4_ref)):
        grad_ref[2 * s * tok : (2 * s + 1) * tok, :] = part[...]
    for s in range(2):
        grad_ref[(2 * s + 1) * tok : (2 * s + 2) * tok, :] = swapped_ref[s]
    grad_ref[5 * tok :, :] = jnp.zeros((grad_ref.shape[0] - 5 * tok, LANE), BF16)
    table = table_ref[...].reshape(filt_count * rows, width)

    @pl.loop(0, tok // (2 * rows))
    def _(pair):
        start = pl.multiple_of(pair * (2 * rows), 2 * rows)
        both = pair_of_blocks(grad_ref, start, rows, width)
        result = jnp.dot(table, both, preferred_element_type=F32)
        result = (result + acc_ref[pair]).astype(BF16)
        for k in range(filt_count):
            for half in range(2):
                corr_ref[pl.ds(start + half * rows, rows), k * LANE : (k + 1) * LANE] = result[
                    k * rows : (k + 1) * rows, half * LANE : (half + 1) * LANE
                ]

    for s, part in enumerate((x0_ref, x1_ref, x2_ref, x3_ref)):
        for h in range(NZ_HI):
            at = lax.rem(x + NX - s, NX) * NZ_HI + lax.rem(z_hi + h, NZ_HI)
            full_ref[:, pl.ds(pl.multiple_of(at * LANE, LANE), LANE)] = part[h]

    deep = NZ_LO * NCORE * 32

    for s, at in enumerate(ring_slots(y, crossed)):
        part = full_ref[:, pl.ds(pl.multiple_of(at * deep, deep), deep)]
        result = lax.dot_general(
            part, corr_ref[...], (((0,), (0,)), ((), ())), preferred_element_type=F32
        ).astype(BF16)
        for z in range(NZ_LO):
            slot = z ^ z_lo
            for k in range(filt_count):
                columns = slice(k * LANE, (k + 1) * LANE)
                even = result[z * 64 : z * 64 + 32, columns]
                odd = result[z * 64 + 32 : z * 64 + 64, columns]
                keep_ref[s, slot, k] = jnp.where(core == 0, even, odd)
                send_ref[s, slot, k] = jnp.where(core == 0, odd, even)


def conv_and_product(crossed, pos, table, acc, far_halo, swapped, gathered):
    filt_count, rows, width = table.shape
    tok = far_halo[0].shape[0]
    part = jax.ShapeDtypeStruct((NY, NZ_LO, filt_count, 32, LANE), BF16)
    vmem = pl.BlockSpec(memory_space=pltpu.VMEM)
    return pl.pallas_call(
        functools.partial(conv_kernel, crossed),
        out_shape=(jax.ShapeDtypeStruct((tok, filt_count * LANE), BF16), part, part),
        in_specs=[pl.BlockSpec(memory_space=pltpu.SMEM)] + [vmem] * 10,
        out_specs=(vmem,) * 3,
        scratch_shapes=[
            pltpu.VMEM((5 * tok + rows, LANE), BF16),
            pltpu.VMEM((tok, 1024), BF16),
        ],
        compiler_params=pltpu.CompilerParams(vmem_limit_bytes=VMEM_LIMIT),
        cost_estimate=SMALL_COST,
        name="conv_product",
    )(pos, table, acc, *far_halo, swapped, *gathered)


def share_kernel(pos_ref, _, *refs):
    corr_refs, proj_ref = refs[:-6], refs[-6]
    near_keep, near_send, far_keep, far_send, all_ref = refs[-5:]
    filt_count = proj_ref.shape[0]
    x, z_hi = pos_ref[0] // NZ_HI, lax.rem(pos_ref[0], NZ_HI)
    at = 0
    for part in corr_refs:
        all_ref[:, at : at + part.shape[1]] = part[...]
        at += part.shape[1]
    wide = NZ_HI * LANE
    near_slots = (near_keep, 0), (near_send, 0), (near_keep, 1), (near_send, 1)
    far_slots = (far_keep, 0), (far_keep, 1), (far_send, 0), (far_send, 1)
    for at, near, far in zip(ring_slots(x, False), near_slots, far_slots):
        base = pl.multiple_of(at * wide, wide)
        weights = jnp.concatenate(
            [proj_ref[k, pl.ds(base, wide), :] for k in range(filt_count)], axis=1
        )
        result = lax.dot_general(
            all_ref[...], weights, (((1,), (1,)), ((), ())), preferred_element_type=F32
        )
        low, high = result[:, :LANE], result[:, LANE:]
        near[0][near[1]] = jnp.where(z_hi == 0, low, high).astype(near[0].dtype)
        far[0][far[1]] = jnp.where(z_hi == 0, high, low).astype(far[0].dtype)


def input_shares(pos, after, corrs, projection):
    tok = corrs[0].shape[0]
    filt_count = projection.shape[0]
    vmem = pl.BlockSpec(memory_space=pltpu.VMEM)
    keep = jax.ShapeDtypeStruct((2, tok, LANE), F32)
    send = jax.ShapeDtypeStruct((2, tok, LANE), BF16)
    return pl.pallas_call(
        share_kernel,
        out_shape=(keep, send, keep, send),
        in_specs=[pl.BlockSpec(memory_space=pltpu.SMEM), pl.BlockSpec(memory_space=pl.ANY)]
        + [vmem] * (len(corrs) + 1),
        out_specs=(vmem,) * 4,
        scratch_shapes=[pltpu.VMEM((tok, filt_count * LANE), BF16)],
        compiler_params=pltpu.CompilerParams(vmem_limit_bytes=VMEM_LIMIT),
        cost_estimate=SMALL_COST,
        name="input_shares",
    )(pos, after, *corrs, projection)


GROUPS = 2


def per_device(inputs, grad_out, filters, projection):
    tp, ctx = lax.axis_index("tp"), lax.axis_index("ctx")
    first_core = lax.rem(ctx, NCORE) == 0
    pos = jnp.stack([tp, ctx]).astype(jnp.int32)

    halo = [grad_out] + [lax.ppermute(grad_out, "ctx", from_later_chip(s)) for s in range(1, 5)]
    pair = jnp.stack([inputs, lax.ppermute(inputs, "tp", Z_HI_SWAP)])
    gathered = [pair] + [lax.ppermute(pair, "tp", along_x(s)) for s in range(1, NX)]
    near_table, *far_tables = toeplitz_tables(filters, GROUPS)
    swapped = []
    for at in (0, 2):
        sent = jnp.stack([jnp.where(first_core, halo[s + 1], halo[s]) for s in (at, at + 1)])
        swapped.append(lax.ppermute(sent, "ctx", CORE_SWAP))
    accs = near_conv(near_table, halo[:3], swapped[0], GROUPS)

    corrs, columns = [], []
    for group, (table, acc) in enumerate(zip(far_tables, accs)):
        crossed = group % 2 == 1
        corr, keep, send = conv_and_product(
            crossed, pos, table, acc, halo[2:], swapped[1], gathered
        )
        corrs.append(corr)
        other = lax.ppermute(send, "ctx", CORE_SWAP)
        leave = (keep[2:].astype(F32) + other[2:].astype(F32)).astype(BF16)
        stay = keep[:2].astype(F32) + other[:2].astype(F32)
        columns.append((crossed, stay, leave))

    near, near_send, far, far_send = input_shares(
        pos, columns[0][2], corrs, projection.transpose(1, 0, 2)
    )
    gradients = []
    for crossed, stay, leave in columns:
        stay = stay + lax.ppermute(leave, "ctx", y_swap(crossed)).astype(F32)
        leave = stay[1].astype(BF16)
        stay = stay[0] + lax.ppermute(leave, "ctx", y_swap(not crossed)).astype(F32)
        leave = jnp.stack([stay[1], stay[3]]).astype(BF16)
        stay = jnp.stack([stay[0], stay[2]])
        stay = stay + lax.ppermute(leave, "ctx", z_swap(1)).astype(F32)
        leave = stay[1].astype(BF16)
        gradients.append(stay[0] + lax.ppermute(leave, "ctx", z_swap(2)).astype(F32))
    grad_proj = jnp.concatenate(gradients, axis=0).transpose(1, 0, 2)

    far = far + lax.ppermute(far_send, "tp", x_swap(False)).astype(F32)
    far = far[0] + lax.ppermute(far[1].astype(BF16), "tp", x_swap(True)).astype(F32)
    near = near + lax.ppermute(near_send, "tp", x_swap(True)).astype(F32)
    near = near[0] + lax.ppermute(near[1].astype(BF16), "tp", x_swap(False)).astype(F32)
    far = lax.ppermute(far.astype(BF16), "tp", Z_HI_SWAP)
    grad_input = (near + far.astype(F32)).astype(BF16)
    return grad_input, grad_proj


def solution(mesh):
    return jax.shard_map(
        per_device,
        mesh=mesh,
        in_specs=(P("ctx", "tp"), P("ctx", "tp"), P(), P(None, None, "tp")),
        out_specs=(P("ctx", "tp"), P("ctx", None, "tp")),
        check_vma=False,
    )
```

```python
import functools

import jax
import jax.numpy as jnp
from jax import lax
from jax.experimental import pallas as pl
from jax.experimental.pallas import tpu as pltpu
from jax.sharding import PartitionSpec as P

BF16, F32 = jnp.bfloat16, jnp.float32
ROWS = 64
LANE = 128
NX, NZ_HI, NY, NZ_LO, NCORE = 4, 2, 4, 4, 2
CHIPS = NY * NZ_LO
VMEM_LIMIT = 20 * 1024 * 1024
LARGE_COST = pl.CostEstimate(flops=4_000_000_000, bytes_accessed=8_000_000, transcendentals=0)
SMALL_COST = pl.CostEstimate(flops=1000, bytes_accessed=1000, transcendentals=0)


def ctx_of(y, z, core):
    return (y * NZ_LO + z) * NCORE + core


CTX = [(y, z, core) for y in range(NY) for z in range(NZ_LO) for core in range(NCORE)]
TP = [(x, z) for x in range(NX) for z in range(NZ_HI)]
CORE_SWAP = [(ctx_of(y, z, c), ctx_of(y, z, 1 - c)) for y, z, c in CTX]
Z_HI_SWAP = [(x * NZ_HI + z, x * NZ_HI + 1 - z) for x, z in TP]


def ring_partner(at, crossed):
    return NX - 1 - at if crossed else at ^ 1


def ring_slots(at, crossed):
    near, far = ring_partner(at, crossed), ring_partner(at, not crossed)
    return at, far, near, ring_partner(near, not crossed)


def y_swap(crossed):
    return [(ctx_of(y, z, c), ctx_of(ring_partner(y, crossed), z, c)) for y, z, c in CTX]


def x_swap(crossed):
    return [(x * NZ_HI + z, ring_partner(x, crossed) * NZ_HI + z) for x, z in TP]


def z_swap(bit):
    return [(ctx_of(y, z, c), ctx_of(y, z ^ bit, c)) for y, z, c in CTX]


def along_x(steps):
    return [(x * NZ_HI + z, (x + steps) % NX * NZ_HI + z) for x, z in TP]


def from_later_chip(steps):
    return [
        (NCORE * (chip + steps) + core, NCORE * chip + core)
        for chip in range(CHIPS - steps)
        for core in range(NCORE)
    ]


def table_kernel(filters_ref, grad_ref, near_ref, copy_ref, *far_refs):
    copy_ref[...] = grad_ref[...]
    filt_count, rows, near = near_ref.shape
    per_group, _, far = far_refs[0].shape
    taps = filters_ref.shape[1]
    width = near + far
    for k in range(filt_count):
        line = filters_ref[k : k + 1, :].astype(F32)
        line = jnp.concatenate([line, jnp.zeros((1, width - taps), F32)], axis=1)
        block = jnp.broadcast_to(line, (rows, width))
        block = pltpu.roll(block, 0, 1, stride=1, stride_axis=0).astype(BF16)
        near_ref[k] = block[:, :near]
        far_refs[k // per_group][k % per_group] = block[:, near:]


def toeplitz_tables(filters, grad_out, groups):
    filt_count, taps = filters.shape
    near, far = taps // 2, taps // 2 + LANE
    vmem = pl.BlockSpec(memory_space=pltpu.VMEM)
    outs = [jax.ShapeDtypeStruct((filt_count, ROWS, near), BF16)]
    outs += [jax.ShapeDtypeStruct(grad_out.shape, BF16)]
    outs += [jax.ShapeDtypeStruct((filt_count // groups, ROWS, far), BF16)] * groups
    return pl.pallas_call(
        table_kernel,
        out_shape=outs,
        in_specs=[vmem] * 2,
        out_specs=[vmem] * (2 + groups),
        compiler_params=pltpu.CompilerParams(vmem_limit_bytes=VMEM_LIMIT),
        cost_estimate=LARGE_COST,
        name="tables",
    )(filters, grad_out)


def pair_of_blocks(grad_ref, start, rows, width):
    first = grad_ref[pl.ds(start, width), :]
    second = grad_ref[pl.ds(start + rows, width), :]
    return jnp.concatenate([first, second], axis=1)


def coords(pos_ref):
    x, z_hi = pos_ref[0] // NZ_HI, lax.rem(pos_ref[0], NZ_HI)
    chip, core = pos_ref[1] // NCORE, lax.rem(pos_ref[1], NCORE)
    return x, z_hi, chip // NZ_LO, lax.rem(chip, NZ_LO), core


def lay_out(core, grad_ref, even_refs, odd_refs):
    tok = even_refs[0].shape[0]
    for s, part in enumerate(even_refs):
        grad_ref[2 * s * tok : (2 * s + 1) * tok, :] = part[...]
    for s in range(len(even_refs) - 1):
        grad_ref[(2 * s + 1) * tok : (2 * s + 2) * tok, :] = jnp.where(
            core == 0, odd_refs[s][...], odd_refs[s + 1][...]
        )


def near_kernel(pos_ref, table_ref, own_ref, r1_ref, r2_ref, s0_ref, s1_ref, s2_ref, *refs):
    acc_refs, grad_ref = refs[:-1], refs[-1]
    filt_count, rows, width = table_ref.shape
    tok = own_ref.shape[0]
    core = coords(pos_ref)[-1]
    lay_out(core, grad_ref, (own_ref, r1_ref, r2_ref), (s0_ref, s1_ref, s2_ref))
    table = table_ref[...].reshape(filt_count * rows, width)

    @pl.loop(0, tok // (2 * rows))
    def _(pair):
        start = pl.multiple_of(pair * (2 * rows), 2 * rows)
        both = pair_of_blocks(grad_ref, start, rows, width)
        result = jnp.dot(table, both, preferred_element_type=F32)
        part = acc_refs[0].shape[1]
        for group, acc_ref in enumerate(acc_refs):
            acc_ref[pair] = result[group * part : (group + 1) * part]


def near_conv(pos, table, halo, swapped, groups):
    filt_count, rows, width = table.shape
    tok = halo[0].shape[0]
    vmem = pl.BlockSpec(memory_space=pltpu.VMEM)
    acc = jax.ShapeDtypeStruct((tok // (2 * rows), filt_count // groups * rows, 2 * LANE), F32)
    return pl.pallas_call(
        near_kernel,
        out_shape=[acc] * groups,
        in_specs=[pl.BlockSpec(memory_space=pltpu.SMEM)] + [vmem] * 7,
        out_specs=[vmem] * groups,
        scratch_shapes=[pltpu.VMEM((5 * tok, LANE), BF16)],
        compiler_params=pltpu.CompilerParams(vmem_limit_bytes=VMEM_LIMIT),
        cost_estimate=LARGE_COST,
        name="near_conv",
    )(pos, table, *halo, *swapped)


def far_kernel(
    pos_ref, _, table_ref, acc_ref, r2_ref, r3_ref, r4_ref, s2_ref, s3_ref, s4_ref,
    corr_ref, grad_ref,
):
    filt_count, rows, width = table_ref.shape
    tok = r2_ref.shape[0]
    core = coords(pos_ref)[-1]
    lay_out(core, grad_ref, (r2_ref, r3_ref, r4_ref), (s2_ref, s3_ref, s4_ref))
    grad_ref[5 * tok :, :] = jnp.zeros((grad_ref.shape[0] - 5 * tok, LANE), BF16)
    table = table_ref[...].reshape(filt_count * rows, width)

    @pl.loop(0, tok // (2 * rows))
    def _(pair):
        start = pl.multiple_of(pair * (2 * rows), 2 * rows)
        both = pair_of_blocks(grad_ref, start, rows, width)
        result = jnp.dot(table, both, preferred_element_type=F32)
        result = (result + acc_ref[pair]).astype(BF16)
        for k in range(filt_count):
            for half in range(2):
                corr_ref[pl.ds(start + half * rows, rows), k * LANE : (k + 1) * LANE] = result[
                    k * rows : (k + 1) * rows, half * LANE : (half + 1) * LANE
                ]


def far_conv(pos, after, table, acc, halo, swapped):
    filt_count, rows, width = table.shape
    tok = halo[0].shape[0]
    vmem = pl.BlockSpec(memory_space=pltpu.VMEM)
    return pl.pallas_call(
        far_kernel,
        out_shape=jax.ShapeDtypeStruct((tok, filt_count * LANE), BF16),
        in_specs=[pl.BlockSpec(memory_space=pltpu.SMEM), pl.BlockSpec(memory_space=pl.ANY)]
        + [vmem] * 8,
        out_specs=vmem,
        scratch_shapes=[pltpu.VMEM((5 * tok + rows, LANE), BF16)],
        compiler_params=pltpu.CompilerParams(vmem_limit_bytes=VMEM_LIMIT),
        cost_estimate=SMALL_COST,
        name="far_conv",
    )(pos, after, table, acc, *halo, *swapped)


def product_kernel(
    crossed, pos_ref, corr_ref, x0_ref, x1_ref, x2_ref, x3_ref, keep_ref, send_ref, full_ref
):
    x, z_hi, y, z_lo, core = coords(pos_ref)
    for s, part in enumerate((x0_ref, x1_ref, x2_ref, x3_ref)):
        for h in range(NZ_HI):
            at = lax.rem(x + NX - s, NX) * NZ_HI + lax.rem(z_hi + h, NZ_HI)
            full_ref[:, pl.ds(pl.multiple_of(at * LANE, LANE), LANE)] = part[h]

    deep = NZ_LO * NCORE * 32
    for s, at in enumerate(ring_slots(y, crossed)):
        part = full_ref[:, pl.ds(pl.multiple_of(at * deep, deep), deep)]
        result = lax.dot_general(
            part, corr_ref[...], (((0,), (0,)), ((), ())), preferred_element_type=F32
        ).astype(BF16)
        for z in range(NZ_LO):
            shift = z ^ z_lo
            slot = lax.rem(shift, 2) * 2 + shift // 2
            for k in range(keep_ref.shape[2]):
                columns = slice(k * LANE, (k + 1) * LANE)
                even = result[z * 64 : z * 64 + 32, columns]
                odd = result[z * 64 + 32 : z * 64 + 64, columns]
                keep_ref[s, slot, k] = jnp.where(core == 0, even, odd)
                send_ref[s, slot, k] = jnp.where(core == 0, odd, even)


def product(crossed, pos, corr, gathered):
    tok, width = corr.shape
    part = jax.ShapeDtypeStruct((NY, NZ_LO, width // LANE, 32, LANE), BF16)
    vmem = pl.BlockSpec(memory_space=pltpu.VMEM)
    return pl.pallas_call(
        functools.partial(product_kernel, crossed),
        out_shape=(part, part),
        in_specs=[pl.BlockSpec(memory_space=pltpu.SMEM)] + [vmem] * 5,
        out_specs=(vmem,) * 2,
        scratch_shapes=[pltpu.VMEM((tok, 1024), BF16)],
        compiler_params=pltpu.CompilerParams(vmem_limit_bytes=VMEM_LIMIT),
        cost_estimate=SMALL_COST,
        name="product",
    )(pos, corr, *gathered)


def halve_kernel(_, mine_ref, other_ref, stay_ref, leave_ref):
    half = leave_ref.shape[0]
    stay_ref[...] = mine_ref[:half].astype(F32) + other_ref[:half].astype(F32)
    leave_ref[...] = (mine_ref[half:].astype(F32) + other_ref[half:].astype(F32)).astype(BF16)


def halve(after, mine, other):
    half = (mine.shape[0] // 2,) + mine.shape[1:]
    vmem = pl.BlockSpec(memory_space=pltpu.VMEM)
    return pl.pallas_call(
        halve_kernel,
        out_shape=(jax.ShapeDtypeStruct(half, F32), jax.ShapeDtypeStruct(half, BF16)),
        in_specs=[pl.BlockSpec(memory_space=pl.ANY), vmem, vmem],
        out_specs=(vmem, vmem),
        compiler_params=pltpu.CompilerParams(vmem_limit_bytes=VMEM_LIMIT),
        cost_estimate=SMALL_COST,
        name="halve",
    )(after, mine, other)


def add_kernel(_, mine_ref, other_ref, sum_ref):
    sum_ref[...] = (mine_ref[...] + other_ref[...].astype(F32)).astype(BF16)


def add(after, mine, other):
    vmem = pl.BlockSpec(memory_space=pltpu.VMEM)
    return pl.pallas_call(
        add_kernel,
        out_shape=jax.ShapeDtypeStruct(mine.shape, BF16),
        in_specs=[pl.BlockSpec(memory_space=pl.ANY), vmem, vmem],
        out_specs=vmem,
        compiler_params=pltpu.CompilerParams(vmem_limit_bytes=VMEM_LIMIT),
        cost_estimate=SMALL_COST,
        name="add",
    )(after, mine, other)


def share_kernel(pos_ref, _, *refs):
    corr_refs, proj_ref = refs[:-6], refs[-6]
    near_keep, near_send, far_keep, far_send, all_ref = refs[-5:]
    filt_count = proj_ref.shape[0]
    x, z_hi = coords(pos_ref)[:2]
    at = 0
    for part in corr_refs:
        all_ref[:, at : at + part.shape[1]] = part[...]
        at += part.shape[1]
    wide = NZ_HI * LANE
    near_slots = (near_keep, 0), (near_send, 0), (near_keep, 1), (near_send, 1)
    far_slots = (far_keep, 0), (far_keep, 1), (far_send, 0), (far_send, 1)
    for at, near, far in zip(ring_slots(x, False), near_slots, far_slots):
        base = pl.multiple_of(at * wide, wide)
        weights = jnp.concatenate(
            [proj_ref[k, pl.ds(base, wide), :] for k in range(filt_count)], axis=1
        )
        result = lax.dot_general(
            all_ref[...], weights, (((1,), (1,)), ((), ())), preferred_element_type=F32
        )
        low, high = result[:, :LANE], result[:, LANE:]
        near[0][near[1]] = jnp.where(z_hi == 0, low, high).astype(near[0].dtype)
        far[0][far[1]] = jnp.where(z_hi == 0, high, low).astype(far[0].dtype)


def input_shares(pos, after, corrs, projection):
    tok = corrs[0].shape[0]
    filt_count = projection.shape[0]
    vmem = pl.BlockSpec(memory_space=pltpu.VMEM)
    keep = jax.ShapeDtypeStruct((2, tok, LANE), F32)
    send = jax.ShapeDtypeStruct((2, tok, LANE), BF16)
    return pl.pallas_call(
        share_kernel,
        out_shape=(keep, send, keep, send),
        in_specs=[pl.BlockSpec(memory_space=pltpu.SMEM), pl.BlockSpec(memory_space=pl.ANY)]
        + [vmem] * (len(corrs) + 1),
        out_specs=(vmem,) * 4,
        scratch_shapes=[pltpu.VMEM((tok, filt_count * LANE), BF16)],
        compiler_params=pltpu.CompilerParams(vmem_limit_bytes=VMEM_LIMIT),
        cost_estimate=SMALL_COST,
        name="input_shares",
    )(pos, after, *corrs, projection)


GROUPS = 2


def per_device(inputs, grad_out, filters, projection):
    tp, ctx = lax.axis_index("tp"), lax.axis_index("ctx")
    pos = jnp.stack([tp, ctx]).astype(jnp.int32)

    def later(value, steps):
        return lax.ppermute(value, "ctx", from_later_chip(steps))

    def sibling(value):
        return lax.ppermute(value, "ctx", CORE_SWAP)

    def y_swapped(value, crossed):
        return lax.ppermute(value, "ctx", y_swap(crossed))

    def z_swapped(value, bit):
        return lax.ppermute(value, "ctx", z_swap(bit))

    def x_swapped(value, crossed):
        return lax.ppermute(value, "tp", x_swap(crossed))

    pair = jnp.stack([inputs, lax.ppermute(inputs, "tp", Z_HI_SWAP)])
    gathered = [pair] + [lax.ppermute(pair, "tp", along_x(s)) for s in range(1, NX)]
    near_table, grad_copy, *far_tables = toeplitz_tables(filters, grad_out, GROUPS)
    halo = [grad_out, later(grad_out, 1), later(grad_out, 2)]
    halo += [later(grad_copy, 3), later(grad_copy, 4)]
    swapped = [sibling(part) for part in halo]
    accs = near_conv(pos, near_table, halo[:3], swapped[:3], GROUPS)

    def conv(group, after):
        return far_conv(pos, after, far_tables[group], accs[group], halo[2:], swapped[2:])

    corr_0 = conv(0, near_table)
    keep_0, send_0 = product(False, pos, corr_0, gathered)
    corr_1 = conv(1, send_0)
    keep_1, send_1 = product(True, pos, corr_1, gathered)

    stay_0, leave_0 = halve(send_1, keep_0, sibling(send_0))
    near, near_send, far, far_send = input_shares(
        pos, leave_0, [corr_0, corr_1], projection.transpose(1, 0, 2)
    )
    y_0 = y_swapped(leave_0, False)
    stay_1, leave_1 = halve(near_send, keep_1, sibling(send_1))
    y_1 = y_swapped(leave_1, True)
    far, leave = halve(leave_1, far, x_swapped(far_send, False))
    x_far = x_swapped(leave, True)
    stay_0, leave_0 = halve(leave, stay_0, y_0)
    y_0 = y_swapped(leave_0, True)
    near, leave = halve(leave_0, near, x_swapped(near_send, True))
    x_near = x_swapped(leave, False)
    stay_1, leave_1 = halve(leave, stay_1, y_1)
    y_1 = y_swapped(leave_1, False)
    far = add(leave_1, far, x_far)
    opposite = lax.ppermute(far, "tp", Z_HI_SWAP)

    stay_0, leave_0 = halve(far, stay_0[0], y_0[0])
    z_0 = z_swapped(leave_0, 1)
    stay_1, leave_1 = halve(leave_0, stay_1[0], y_1[0])
    z_1 = z_swapped(leave_1, 1)
    stay_0, leave_0 = halve(leave_1, stay_0, z_0)
    z_0 = z_swapped(leave_0, 2)
    stay_1, leave_1 = halve(leave_0, stay_1, z_1)
    z_1 = z_swapped(leave_1, 2)
    parts = [stay_0[0] + z_0[0].astype(F32), stay_1[0] + z_1[0].astype(F32)]
    grad_proj = jnp.concatenate(parts, axis=0).transpose(1, 0, 2)
    total = near[0] + x_near[0].astype(F32) + opposite[0].astype(F32)
    return total.astype(BF16), grad_proj


def solution(mesh):
    return jax.shard_map(
        per_device,
        mesh=mesh,
        in_specs=(P("ctx", "tp"), P("ctx", "tp"), P(), P(None, None, "tp")),
        out_specs=(P("ctx", "tp"), P("ctx", None, "tp")),
        check_vma=False,
    )
```

```python
import functools

import jax
import jax.numpy as jnp
from jax import lax
from jax.experimental import pallas as pl
from jax.experimental.pallas import tpu as pltpu
from jax.sharding import PartitionSpec as P

BF16, F32 = jnp.bfloat16, jnp.float32
ROWS = 64
LANE = 128
NX, NZ_HI, NY, NZ_LO, NCORE = 4, 2, 4, 4, 2
CHIPS = NY * NZ_LO
VMEM_LIMIT = 20 * 1024 * 1024
LARGE_COST = pl.CostEstimate(flops=4_000_000_000, bytes_accessed=8_000_000, transcendentals=0)
SMALL_COST = pl.CostEstimate(flops=1000, bytes_accessed=1000, transcendentals=0)


def ctx_of(y, z, core):
    return (y * NZ_LO + z) * NCORE + core


CTX = [(y, z, core) for y in range(NY) for z in range(NZ_LO) for core in range(NCORE)]
TP = [(x, z) for x in range(NX) for z in range(NZ_HI)]
CORE_SWAP = [(ctx_of(y, z, c), ctx_of(y, z, 1 - c)) for y, z, c in CTX]
Z_HI_SWAP = [(x * NZ_HI + z, x * NZ_HI + 1 - z) for x, z in TP]


def ring_partner(at, crossed):
    return NX - 1 - at if crossed else at ^ 1


def ring_slots(at, crossed):
    near, far = ring_partner(at, crossed), ring_partner(at, not crossed)
    return at, far, near, ring_partner(near, not crossed)


def y_swap(crossed):
    return [(ctx_of(y, z, c), ctx_of(ring_partner(y, crossed), z, c)) for y, z, c in CTX]


def x_swap(crossed):
    return [(x * NZ_HI + z, ring_partner(x, crossed) * NZ_HI + z) for x, z in TP]


def z_swap(bit):
    return [(ctx_of(y, z, c), ctx_of(y, z ^ bit, c)) for y, z, c in CTX]


def along_x(steps):
    return [(x * NZ_HI + z, (x + steps) % NX * NZ_HI + z) for x, z in TP]


def from_later_chip(steps):
    return [
        (NCORE * (chip + steps) + core, NCORE * chip + core)
        for chip in range(CHIPS - steps)
        for core in range(NCORE)
    ]


def shifted_rows(line, rows):
    block = jnp.broadcast_to(line, (rows, line.shape[1]))
    return pltpu.roll(block, 0, 1, stride=1, stride_axis=0).astype(BF16)


def table_kernel(filters_ref, near_ref):
    filt_count, rows, near = near_ref.shape
    edge = jnp.zeros((1, LANE), F32)
    for k in range(filt_count):
        line = filters_ref[k : k + 1, :near].astype(F32)
        near_ref[k] = shifted_rows(jnp.concatenate([line, edge], axis=1), rows)[:, :near]


def near_table(filters):
    filt_count, taps = filters.shape
    vmem = pl.BlockSpec(memory_space=pltpu.VMEM)
    return pl.pallas_call(
        table_kernel,
        out_shape=jax.ShapeDtypeStruct((filt_count, ROWS, taps // 2), BF16),
        in_specs=[vmem],
        out_specs=vmem,
        compiler_params=pltpu.CompilerParams(vmem_limit_bytes=VMEM_LIMIT),
        cost_estimate=LARGE_COST,
        name="near_table",
    )(filters)


def prep_kernel(_, own_ref, r1_ref, r2_ref, r4_ref, in_ref, far_in_ref, stack_ref, pair_ref, copy_ref):
    copy_ref[...] = own_ref[...]
    for s, part in enumerate((own_ref, r1_ref, r2_ref, r4_ref)):
        stack_ref[s] = part[...]
    pair_ref[0] = in_ref[...]
    pair_ref[1] = far_in_ref[...]


def prepare(after, *parts):
    block = parts[0].shape
    vmem = pl.BlockSpec(memory_space=pltpu.VMEM)
    return pl.pallas_call(
        prep_kernel,
        out_shape=[
            jax.ShapeDtypeStruct((4,) + block, BF16),
            jax.ShapeDtypeStruct((2,) + block, BF16),
            jax.ShapeDtypeStruct(block, BF16),
        ],
        in_specs=[pl.BlockSpec(memory_space=pl.ANY)] + [vmem] * 6,
        out_specs=[vmem] * 3,
        compiler_params=pltpu.CompilerParams(vmem_limit_bytes=VMEM_LIMIT),
        cost_estimate=SMALL_COST,
        name="prepare",
    )(after, *parts)


def pair_of_blocks(grad_ref, start, rows, width):
    first = grad_ref[pl.ds(start, width), :]
    second = grad_ref[pl.ds(start + rows, width), :]
    return jnp.concatenate([first, second], axis=1)


def coords(pos_ref):
    x, z_hi = pos_ref[0] // NZ_HI, lax.rem(pos_ref[0], NZ_HI)
    chip, core = pos_ref[1] // NCORE, lax.rem(pos_ref[1], NCORE)
    return x, z_hi, chip // NZ_LO, lax.rem(chip, NZ_LO), core


def lay_out(core, grad_ref, even_refs, odd_refs):
    tok = even_refs[0].shape[0]
    for s, part in enumerate(even_refs):
        grad_ref[2 * s * tok : (2 * s + 1) * tok, :] = part[...]
    for s in range(len(even_refs) - 1):
        grad_ref[(2 * s + 1) * tok : (2 * s + 2) * tok, :] = jnp.where(
            core == 0, odd_refs[s][...], odd_refs[s + 1][...]
        )


def near_kernel(pos_ref, table_ref, own_ref, r1_ref, r2_ref, sib_ref, *refs):
    acc_refs, grad_ref = refs[:-1], refs[-1]
    filt_count, rows, width = table_ref.shape
    tok = own_ref.shape[0]
    core = coords(pos_ref)[-1]
    lay_out(core, grad_ref, (own_ref, r1_ref, r2_ref), [sib_ref.at[s] for s in range(3)])
    table = table_ref[...].reshape(filt_count * rows, width)

    @pl.loop(0, tok // (2 * rows))
    def _(pair):
        start = pl.multiple_of(pair * (2 * rows), 2 * rows)
        both = pair_of_blocks(grad_ref, start, rows, width)
        result = jnp.dot(table, both, preferred_element_type=F32)
        part = acc_refs[0].shape[1]
        for group, acc_ref in enumerate(acc_refs):
            acc_ref[pair] = result[group * part : (group + 1) * part]


def near_conv(pos, table, halo, sibling, groups):
    filt_count, rows, width = table.shape
    tok = halo[0].shape[0]
    vmem = pl.BlockSpec(memory_space=pltpu.VMEM)
    acc = jax.ShapeDtypeStruct((tok // (2 * rows), filt_count // groups * rows, 2 * LANE), F32)
    return pl.pallas_call(
        near_kernel,
        out_shape=[acc] * groups,
        in_specs=[pl.BlockSpec(memory_space=pltpu.SMEM)] + [vmem] * 5,
        out_specs=[vmem] * groups,
        scratch_shapes=[pltpu.VMEM((5 * tok, LANE), BF16)],
        compiler_params=pltpu.CompilerParams(vmem_limit_bytes=VMEM_LIMIT),
        cost_estimate=LARGE_COST,
        name="near_conv",
    )(pos, table, *halo, sibling)


def far_kernel(
    first, pos_ref, _, filters_ref, acc_ref, r2_ref, r3_ref, r4_ref, sib_ref, sib_r3_ref,
    corr_ref, grad_ref, table_ref,
):
    filt_count, rows, width = table_ref.shape
    tok = r2_ref.shape[0]
    core = coords(pos_ref)[-1]
    edge = jnp.zeros((1, LANE), F32)
    start = filters_ref.shape[1] + LANE - width - LANE
    for k in range(filt_count):
        line = filters_ref[first + k : first + k + 1, start:].astype(F32)
        table_ref[k] = shifted_rows(jnp.concatenate([line, edge], axis=1), rows)[:, LANE:]
    lay_out(core, grad_ref, (r2_ref, r3_ref, r4_ref), (sib_ref.at[2], sib_r3_ref, sib_ref.at[3]))
    grad_ref[5 * tok :, :] = jnp.zeros((grad_ref.shape[0] - 5 * tok, LANE), BF16)

    @pl.loop(0, tok // (2 * rows))
    def _(pair):
        start = pl.multiple_of(pair * (2 * rows), 2 * rows)
        both = pair_of_blocks(grad_ref, start, rows, width)
        table = table_ref[...].reshape(filt_count * rows, width)
        result = jnp.dot(table, both, preferred_element_type=F32)
        result = (result + acc_ref[pair]).astype(BF16)
        for k in range(filt_count):
            for half in range(2):
                corr_ref[pl.ds(start + half * rows, rows), k * LANE : (k + 1) * LANE] = result[
                    k * rows : (k + 1) * rows, half * LANE : (half + 1) * LANE
                ]


def far_conv(first, count, pos, after, filters, acc, halo, sibling, sibling_r3):
    tok = halo[0].shape[0]
    width = filters.shape[1] // 2 + LANE
    vmem = pl.BlockSpec(memory_space=pltpu.VMEM)
    return pl.pallas_call(
        functools.partial(far_kernel, first),
        out_shape=jax.ShapeDtypeStruct((tok, count * LANE), BF16),
        in_specs=[pl.BlockSpec(memory_space=pltpu.SMEM), pl.BlockSpec(memory_space=pl.ANY)]
        + [vmem] * 7,
        out_specs=vmem,
        scratch_shapes=[
            pltpu.VMEM((5 * tok + ROWS, LANE), BF16),
            pltpu.VMEM((count, ROWS, width), BF16),
        ],
        compiler_params=pltpu.CompilerParams(vmem_limit_bytes=VMEM_LIMIT),
        cost_estimate=SMALL_COST,
        name="far_conv",
    )(pos, after, filters, acc, *halo, sibling, sibling_r3)


def product_kernel(
    crossed, pos_ref, _, corr_ref, x0_ref, x1_ref, x2_ref, x3_ref, keep_ref, send_ref, full_ref
):
    x, z_hi, y, z_lo, core = coords(pos_ref)
    for s, part in enumerate((x0_ref, x1_ref, x2_ref, x3_ref)):
        for h in range(NZ_HI):
            at = lax.rem(x + NX - s, NX) * NZ_HI + lax.rem(z_hi + h, NZ_HI)
            full_ref[:, pl.ds(pl.multiple_of(at * LANE, LANE), LANE)] = part[h]

    deep = NZ_LO * NCORE * 32
    for s, at in enumerate(ring_slots(y, crossed)):
        part = full_ref[:, pl.ds(pl.multiple_of(at * deep, deep), deep)]
        result = lax.dot_general(
            part, corr_ref[...], (((0,), (0,)), ((), ())), preferred_element_type=F32
        ).astype(BF16)
        for z in range(NZ_LO):
            shift = z ^ z_lo
            slot = lax.rem(shift, 2) * 2 + shift // 2
            for k in range(keep_ref.shape[2]):
                columns = slice(k * LANE, (k + 1) * LANE)
                even = result[z * 64 : z * 64 + 32, columns]
                odd = result[z * 64 + 32 : z * 64 + 64, columns]
                keep_ref[s, slot, k] = jnp.where(core == 0, even, odd)
                send_ref[s, slot, k] = jnp.where(core == 0, odd, even)


def product(crossed, pos, after, corr, gathered):
    tok, width = corr.shape
    part = jax.ShapeDtypeStruct((NY, NZ_LO, width // LANE, 32, LANE), BF16)
    vmem = pl.BlockSpec(memory_space=pltpu.VMEM)
    return pl.pallas_call(
        functools.partial(product_kernel, crossed),
        out_shape=(part, part),
        in_specs=[pl.BlockSpec(memory_space=pltpu.SMEM), pl.BlockSpec(memory_space=pl.ANY)]
        + [vmem] * 5,
        out_specs=(vmem,) * 2,
        scratch_shapes=[pltpu.VMEM((tok, 1024), BF16)],
        compiler_params=pltpu.CompilerParams(vmem_limit_bytes=VMEM_LIMIT),
        cost_estimate=SMALL_COST,
        name="product",
    )(pos, after, corr, *gathered)


def halve_kernel(_, mine_ref, other_ref, stay_ref, leave_ref):
    half = leave_ref.shape[0]
    stay_ref[...] = mine_ref[:half].astype(F32) + other_ref[:half].astype(F32)
    leave_ref[...] = (mine_ref[half:].astype(F32) + other_ref[half:].astype(F32)).astype(BF16)


def halve(after, mine, other):
    half = (mine.shape[0] // 2,) + mine.shape[1:]
    vmem = pl.BlockSpec(memory_space=pltpu.VMEM)
    return pl.pallas_call(
        halve_kernel,
        out_shape=(jax.ShapeDtypeStruct(half, F32), jax.ShapeDtypeStruct(half, BF16)),
        in_specs=[pl.BlockSpec(memory_space=pl.ANY), vmem, vmem],
        out_specs=(vmem, vmem),
        compiler_params=pltpu.CompilerParams(vmem_limit_bytes=VMEM_LIMIT),
        cost_estimate=SMALL_COST,
        name="halve",
    )(after, mine, other)


def add_kernel(_, mine_ref, other_ref, sum_ref):
    sum_ref[...] = (mine_ref[...] + other_ref[...].astype(F32)).astype(BF16)


def add(after, mine, other):
    vmem = pl.BlockSpec(memory_space=pltpu.VMEM)
    return pl.pallas_call(
        add_kernel,
        out_shape=jax.ShapeDtypeStruct(mine.shape, BF16),
        in_specs=[pl.BlockSpec(memory_space=pl.ANY), vmem, vmem],
        out_specs=vmem,
        compiler_params=pltpu.CompilerParams(vmem_limit_bytes=VMEM_LIMIT),
        cost_estimate=SMALL_COST,
        name="add",
    )(after, mine, other)


def share_kernel(pos_ref, _, *refs):
    corr_refs, proj_ref = refs[:-6], refs[-6]
    near_keep, near_send, far_keep, far_send, all_ref = refs[-5:]
    filt_count = proj_ref.shape[0]
    x, z_hi = coords(pos_ref)[:2]
    at = 0
    for part in corr_refs:
        all_ref[:, at : at + part.shape[1]] = part[...]
        at += part.shape[1]
    wide = NZ_HI * LANE
    near_slots = (near_keep, 0), (near_send, 0), (near_keep, 1), (near_send, 1)
    far_slots = (far_keep, 0), (far_keep, 1), (far_send, 0), (far_send, 1)
    for at, near, far in zip(ring_slots(x, False), near_slots, far_slots):
        base = pl.multiple_of(at * wide, wide)
        weights = jnp.concatenate(
            [proj_ref[k, pl.ds(base, wide), :] for k in range(filt_count)], axis=1
        )
        result = lax.dot_general(
            all_ref[...], weights, (((1,), (1,)), ((), ())), preferred_element_type=F32
        )
        low, high = result[:, :LANE], result[:, LANE:]
        near[0][near[1]] = jnp.where(z_hi == 0, low, high).astype(near[0].dtype)
        far[0][far[1]] = jnp.where(z_hi == 0, high, low).astype(far[0].dtype)


def input_shares(pos, after, corrs, projection):
    tok = corrs[0].shape[0]
    filt_count = projection.shape[0]
    vmem = pl.BlockSpec(memory_space=pltpu.VMEM)
    keep = jax.ShapeDtypeStruct((2, tok, LANE), F32)
    send = jax.ShapeDtypeStruct((2, tok, LANE), BF16)
    return pl.pallas_call(
        share_kernel,
        out_shape=(keep, send, keep, send),
        in_specs=[pl.BlockSpec(memory_space=pltpu.SMEM), pl.BlockSpec(memory_space=pl.ANY)]
        + [vmem] * (len(corrs) + 1),
        out_specs=(vmem,) * 4,
        scratch_shapes=[pltpu.VMEM((tok, filt_count * LANE), BF16)],
        compiler_params=pltpu.CompilerParams(vmem_limit_bytes=VMEM_LIMIT),
        cost_estimate=SMALL_COST,
        name="input_shares",
    )(pos, after, *corrs, projection)


GROUPS = 2


def per_device(inputs, grad_out, filters, projection):
    tp, ctx = lax.axis_index("tp"), lax.axis_index("ctx")
    pos = jnp.stack([tp, ctx]).astype(jnp.int32)

    def later(value, steps):
        return lax.ppermute(value, "ctx", from_later_chip(steps))

    def sibling(value):
        return lax.ppermute(value, "ctx", CORE_SWAP)

    def y_swapped(value, crossed):
        return lax.ppermute(value, "ctx", y_swap(crossed))

    def z_swapped(value, bit):
        return lax.ppermute(value, "ctx", z_swap(bit))

    def x_swapped(value, crossed):
        return lax.ppermute(value, "tp", x_swap(crossed))

    count = filters.shape[0] // GROUPS
    r1, r2, r4 = (later(grad_out, steps) for steps in (1, 2, 4))
    table = near_table(filters)
    stack, pair, grad_copy = prepare(
        table, grad_out, r1, r2, r4, inputs, lax.ppermute(inputs, "tp", Z_HI_SWAP)
    )
    beside = sibling(stack)
    gathered = [pair] + [lax.ppermute(pair, "tp", along_x(s)) for s in range(1, NX)]
    r3 = later(grad_copy, 3)
    beside_r3 = sibling(r3)
    accs = near_conv(pos, table, (grad_out, r1, r2), beside, GROUPS)

    def conv(group, after):
        return far_conv(
            group * count, count, pos, after, filters, accs[group], (r2, r3, r4), beside, beside_r3
        )

    corr_0 = conv(0, table)
    keep_0, send_0 = product(False, pos, table, corr_0, gathered)
    corr_1 = conv(1, send_0)
    stay_0, leave_0 = halve(corr_1, keep_0, sibling(send_0))
    y_0 = y_swapped(leave_0, False)
    keep_1, send_1 = product(True, pos, leave_0, corr_1, gathered)

    near, near_send, far, far_send = input_shares(
        pos, send_1, [corr_0, corr_1], projection.transpose(1, 0, 2)
    )
    stay_1, leave_1 = halve(near_send, keep_1, sibling(send_1))
    y_1 = y_swapped(leave_1, True)
    far, leave = halve(leave_1, far, x_swapped(far_send, False))
    x_far = x_swapped(leave, True)
    stay_0, leave_0 = halve(leave, stay_0, y_0)
    y_0 = y_swapped(leave_0, True)
    near, leave = halve(leave_0, near, x_swapped(near_send, True))
    x_near = x_swapped(leave, False)
    stay_1, leave_1 = halve(leave, stay_1, y_1)
    y_1 = y_swapped(leave_1, False)
    far = add(leave_1, far, x_far)
    opposite = lax.ppermute(far, "tp", Z_HI_SWAP)

    stay_0, leave_0 = halve(far, stay_0[0], y_0[0])
    z_0 = z_swapped(leave_0, 1)
    stay_1, leave_1 = halve(leave_0, stay_1[0], y_1[0])
    z_1 = z_swapped(leave_1, 1)
    stay_0, leave_0 = halve(leave_1, stay_0, z_0)
    z_0 = z_swapped(leave_0, 2)
    stay_1, leave_1 = halve(leave_0, stay_1, z_1)
    z_1 = z_swapped(leave_1, 2)
    parts = [stay_0[0] + z_0[0].astype(F32), stay_1[0] + z_1[0].astype(F32)]
    grad_proj = jnp.concatenate(parts, axis=0).transpose(1, 0, 2)
    total = near[0] + x_near[0].astype(F32) + opposite[0].astype(F32)
    return total.astype(BF16), grad_proj


def solution(mesh):
    return jax.shard_map(
        per_device,
        mesh=mesh,
        in_specs=(P("ctx", "tp"), P("ctx", "tp"), P(), P(None, None, "tp")),
        out_specs=(P("ctx", "tp"), P("ctx", None, "tp")),
        check_vma=False,
    )
```

```python
import functools

import jax
import jax.numpy as jnp
from jax import lax
from jax.experimental import pallas as pl
from jax.experimental.pallas import tpu as pltpu
from jax.sharding import PartitionSpec as P

BF16, F32 = jnp.bfloat16, jnp.float32
ROWS = 64
LANE = 128
NX, NZ_HI, NY, NZ_LO, NCORE = 4, 2, 4, 4, 2
CHIPS = NY * NZ_LO
VMEM_LIMIT = 20 * 1024 * 1024
LARGE_COST = pl.CostEstimate(flops=4_000_000_000, bytes_accessed=8_000_000, transcendentals=0)
SMALL_COST = pl.CostEstimate(flops=1000, bytes_accessed=1000, transcendentals=0)


def ctx_of(y, z, core):
    return (y * NZ_LO + z) * NCORE + core


CTX = [(y, z, core) for y in range(NY) for z in range(NZ_LO) for core in range(NCORE)]
TP = [(x, z) for x in range(NX) for z in range(NZ_HI)]
CORE_SWAP = [(ctx_of(y, z, c), ctx_of(y, z, 1 - c)) for y, z, c in CTX]
Z_HI_SWAP = [(x * NZ_HI + z, x * NZ_HI + 1 - z) for x, z in TP]


def ring_partner(at, crossed):
    return NX - 1 - at if crossed else at ^ 1


def ring_slots(at, crossed):
    near, far = ring_partner(at, crossed), ring_partner(at, not crossed)
    return at, far, near, ring_partner(near, not crossed)


def y_swap(crossed):
    return [(ctx_of(y, z, c), ctx_of(ring_partner(y, crossed), z, c)) for y, z, c in CTX]


def x_swap(crossed):
    return [(x * NZ_HI + z, ring_partner(x, crossed) * NZ_HI + z) for x, z in TP]


def z_swap(bit):
    return [(ctx_of(y, z, c), ctx_of(y, z ^ bit, c)) for y, z, c in CTX]


def along_x(steps):
    return [(x * NZ_HI + z, (x + steps) % NX * NZ_HI + z) for x, z in TP]


def from_later_chip(steps):
    return [
        (NCORE * (chip + steps) + core, NCORE * chip + core)
        for chip in range(CHIPS - steps)
        for core in range(NCORE)
    ]


def shifted_rows(line, rows):
    block = jnp.broadcast_to(line, (rows, line.shape[1]))
    return pltpu.roll(block, 0, 1, stride=1, stride_axis=0).astype(BF16)


def table_kernel(filters_ref, near_ref):
    filt_count, rows, near = near_ref.shape
    edge = jnp.zeros((1, LANE), F32)
    for k in range(filt_count):
        line = filters_ref[k : k + 1, :near].astype(F32)
        near_ref[k] = shifted_rows(jnp.concatenate([line, edge], axis=1), rows)[:, :near]


def near_table(filters):
    filt_count, taps = filters.shape
    vmem = pl.BlockSpec(memory_space=pltpu.VMEM)
    return pl.pallas_call(
        table_kernel,
        out_shape=jax.ShapeDtypeStruct((filt_count, ROWS, taps // 2), BF16),
        in_specs=[vmem],
        out_specs=vmem,
        compiler_params=pltpu.CompilerParams(vmem_limit_bytes=VMEM_LIMIT),
        cost_estimate=LARGE_COST,
        name="near_table",
    )(filters)


def prep_kernel(pos_ref, _, __, *refs):
    parts, stack_ref = refs[:-1], refs[-1]
    core = lax.rem(pos_ref[1], NCORE)
    for s in range(stack_ref.shape[0]):
        stack_ref[s] = jnp.where(core == 0, parts[s + 1][...], parts[s][...])


def for_sibling(pos, after, *parts):
    vmem = pl.BlockSpec(memory_space=pltpu.VMEM)
    return pl.pallas_call(
        prep_kernel,
        out_shape=jax.ShapeDtypeStruct((len(parts) - 1,) + parts[0].shape, BF16),
        in_specs=[pl.BlockSpec(memory_space=pltpu.SMEM)]
        + [pl.BlockSpec(memory_space=pl.ANY)] * 2
        + [vmem] * len(parts),
        out_specs=vmem,
        compiler_params=pltpu.CompilerParams(vmem_limit_bytes=VMEM_LIMIT),
        cost_estimate=SMALL_COST,
        name="for_sibling",
    )(pos, *after, *parts)


def pair_of_blocks(grad_ref, start, rows, width):
    first = grad_ref[pl.ds(start, width), :]
    second = grad_ref[pl.ds(start + rows, width), :]
    return jnp.concatenate([first, second], axis=1)


def coords(pos_ref):
    x, z_hi = pos_ref[0] // NZ_HI, lax.rem(pos_ref[0], NZ_HI)
    chip, core = pos_ref[1] // NCORE, lax.rem(pos_ref[1], NCORE)
    return x, z_hi, chip // NZ_LO, lax.rem(chip, NZ_LO), core


def lay_out(grad_ref, refs):
    tok = refs[0].shape[0]
    for s, part in enumerate(refs):
        grad_ref[s * tok : (s + 1) * tok, :] = part[...]


def near_kernel(table_ref, own_ref, r1_ref, r2_ref, sib_ref, *refs):
    acc_refs, grad_ref = refs[:-1], refs[-1]
    filt_count, rows, width = table_ref.shape
    tok = own_ref.shape[0]
    lay_out(grad_ref, (own_ref, sib_ref.at[0], r1_ref, sib_ref.at[1], r2_ref))
    table = table_ref[...].reshape(filt_count * rows, width)

    @pl.loop(0, tok // (2 * rows), unroll=True)
    def _(pair):
        start = pl.multiple_of(pair * (2 * rows), 2 * rows)
        both = pair_of_blocks(grad_ref, start, rows, width)
        result = jnp.dot(table, both, preferred_element_type=F32)
        part = acc_refs[0].shape[1]
        for group, acc_ref in enumerate(acc_refs):
            acc_ref[pair] = result[group * part : (group + 1) * part]


def near_conv(table, halo, sibling, groups):
    filt_count, rows, width = table.shape
    tok = halo[0].shape[0]
    vmem = pl.BlockSpec(memory_space=pltpu.VMEM)
    acc = jax.ShapeDtypeStruct((tok // (2 * rows), filt_count // groups * rows, 2 * LANE), F32)
    return pl.pallas_call(
        near_kernel,
        out_shape=[acc] * groups,
        in_specs=[vmem] * 5,
        out_specs=[vmem] * groups,
        scratch_shapes=[pltpu.VMEM((5 * tok, LANE), BF16)],
        compiler_params=pltpu.CompilerParams(vmem_limit_bytes=VMEM_LIMIT),
        cost_estimate=LARGE_COST,
        name="near_conv",
    )(table, *halo, sibling)


def far_kernel(
    first, _, filters_ref, acc_ref, r2_ref, r3_ref, r4_ref, sib_ref,
    corr_ref, grad_ref, table_ref,
):
    filt_count, rows, width = table_ref.shape
    tok = r2_ref.shape[0]
    edge = jnp.zeros((1, LANE), F32)
    start = filters_ref.shape[1] + LANE - width - LANE
    for k in range(filt_count):
        line = filters_ref[first + k : first + k + 1, start:].astype(F32)
        table_ref[k] = shifted_rows(jnp.concatenate([line, edge], axis=1), rows)[:, LANE:]
    lay_out(grad_ref, (r2_ref, sib_ref.at[2], r3_ref, sib_ref.at[3], r4_ref))
    grad_ref[5 * tok :, :] = jnp.zeros((grad_ref.shape[0] - 5 * tok, LANE), BF16)

    @pl.loop(0, tok // (2 * rows), unroll=True)
    def _(pair):
        start = pl.multiple_of(pair * (2 * rows), 2 * rows)
        both = pair_of_blocks(grad_ref, start, rows, width)
        table = table_ref[...].reshape(filt_count * rows, width)
        result = jnp.dot(table, both, preferred_element_type=F32)
        result = (result + acc_ref[pair]).astype(BF16)
        for k in range(filt_count):
            for half in range(2):
                corr_ref[pl.ds(start + half * rows, rows), k * LANE : (k + 1) * LANE] = result[
                    k * rows : (k + 1) * rows, half * LANE : (half + 1) * LANE
                ]


def far_conv(first, count, after, filters, acc, halo, sibling):
    tok = halo[0].shape[0]
    width = filters.shape[1] // 2 + LANE
    vmem = pl.BlockSpec(memory_space=pltpu.VMEM)
    return pl.pallas_call(
        functools.partial(far_kernel, first),
        out_shape=jax.ShapeDtypeStruct((tok, count * LANE), BF16),
        in_specs=[pl.BlockSpec(memory_space=pl.ANY)] + [vmem] * 6,
        out_specs=vmem,
        scratch_shapes=[
            pltpu.VMEM((5 * tok + ROWS, LANE), BF16),
            pltpu.VMEM((count, ROWS, width), BF16),
        ],
        compiler_params=pltpu.CompilerParams(vmem_limit_bytes=VMEM_LIMIT),
        cost_estimate=SMALL_COST,
        name="far_conv",
    )(after, filters, acc, *halo, sibling)


def product_kernel(
    crossed, pos_ref, _, corr_ref, x0_ref, x1_ref, x2_ref, x3_ref, keep_ref, send_ref, full_ref
):
    x, z_hi, y, z_lo, core = coords(pos_ref)
    for s, part in enumerate((x0_ref, x1_ref, x2_ref, x3_ref)):
        for h in range(NZ_HI):
            at = lax.rem(x + NX - s, NX) * NZ_HI + lax.rem(z_hi + h, NZ_HI)
            full_ref[:, pl.ds(pl.multiple_of(at * LANE, LANE), LANE)] = part[h]

    deep = NZ_LO * NCORE * 32
    for s, at in enumerate(ring_slots(y, crossed)):
        part = full_ref[:, pl.ds(pl.multiple_of(at * deep, deep), deep)]
        result = lax.dot_general(
            part, corr_ref[...], (((0,), (0,)), ((), ())), preferred_element_type=F32
        ).astype(BF16)
        for z in range(NZ_LO):
            shift = z ^ z_lo
            slot = lax.rem(shift, 2) * 2 + shift // 2
            for k in range(keep_ref.shape[2]):
                columns = slice(k * LANE, (k + 1) * LANE)
                even = result[z * 64 : z * 64 + 32, columns]
                odd = result[z * 64 + 32 : z * 64 + 64, columns]
                keep_ref[s, slot, k] = jnp.where(core == 0, even, odd)
                send_ref[s, slot, k] = jnp.where(core == 0, odd, even)


def product(crossed, pos, after, corr, gathered):
    tok, width = corr.shape
    part = jax.ShapeDtypeStruct((NY, NZ_LO, width // LANE, 32, LANE), BF16)
    vmem = pl.BlockSpec(memory_space=pltpu.VMEM)
    return pl.pallas_call(
        functools.partial(product_kernel, crossed),
        out_shape=(part, part),
        in_specs=[pl.BlockSpec(memory_space=pltpu.SMEM), pl.BlockSpec(memory_space=pl.ANY)]
        + [vmem] * 5,
        out_specs=(vmem,) * 2,
        scratch_shapes=[pltpu.VMEM((tok, 1024), BF16)],
        compiler_params=pltpu.CompilerParams(vmem_limit_bytes=VMEM_LIMIT),
        cost_estimate=SMALL_COST,
        name="product",
    )(pos, after, corr, *gathered)


def halve_kernel(_, mine_ref, other_ref, stay_ref, leave_ref):
    half = leave_ref.shape[0]
    stay_ref[...] = mine_ref[:half].astype(F32) + other_ref[:half].astype(F32)
    leave_ref[...] = (mine_ref[half:].astype(F32) + other_ref[half:].astype(F32)).astype(BF16)


def halve(after, mine, other):
    half = (mine.shape[0] // 2,) + mine.shape[1:]
    vmem = pl.BlockSpec(memory_space=pltpu.VMEM)
    return pl.pallas_call(
        halve_kernel,
        out_shape=(jax.ShapeDtypeStruct(half, F32), jax.ShapeDtypeStruct(half, BF16)),
        in_specs=[pl.BlockSpec(memory_space=pl.ANY), vmem, vmem],
        out_specs=(vmem, vmem),
        compiler_params=pltpu.CompilerParams(vmem_limit_bytes=VMEM_LIMIT),
        cost_estimate=SMALL_COST,
        name="halve",
    )(after, mine, other)


def add_kernel(_, mine_ref, other_ref, sum_ref):
    sum_ref[...] = (mine_ref[...] + other_ref[...].astype(F32)).astype(BF16)


def add(after, mine, other):
    vmem = pl.BlockSpec(memory_space=pltpu.VMEM)
    return pl.pallas_call(
        add_kernel,
        out_shape=jax.ShapeDtypeStruct(mine.shape, BF16),
        in_specs=[pl.BlockSpec(memory_space=pl.ANY), vmem, vmem],
        out_specs=vmem,
        compiler_params=pltpu.CompilerParams(vmem_limit_bytes=VMEM_LIMIT),
        cost_estimate=SMALL_COST,
        name="add",
    )(after, mine, other)


def share_kernel(pos_ref, _, *refs):
    corr_refs, proj_ref = refs[:-6], refs[-6]
    near_keep, near_send, far_keep, far_send, all_ref = refs[-5:]
    filt_count = proj_ref.shape[0]
    x, z_hi = coords(pos_ref)[:2]
    at = 0
    for part in corr_refs:
        all_ref[:, at : at + part.shape[1]] = part[...]
        at += part.shape[1]
    wide = NZ_HI * LANE
    near_slots = (near_keep, 0), (near_send, 0), (near_keep, 1), (near_send, 1)
    far_slots = (far_keep, 0), (far_keep, 1), (far_send, 0), (far_send, 1)
    for at, near, far in zip(ring_slots(x, False), near_slots, far_slots):
        base = pl.multiple_of(at * wide, wide)
        weights = jnp.concatenate(
            [proj_ref[k, pl.ds(base, wide), :] for k in range(filt_count)], axis=1
        )
        result = lax.dot_general(
            all_ref[...], weights, (((1,), (1,)), ((), ())), preferred_element_type=F32
        )
        low, high = result[:, :LANE], result[:, LANE:]
        near[0][near[1]] = jnp.where(z_hi == 0, low, high).astype(near[0].dtype)
        far[0][far[1]] = jnp.where(z_hi == 0, high, low).astype(far[0].dtype)


def input_shares(pos, after, corrs, projection):
    tok = corrs[0].shape[0]
    filt_count = projection.shape[0]
    vmem = pl.BlockSpec(memory_space=pltpu.VMEM)
    keep = jax.ShapeDtypeStruct((2, tok, LANE), F32)
    send = jax.ShapeDtypeStruct((2, tok, LANE), BF16)
    return pl.pallas_call(
        share_kernel,
        out_shape=(keep, send, keep, send),
        in_specs=[pl.BlockSpec(memory_space=pltpu.SMEM), pl.BlockSpec(memory_space=pl.ANY)]
        + [vmem] * (len(corrs) + 1),
        out_specs=(vmem,) * 4,
        scratch_shapes=[pltpu.VMEM((tok, filt_count * LANE), BF16)],
        compiler_params=pltpu.CompilerParams(vmem_limit_bytes=VMEM_LIMIT),
        cost_estimate=SMALL_COST,
        name="input_shares",
    )(pos, after, *corrs, projection)


GROUPS = 2


def per_device(inputs, grad_out, filters, projection):
    tp, ctx = lax.axis_index("tp"), lax.axis_index("ctx")
    pos = jnp.stack([tp, ctx]).astype(jnp.int32)

    def later(value, steps):
        return lax.ppermute(value, "ctx", from_later_chip(steps))

    def sibling(value):
        return lax.ppermute(value, "ctx", CORE_SWAP)

    def y_swapped(value, crossed):
        return lax.ppermute(value, "ctx", y_swap(crossed))

    def z_swapped(value, bit):
        return lax.ppermute(value, "ctx", z_swap(bit))

    def x_swapped(value, crossed):
        return lax.ppermute(value, "tp", x_swap(crossed))

    count = filters.shape[0] // GROUPS
    pair = jnp.stack([inputs, lax.ppermute(inputs, "tp", Z_HI_SWAP)])
    gathered = [pair] + [lax.ppermute(pair, "tp", along_x(s)) for s in range(1, NX)]
    table = near_table(filters)
    halo = [grad_out] + [later(grad_out, steps) for steps in range(1, 5)]
    beside = sibling(for_sibling(pos, (table, pair), *halo))
    accs = near_conv(table, halo[:3], beside, GROUPS)

    def conv(group, after):
        return far_conv(group * count, count, after, filters, accs[group], halo[2:], beside)

    corr_0 = conv(0, table)
    corr_1 = conv(1, corr_0)
    keep_0, send_0 = product(False, pos, corr_1, corr_0, gathered)
    near, near_send, far, far_send = input_shares(
        pos, send_0, [corr_0, corr_1], projection.transpose(1, 0, 2)
    )
    stay_0, leave_0 = halve(near_send, keep_0, sibling(send_0))
    y_0 = y_swapped(leave_0, False)
    keep_1, send_1 = product(True, pos, leave_0, corr_1, gathered)
    stay_1, leave_1 = halve(send_1, keep_1, sibling(send_1))
    y_1 = y_swapped(leave_1, True)
    far, leave = halve(leave_1, far, x_swapped(far_send, False))
    x_far = x_swapped(leave, True)
    stay_0, leave_0 = halve(leave, stay_0, y_0)
    y_0 = y_swapped(leave_0, True)
    near, leave = halve(leave_0, near, x_swapped(near_send, True))
    x_near = x_swapped(leave, False)
    stay_1, leave_1 = halve(leave, stay_1, y_1)
    y_1 = y_swapped(leave_1, False)
    far = add(leave_1, far, x_far)
    opposite = lax.ppermute(far, "tp", Z_HI_SWAP)

    stay_0, leave_0 = halve(far, stay_0[0], y_0[0])
    z_0 = z_swapped(leave_0, 1)
    stay_1, leave_1 = halve(leave_0, stay_1[0], y_1[0])
    z_1 = z_swapped(leave_1, 1)
    stay_0, leave_0 = halve(leave_1, stay_0, z_0)
    z_0 = z_swapped(leave_0, 2)
    stay_1, leave_1 = halve(leave_0, stay_1, z_1)
    z_1 = z_swapped(leave_1, 2)
    parts = [stay_0[0] + z_0[0].astype(F32), stay_1[0] + z_1[0].astype(F32)]
    grad_proj = jnp.concatenate(parts, axis=0).transpose(1, 0, 2)
    total = near[0] + x_near[0].astype(F32) + opposite[0].astype(F32)
    return total.astype(BF16), grad_proj


def solution(mesh):
    return jax.shard_map(
        per_device,
        mesh=mesh,
        in_specs=(P("ctx", "tp"), P("ctx", "tp"), P(), P(None, None, "tp")),
        out_specs=(P("ctx", "tp"), P("ctx", None, "tp")),
        check_vma=False,
    )
```

```python
import functools

import jax
import jax.numpy as jnp
from jax import lax
from jax.experimental import pallas as pl
from jax.experimental.pallas import tpu as pltpu
from jax.sharding import PartitionSpec as P

BF16, F32 = jnp.bfloat16, jnp.float32
ROWS = 64
LANE = 128
NX, NZ_HI, NY, NZ_LO, NCORE = 4, 2, 4, 4, 2
CHIPS = NY * NZ_LO
VMEM_LIMIT = 20 * 1024 * 1024
LARGE_COST = pl.CostEstimate(flops=4_000_000_000, bytes_accessed=8_000_000, transcendentals=0)
SMALL_COST = pl.CostEstimate(flops=1000, bytes_accessed=1000, transcendentals=0)


def ctx_of(y, z, core):
    return (y * NZ_LO + z) * NCORE + core


CTX = [(y, z, core) for y in range(NY) for z in range(NZ_LO) for core in range(NCORE)]
TP = [(x, z) for x in range(NX) for z in range(NZ_HI)]
CORE_SWAP = [(ctx_of(y, z, c), ctx_of(y, z, 1 - c)) for y, z, c in CTX]
Z_HI_SWAP = [(x * NZ_HI + z, x * NZ_HI + 1 - z) for x, z in TP]


def ring_partner(at, crossed):
    return NX - 1 - at if crossed else at ^ 1


def ring_slots(at, crossed):
    near, far = ring_partner(at, crossed), ring_partner(at, not crossed)
    return at, far, near, ring_partner(near, not crossed)


def y_swap(crossed):
    return [(ctx_of(y, z, c), ctx_of(ring_partner(y, crossed), z, c)) for y, z, c in CTX]


def x_swap(crossed):
    return [(x * NZ_HI + z, ring_partner(x, crossed) * NZ_HI + z) for x, z in TP]


def z_swap(bit):
    return [(ctx_of(y, z, c), ctx_of(y, z ^ bit, c)) for y, z, c in CTX]


def along_x(steps):
    return [(x * NZ_HI + z, (x + steps) % NX * NZ_HI + z) for x, z in TP]


def from_later_chip(steps):
    return [
        (NCORE * (chip + steps) + core, NCORE * chip + core)
        for chip in range(CHIPS - steps)
        for core in range(NCORE)
    ]


def shifted_rows(line, rows):
    block = jnp.broadcast_to(line, (rows, line.shape[1]))
    return pltpu.roll(block, 0, 1, stride=1, stride_axis=0).astype(BF16)


def table_kernel(filters_ref, grad_ref, in_ref, near_ref, grad_copy_ref, in_copy_ref):
    grad_copy_ref[...] = grad_ref[...]
    in_copy_ref[...] = in_ref[...]
    filt_count, rows, near = near_ref.shape
    edge = jnp.zeros((1, LANE), F32)
    for k in range(filt_count):
        line = filters_ref[k : k + 1, :near].astype(F32)
        near_ref[k] = shifted_rows(jnp.concatenate([line, edge], axis=1), rows)[:, :near]


def near_table(filters, grad_out, inputs):
    filt_count, taps = filters.shape
    block = jax.ShapeDtypeStruct(grad_out.shape, BF16)
    vmem = pl.BlockSpec(memory_space=pltpu.VMEM)
    return pl.pallas_call(
        table_kernel,
        out_shape=(jax.ShapeDtypeStruct((filt_count, ROWS, taps // 2), BF16), block, block),
        in_specs=[vmem] * 3,
        out_specs=[vmem] * 3,
        compiler_params=pltpu.CompilerParams(vmem_limit_bytes=VMEM_LIMIT),
        cost_estimate=LARGE_COST,
        name="near_table",
    )(filters, grad_out, inputs)


def prep_kernel(pos_ref, own_ref, r1_ref, r2_ref, r3_ref, r4_ref, in_ref, far_in_ref, stack_ref, pair_ref):
    parts = own_ref, r1_ref, r2_ref, r3_ref, r4_ref
    core = lax.rem(pos_ref[1], NCORE)
    for s in range(stack_ref.shape[0]):
        stack_ref[s] = jnp.where(core == 0, parts[s + 1][...], parts[s][...])
    pair_ref[0] = in_ref[...]
    pair_ref[1] = far_in_ref[...]


def prepare(pos, *parts):
    block = parts[0].shape
    vmem = pl.BlockSpec(memory_space=pltpu.VMEM)
    return pl.pallas_call(
        prep_kernel,
        out_shape=(
            jax.ShapeDtypeStruct((4,) + block, BF16),
            jax.ShapeDtypeStruct((2,) + block, BF16),
        ),
        in_specs=[pl.BlockSpec(memory_space=pltpu.SMEM)] + [vmem] * len(parts),
        out_specs=(vmem, vmem),
        compiler_params=pltpu.CompilerParams(vmem_limit_bytes=VMEM_LIMIT),
        cost_estimate=SMALL_COST,
        name="prepare",
    )(pos, *parts)


def pair_of_blocks(grad_ref, start, rows, width):
    first = grad_ref[pl.ds(start, width), :]
    second = grad_ref[pl.ds(start + rows, width), :]
    return jnp.concatenate([first, second], axis=1)


def coords(pos_ref):
    x, z_hi = pos_ref[0] // NZ_HI, lax.rem(pos_ref[0], NZ_HI)
    chip, core = pos_ref[1] // NCORE, lax.rem(pos_ref[1], NCORE)
    return x, z_hi, chip // NZ_LO, lax.rem(chip, NZ_LO), core


def lay_out(grad_ref, refs):
    tok = refs[0].shape[0]
    for s, part in enumerate(refs):
        grad_ref[s * tok : (s + 1) * tok, :] = part[...]


def near_kernel(table_ref, own_ref, r1_ref, r2_ref, sib_ref, *refs):
    acc_refs, grad_ref = refs[:-1], refs[-1]
    filt_count, rows, width = table_ref.shape
    tok = own_ref.shape[0]
    lay_out(grad_ref, (own_ref, sib_ref.at[0], r1_ref, sib_ref.at[1], r2_ref))
    table = table_ref[...].reshape(filt_count * rows, width)

    @pl.loop(0, tok // (2 * rows), unroll=True)
    def _(pair):
        start = pl.multiple_of(pair * (2 * rows), 2 * rows)
        both = pair_of_blocks(grad_ref, start, rows, width)
        result = jnp.dot(table, both, preferred_element_type=F32)
        part = acc_refs[0].shape[1]
        for group, acc_ref in enumerate(acc_refs):
            acc_ref[pair] = result[group * part : (group + 1) * part]


def near_conv(table, halo, sibling, groups):
    filt_count, rows, width = table.shape
    tok = halo[0].shape[0]
    vmem = pl.BlockSpec(memory_space=pltpu.VMEM)
    acc = jax.ShapeDtypeStruct((tok // (2 * rows), filt_count // groups * rows, 2 * LANE), F32)
    return pl.pallas_call(
        near_kernel,
        out_shape=[acc] * groups,
        in_specs=[vmem] * 5,
        out_specs=[vmem] * groups,
        scratch_shapes=[pltpu.VMEM((5 * tok, LANE), BF16)],
        compiler_params=pltpu.CompilerParams(vmem_limit_bytes=VMEM_LIMIT),
        cost_estimate=LARGE_COST,
        name="near_conv",
    )(table, *halo, sibling)


def far_kernel(
    first, _, filters_ref, acc_ref, r2_ref, r3_ref, r4_ref, sib_ref,
    corr_ref, grad_ref, table_ref,
):
    filt_count, rows, width = table_ref.shape
    tok = r2_ref.shape[0]
    edge = jnp.zeros((1, LANE), F32)
    start = filters_ref.shape[1] + LANE - width - LANE
    for k in range(filt_count):
        line = filters_ref[first + k : first + k + 1, start:].astype(F32)
        table_ref[k] = shifted_rows(jnp.concatenate([line, edge], axis=1), rows)[:, LANE:]
    lay_out(grad_ref, (r2_ref, sib_ref.at[2], r3_ref, sib_ref.at[3], r4_ref))
    grad_ref[5 * tok :, :] = jnp.zeros((grad_ref.shape[0] - 5 * tok, LANE), BF16)

    @pl.loop(0, tok // (2 * rows), unroll=True)
    def _(pair):
        start = pl.multiple_of(pair * (2 * rows), 2 * rows)
        both = pair_of_blocks(grad_ref, start, rows, width)
        table = table_ref[...].reshape(filt_count * rows, width)
        result = jnp.dot(table, both, preferred_element_type=F32)
        result = (result + acc_ref[pair]).astype(BF16)
        for k in range(filt_count):
            for half in range(2):
                corr_ref[pl.ds(start + half * rows, rows), k * LANE : (k + 1) * LANE] = result[
                    k * rows : (k + 1) * rows, half * LANE : (half + 1) * LANE
                ]


def far_conv(first, count, after, filters, acc, halo, sibling):
    tok = halo[0].shape[0]
    width = filters.shape[1] // 2 + LANE
    vmem = pl.BlockSpec(memory_space=pltpu.VMEM)
    return pl.pallas_call(
        functools.partial(far_kernel, first),
        out_shape=jax.ShapeDtypeStruct((tok, count * LANE), BF16),
        in_specs=[pl.BlockSpec(memory_space=pl.ANY)] + [vmem] * 6,
        out_specs=vmem,
        scratch_shapes=[
            pltpu.VMEM((5 * tok + ROWS, LANE), BF16),
            pltpu.VMEM((count, ROWS, width), BF16),
        ],
        compiler_params=pltpu.CompilerParams(vmem_limit_bytes=VMEM_LIMIT),
        cost_estimate=SMALL_COST,
        name="far_conv",
    )(after, filters, acc, *halo, sibling)


def product_kernel(
    crossed, pos_ref, _, corr_ref, x0_ref, x1_ref, x2_ref, x3_ref, keep_ref, send_ref, full_ref
):
    x, z_hi, y, z_lo, core = coords(pos_ref)
    for s, part in enumerate((x0_ref, x1_ref, x2_ref, x3_ref)):
        for h in range(NZ_HI):
            at = lax.rem(x + NX - s, NX) * NZ_HI + lax.rem(z_hi + h, NZ_HI)
            full_ref[:, pl.ds(pl.multiple_of(at * LANE, LANE), LANE)] = part[h]

    deep = NZ_LO * NCORE * 32
    for s, at in enumerate(ring_slots(y, crossed)):
        part = full_ref[:, pl.ds(pl.multiple_of(at * deep, deep), deep)]
        result = lax.dot_general(
            part, corr_ref[...], (((0,), (0,)), ((), ())), preferred_element_type=F32
        ).astype(BF16)
        for z in range(NZ_LO):
            shift = z ^ z_lo
            slot = lax.rem(shift, 2) * 2 + shift // 2
            for k in range(keep_ref.shape[2]):
                columns = slice(k * LANE, (k + 1) * LANE)
                even = result[z * 64 : z * 64 + 32, columns]
                odd = result[z * 64 + 32 : z * 64 + 64, columns]
                keep_ref[s, slot, k] = jnp.where(core == 0, even, odd)
                send_ref[s, slot, k] = jnp.where(core == 0, odd, even)


def product(crossed, pos, after, corr, gathered):
    tok, width = corr.shape
    part = jax.ShapeDtypeStruct((NY, NZ_LO, width // LANE, 32, LANE), BF16)
    vmem = pl.BlockSpec(memory_space=pltpu.VMEM)
    return pl.pallas_call(
        functools.partial(product_kernel, crossed),
        out_shape=(part, part),
        in_specs=[pl.BlockSpec(memory_space=pltpu.SMEM), pl.BlockSpec(memory_space=pl.ANY)]
        + [vmem] * 5,
        out_specs=(vmem,) * 2,
        scratch_shapes=[pltpu.VMEM((tok, 1024), BF16)],
        compiler_params=pltpu.CompilerParams(vmem_limit_bytes=VMEM_LIMIT),
        cost_estimate=SMALL_COST,
        name="product",
    )(pos, after, corr, *gathered)


def halve_kernel(_, mine_ref, other_ref, stay_ref, leave_ref):
    half = leave_ref.shape[0]
    stay_ref[...] = mine_ref[:half].astype(F32) + other_ref[:half].astype(F32)
    leave_ref[...] = (mine_ref[half:].astype(F32) + other_ref[half:].astype(F32)).astype(BF16)


def halve(after, mine, other):
    half = (mine.shape[0] // 2,) + mine.shape[1:]
    vmem = pl.BlockSpec(memory_space=pltpu.VMEM)
    return pl.pallas_call(
        halve_kernel,
        out_shape=(jax.ShapeDtypeStruct(half, F32), jax.ShapeDtypeStruct(half, BF16)),
        in_specs=[pl.BlockSpec(memory_space=pl.ANY), vmem, vmem],
        out_specs=(vmem, vmem),
        compiler_params=pltpu.CompilerParams(vmem_limit_bytes=VMEM_LIMIT),
        cost_estimate=SMALL_COST,
        name="halve",
    )(after, mine, other)


def add_kernel(_, mine_ref, other_ref, sum_ref):
    sum_ref[...] = (mine_ref[...] + other_ref[...].astype(F32)).astype(BF16)


def add(after, mine, other):
    vmem = pl.BlockSpec(memory_space=pltpu.VMEM)
    return pl.pallas_call(
        add_kernel,
        out_shape=jax.ShapeDtypeStruct(mine.shape, BF16),
        in_specs=[pl.BlockSpec(memory_space=pl.ANY), vmem, vmem],
        out_specs=vmem,
        compiler_params=pltpu.CompilerParams(vmem_limit_bytes=VMEM_LIMIT),
        cost_estimate=SMALL_COST,
        name="add",
    )(after, mine, other)


def share_kernel(pos_ref, _, *refs):
    corr_refs, proj_ref = refs[:-6], refs[-6]
    near_keep, near_send, far_keep, far_send, all_ref = refs[-5:]
    filt_count = proj_ref.shape[0]
    x, z_hi = coords(pos_ref)[:2]
    at = 0
    for part in corr_refs:
        all_ref[:, at : at + part.shape[1]] = part[...]
        at += part.shape[1]
    wide = NZ_HI * LANE
    near_slots = (near_keep, 0), (near_send, 0), (near_keep, 1), (near_send, 1)
    far_slots = (far_keep, 0), (far_keep, 1), (far_send, 0), (far_send, 1)
    for at, near, far in zip(ring_slots(x, False), near_slots, far_slots):
        base = pl.multiple_of(at * wide, wide)
        weights = jnp.concatenate(
            [proj_ref[k, pl.ds(base, wide), :] for k in range(filt_count)], axis=1
        )
        result = lax.dot_general(
            all_ref[...], weights, (((1,), (1,)), ((), ())), preferred_element_type=F32
        )
        low, high = result[:, :LANE], result[:, LANE:]
        near[0][near[1]] = jnp.where(z_hi == 0, low, high).astype(near[0].dtype)
        far[0][far[1]] = jnp.where(z_hi == 0, high, low).astype(far[0].dtype)


def input_shares(pos, after, corrs, projection):
    tok = corrs[0].shape[0]
    filt_count = projection.shape[0]
    vmem = pl.BlockSpec(memory_space=pltpu.VMEM)
    keep = jax.ShapeDtypeStruct((2, tok, LANE), F32)
    send = jax.ShapeDtypeStruct((2, tok, LANE), BF16)
    return pl.pallas_call(
        share_kernel,
        out_shape=(keep, send, keep, send),
        in_specs=[pl.BlockSpec(memory_space=pltpu.SMEM), pl.BlockSpec(memory_space=pl.ANY)]
        + [vmem] * (len(corrs) + 1),
        out_specs=(vmem,) * 4,
        scratch_shapes=[pltpu.VMEM((tok, filt_count * LANE), BF16)],
        compiler_params=pltpu.CompilerParams(vmem_limit_bytes=VMEM_LIMIT),
        cost_estimate=SMALL_COST,
        name="input_shares",
    )(pos, after, *corrs, projection)


GROUPS = 2


def per_device(inputs, grad_out, filters, projection):
    tp, ctx = lax.axis_index("tp"), lax.axis_index("ctx")
    pos = jnp.stack([tp, ctx]).astype(jnp.int32)

    def later(value, steps):
        return lax.ppermute(value, "ctx", from_later_chip(steps))

    def sibling(value):
        return lax.ppermute(value, "ctx", CORE_SWAP)

    def y_swapped(value, crossed):
        return lax.ppermute(value, "ctx", y_swap(crossed))

    def z_swapped(value, bit):
        return lax.ppermute(value, "ctx", z_swap(bit))

    def x_swapped(value, crossed):
        return lax.ppermute(value, "tp", x_swap(crossed))

    count = filters.shape[0] // GROUPS
    table, grad_copy, in_copy = near_table(filters, grad_out, inputs)
    halo = [grad_copy] + [later(grad_out, steps) for steps in range(1, 5)]
    stack, pair = prepare(pos, *halo, in_copy, lax.ppermute(inputs, "tp", Z_HI_SWAP))
    gathered = [pair] + [lax.ppermute(pair, "tp", along_x(s)) for s in range(1, NX)]
    beside = sibling(stack)
    accs = near_conv(table, halo[:3], beside, GROUPS)

    def conv(group, after):
        return far_conv(group * count, count, after, filters, accs[group], halo[2:], beside)

    corr_0 = conv(0, table)
    corr_1 = conv(1, corr_0)
    near, near_send, far, far_send = input_shares(
        pos, corr_1, [corr_0, corr_1], projection.transpose(1, 0, 2)
    )
    x_far, x_near = x_swapped(far_send, False), x_swapped(near_send, True)
    keep_0, send_0 = product(False, pos, near_send, corr_0, gathered)
    keep_1, send_1 = product(True, pos, send_0, corr_1, gathered)
    stay_0, leave_0 = halve(send_1, keep_0, sibling(send_0))
    y_0 = y_swapped(leave_0, False)
    stay_1, leave_1 = halve(leave_0, keep_1, sibling(send_1))
    y_1 = y_swapped(leave_1, True)
    far, leave = halve(leave_1, far, x_far)
    x_far = x_swapped(leave, True)
    near, leave = halve(leave, near, x_near)
    x_near = x_swapped(leave, False)
    stay_0, leave_0 = halve(leave, stay_0, y_0)
    y_0 = y_swapped(leave_0, True)
    stay_1, leave_1 = halve(leave_0, stay_1, y_1)
    y_1 = y_swapped(leave_1, False)
    far = add(leave_1, far, x_far)
    opposite = lax.ppermute(far, "tp", Z_HI_SWAP)

    stay_0, leave_0 = halve(far, stay_0[0], y_0[0])
    z_0 = z_swapped(leave_0, 1)
    stay_1, leave_1 = halve(leave_0, stay_1[0], y_1[0])
    z_1 = z_swapped(leave_1, 1)
    stay_0, leave_0 = halve(leave_1, stay_0, z_0)
    z_0 = z_swapped(leave_0, 2)
    stay_1, leave_1 = halve(leave_0, stay_1, z_1)
    z_1 = z_swapped(leave_1, 2)
    parts = [stay_0[0] + z_0[0].astype(F32), stay_1[0] + z_1[0].astype(F32)]
    grad_proj = jnp.concatenate(parts, axis=0).transpose(1, 0, 2)
    total = near[0] + x_near[0].astype(F32) + opposite[0].astype(F32)
    return total.astype(BF16), grad_proj


def solution(mesh):
    return jax.shard_map(
        per_device,
        mesh=mesh,
        in_specs=(P("ctx", "tp"), P("ctx", "tp"), P(), P(None, None, "tp")),
        out_specs=(P("ctx", "tp"), P("ctx", None, "tp")),
        check_vma=False,
    )
```

```python
import functools

import jax
import jax.numpy as jnp
from jax import lax
from jax.experimental import pallas as pl
from jax.experimental.pallas import tpu as pltpu
from jax.sharding import PartitionSpec as P

BF16, F32 = jnp.bfloat16, jnp.float32
ROWS = 64
LANE = 128
NX, NZ_HI, NY, NZ_LO, NCORE = 4, 2, 4, 4, 2
CHIPS = NY * NZ_LO
VMEM_LIMIT = 20 * 1024 * 1024
LARGE_COST = pl.CostEstimate(flops=4_000_000_000, bytes_accessed=8_000_000, transcendentals=0)
SMALL_COST = pl.CostEstimate(flops=1000, bytes_accessed=1000, transcendentals=0)


def ctx_of(y, z, core):
    return (y * NZ_LO + z) * NCORE + core


CTX = [(y, z, core) for y in range(NY) for z in range(NZ_LO) for core in range(NCORE)]
TP = [(x, z) for x in range(NX) for z in range(NZ_HI)]
CORE_SWAP = [(ctx_of(y, z, c), ctx_of(y, z, 1 - c)) for y, z, c in CTX]
Z_HI_SWAP = [(x * NZ_HI + z, x * NZ_HI + 1 - z) for x, z in TP]


def ring_partner(at, crossed):
    return NX - 1 - at if crossed else at ^ 1


def ring_slots(at, crossed):
    near, far = ring_partner(at, crossed), ring_partner(at, not crossed)
    return at, far, near, ring_partner(near, not crossed)


def y_swap(crossed):
    return [(ctx_of(y, z, c), ctx_of(ring_partner(y, crossed), z, c)) for y, z, c in CTX]


def x_swap(crossed):
    return [(x * NZ_HI + z, ring_partner(x, crossed) * NZ_HI + z) for x, z in TP]


def z_swap(bit):
    return [(ctx_of(y, z, c), ctx_of(y, z ^ bit, c)) for y, z, c in CTX]


def along_x(steps):
    return [(x * NZ_HI + z, (x + steps) % NX * NZ_HI + z) for x, z in TP]


def from_later_chip(steps):
    return [
        (NCORE * (chip + steps) + core, NCORE * chip + core)
        for chip in range(CHIPS - steps)
        for core in range(NCORE)
    ]


def shifted_rows(line, rows):
    block = jnp.broadcast_to(line, (rows, line.shape[1]))
    return pltpu.roll(block, 0, 1, stride=1, stride_axis=0).astype(BF16)


def table_kernel(_, filters_ref, near_ref):
    filt_count, rows, near = near_ref.shape
    edge = jnp.zeros((1, LANE), F32)
    for k in range(filt_count):
        line = filters_ref[k : k + 1, :near].astype(F32)
        near_ref[k] = shifted_rows(jnp.concatenate([line, edge], axis=1), rows)[:, :near]


def near_table(after, filters):
    filt_count, taps = filters.shape
    vmem = pl.BlockSpec(memory_space=pltpu.VMEM)
    return pl.pallas_call(
        table_kernel,
        out_shape=jax.ShapeDtypeStruct((filt_count, ROWS, taps // 2), BF16),
        in_specs=[pl.BlockSpec(memory_space=pl.ANY), vmem],
        out_specs=vmem,
        compiler_params=pltpu.CompilerParams(vmem_limit_bytes=VMEM_LIMIT),
        cost_estimate=SMALL_COST,
        name="near_table",
    )(after, filters)


def prep_kernel(pos_ref, _, own_ref, r1_ref, r2_ref, r3_ref, r4_ref, stack_ref, held_ref, arrived):
    copy = pltpu.make_async_copy(own_ref, held_ref, arrived)
    copy.start()
    parts = r1_ref, r2_ref, r3_ref, r4_ref
    core = lax.rem(pos_ref[1], NCORE)
    for s in range(1, stack_ref.shape[0]):
        stack_ref[s] = jnp.where(core == 0, parts[s][...], parts[s - 1][...])
    copy.wait()
    stack_ref[0] = jnp.where(core == 0, r1_ref[...], held_ref[...])


def for_sibling(pos, after, *parts):
    block = parts[0].shape
    vmem = pl.BlockSpec(memory_space=pltpu.VMEM)
    return pl.pallas_call(
        prep_kernel,
        out_shape=jax.ShapeDtypeStruct((4,) + block, BF16),
        in_specs=[pl.BlockSpec(memory_space=pltpu.SMEM)]
        + [pl.BlockSpec(memory_space=pl.ANY)] * 2
        + [vmem] * 4,
        out_specs=vmem,
        scratch_shapes=[pltpu.VMEM(block, BF16), pltpu.SemaphoreType.DMA],
        compiler_params=pltpu.CompilerParams(vmem_limit_bytes=VMEM_LIMIT),
        cost_estimate=SMALL_COST,
        name="for_sibling",
    )(pos, after, *parts)


def pair_of_blocks(grad_ref, start, rows, width):
    first = grad_ref[pl.ds(start, width), :]
    second = grad_ref[pl.ds(start + rows, width), :]
    return jnp.concatenate([first, second], axis=1)


def coords(pos_ref):
    x, z_hi = pos_ref[0] // NZ_HI, lax.rem(pos_ref[0], NZ_HI)
    chip, core = pos_ref[1] // NCORE, lax.rem(pos_ref[1], NCORE)
    return x, z_hi, chip // NZ_LO, lax.rem(chip, NZ_LO), core


def lay_out(grad_ref, refs):
    tok = refs[0].shape[0]
    for s, part in enumerate(refs):
        grad_ref[s * tok : (s + 1) * tok, :] = part[...]


def near_kernel(table_ref, own_ref, r1_ref, r2_ref, sib_ref, *refs):
    acc_refs, grad_ref = refs[:-1], refs[-1]
    filt_count, rows, width = table_ref.shape
    tok = own_ref.shape[0]
    lay_out(grad_ref, (own_ref, sib_ref.at[0], r1_ref, sib_ref.at[1], r2_ref))
    table = table_ref[...].reshape(filt_count * rows, width)

    @pl.loop(0, tok // (2 * rows), unroll=True)
    def _(pair):
        start = pl.multiple_of(pair * (2 * rows), 2 * rows)
        both = pair_of_blocks(grad_ref, start, rows, width)
        result = jnp.dot(table, both, preferred_element_type=F32)
        part = acc_refs[0].shape[1]
        for group, acc_ref in enumerate(acc_refs):
            acc_ref[pair] = result[group * part : (group + 1) * part]


def near_conv(after, table, halo, sibling, groups):
    filt_count, rows, width = table.shape
    tok = halo[0].shape[0]
    vmem = pl.BlockSpec(memory_space=pltpu.VMEM)
    acc = jax.ShapeDtypeStruct((tok // (2 * rows), filt_count // groups * rows, 2 * LANE), F32)
    return pl.pallas_call(
        near_kernel,
        out_shape=[acc] * groups,
        in_specs=[pl.BlockSpec(memory_space=pl.ANY)] * len(after) + [vmem] * 5,
        out_specs=[vmem] * groups,
        scratch_shapes=[pltpu.VMEM((5 * tok, LANE), BF16)],
        compiler_params=pltpu.CompilerParams(vmem_limit_bytes=VMEM_LIMIT),
        cost_estimate=LARGE_COST,
        name="near_conv",
    )(*after, table, *halo, sibling)


def far_kernel(
    first, _, filters_ref, acc_ref, r2_ref, r3_ref, r4_ref, sib_ref,
    corr_ref, grad_ref, table_ref,
):
    filt_count, rows, width = table_ref.shape
    tok = r2_ref.shape[0]
    edge = jnp.zeros((1, LANE), F32)
    start = filters_ref.shape[1] + LANE - width - LANE
    for k in range(filt_count):
        line = filters_ref[first + k : first + k + 1, start:].astype(F32)
        table_ref[k] = shifted_rows(jnp.concatenate([line, edge], axis=1), rows)[:, LANE:]
    lay_out(grad_ref, (r2_ref, sib_ref.at[2], r3_ref, sib_ref.at[3], r4_ref))
    grad_ref[5 * tok :, :] = jnp.zeros((grad_ref.shape[0] - 5 * tok, LANE), BF16)

    @pl.loop(0, tok // (2 * rows), unroll=True)
    def _(pair):
        start = pl.multiple_of(pair * (2 * rows), 2 * rows)
        both = pair_of_blocks(grad_ref, start, rows, width)
        table = table_ref[...].reshape(filt_count * rows, width)
        result = jnp.dot(table, both, preferred_element_type=F32)
        result = (result + acc_ref[pair]).astype(BF16)
        for k in range(filt_count):
            for half in range(2):
                corr_ref[pl.ds(start + half * rows, rows), k * LANE : (k + 1) * LANE] = result[
                    k * rows : (k + 1) * rows, half * LANE : (half + 1) * LANE
                ]


def far_conv(first, count, after, filters, acc, halo, sibling):
    tok = halo[0].shape[0]
    width = filters.shape[1] // 2 + LANE
    vmem = pl.BlockSpec(memory_space=pltpu.VMEM)
    return pl.pallas_call(
        functools.partial(far_kernel, first),
        out_shape=jax.ShapeDtypeStruct((tok, count * LANE), BF16),
        in_specs=[pl.BlockSpec(memory_space=pl.ANY)] + [vmem] * 6,
        out_specs=vmem,
        scratch_shapes=[
            pltpu.VMEM((5 * tok + ROWS, LANE), BF16),
            pltpu.VMEM((count, ROWS, width), BF16),
        ],
        compiler_params=pltpu.CompilerParams(vmem_limit_bytes=VMEM_LIMIT),
        cost_estimate=SMALL_COST,
        name="far_conv",
    )(after, filters, acc, *halo, sibling)


def product_kernel(
    crossed, pos_ref, _, corr_ref, x0_ref, x1_ref, x2_ref, x3_ref, keep_ref, send_ref, full_ref
):
    x, z_hi, y, z_lo, core = coords(pos_ref)
    for s, part in enumerate((x0_ref, x1_ref, x2_ref, x3_ref)):
        for h in range(NZ_HI):
            at = lax.rem(x + NX - s, NX) * NZ_HI + lax.rem(z_hi + h, NZ_HI)
            full_ref[:, pl.ds(pl.multiple_of(at * LANE, LANE), LANE)] = part[h]

    deep = NZ_LO * NCORE * 32
    for s, at in enumerate(ring_slots(y, crossed)):
        part = full_ref[:, pl.ds(pl.multiple_of(at * deep, deep), deep)]
        result = lax.dot_general(
            part, corr_ref[...], (((0,), (0,)), ((), ())), preferred_element_type=F32
        ).astype(BF16)
        for z in range(NZ_LO):
            shift = z ^ z_lo
            slot = lax.rem(shift, 2) * 2 + shift // 2
            for k in range(keep_ref.shape[2]):
                columns = slice(k * LANE, (k + 1) * LANE)
                even = result[z * 64 : z * 64 + 32, columns]
                odd = result[z * 64 + 32 : z * 64 + 64, columns]
                keep_ref[s, slot, k] = jnp.where(core == 0, even, odd)
                send_ref[s, slot, k] = jnp.where(core == 0, odd, even)


def product(crossed, pos, after, corr, gathered):
    tok, width = corr.shape
    part = jax.ShapeDtypeStruct((NY, NZ_LO, width // LANE, 32, LANE), BF16)
    vmem = pl.BlockSpec(memory_space=pltpu.VMEM)
    return pl.pallas_call(
        functools.partial(product_kernel, crossed),
        out_shape=(part, part),
        in_specs=[pl.BlockSpec(memory_space=pltpu.SMEM), pl.BlockSpec(memory_space=pl.ANY)]
        + [vmem] * 5,
        out_specs=(vmem,) * 2,
        scratch_shapes=[pltpu.VMEM((tok, 1024), BF16)],
        compiler_params=pltpu.CompilerParams(vmem_limit_bytes=VMEM_LIMIT),
        cost_estimate=SMALL_COST,
        name="product",
    )(pos, after, corr, *gathered)


def halve_kernel(_, mine_ref, other_ref, stay_ref, leave_ref):
    half = leave_ref.shape[0]
    stay_ref[...] = mine_ref[:half].astype(F32) + other_ref[:half].astype(F32)
    leave_ref[...] = (mine_ref[half:].astype(F32) + other_ref[half:].astype(F32)).astype(BF16)


def halve(after, mine, other):
    half = (mine.shape[0] // 2,) + mine.shape[1:]
    vmem = pl.BlockSpec(memory_space=pltpu.VMEM)
    return pl.pallas_call(
        halve_kernel,
        out_shape=(jax.ShapeDtypeStruct(half, F32), jax.ShapeDtypeStruct(half, BF16)),
        in_specs=[pl.BlockSpec(memory_space=pl.ANY), vmem, vmem],
        out_specs=(vmem, vmem),
        compiler_params=pltpu.CompilerParams(vmem_limit_bytes=VMEM_LIMIT),
        cost_estimate=SMALL_COST,
        name="halve",
    )(after, mine, other)


def add_kernel(_, mine_ref, other_ref, sum_ref):
    sum_ref[...] = (mine_ref[...] + other_ref[...].astype(F32)).astype(BF16)


def add(after, mine, other):
    vmem = pl.BlockSpec(memory_space=pltpu.VMEM)
    return pl.pallas_call(
        add_kernel,
        out_shape=jax.ShapeDtypeStruct(mine.shape, BF16),
        in_specs=[pl.BlockSpec(memory_space=pl.ANY), vmem, vmem],
        out_specs=vmem,
        compiler_params=pltpu.CompilerParams(vmem_limit_bytes=VMEM_LIMIT),
        cost_estimate=SMALL_COST,
        name="add",
    )(after, mine, other)


def share_kernel(pos_ref, _, *refs):
    corr_refs, proj_ref = refs[:-6], refs[-6]
    near_keep, near_send, far_keep, far_send, all_ref = refs[-5:]
    filt_count = proj_ref.shape[0]
    x, z_hi = coords(pos_ref)[:2]
    at = 0
    for part in corr_refs:
        all_ref[:, at : at + part.shape[1]] = part[...]
        at += part.shape[1]
    wide = NZ_HI * LANE
    near_slots = (near_keep, 0), (near_send, 0), (near_keep, 1), (near_send, 1)
    far_slots = (far_keep, 0), (far_keep, 1), (far_send, 0), (far_send, 1)
    for at, near, far in zip(ring_slots(x, False), near_slots, far_slots):
        base = pl.multiple_of(at * wide, wide)
        weights = jnp.concatenate(
            [proj_ref[k, pl.ds(base, wide), :] for k in range(filt_count)], axis=1
        )
        result = lax.dot_general(
            all_ref[...], weights, (((1,), (1,)), ((), ())), preferred_element_type=F32
        )
        low, high = result[:, :LANE], result[:, LANE:]
        near[0][near[1]] = jnp.where(z_hi == 0, low, high).astype(near[0].dtype)
        far[0][far[1]] = jnp.where(z_hi == 0, high, low).astype(far[0].dtype)


def input_shares(pos, after, corrs, projection):
    tok = corrs[0].shape[0]
    filt_count = projection.shape[0]
    vmem = pl.BlockSpec(memory_space=pltpu.VMEM)
    keep = jax.ShapeDtypeStruct((2, tok, LANE), F32)
    send = jax.ShapeDtypeStruct((2, tok, LANE), BF16)
    return pl.pallas_call(
        share_kernel,
        out_shape=(keep, send, keep, send),
        in_specs=[pl.BlockSpec(memory_space=pltpu.SMEM), pl.BlockSpec(memory_space=pl.ANY)]
        + [vmem] * (len(corrs) + 1),
        out_specs=(vmem,) * 4,
        scratch_shapes=[pltpu.VMEM((tok, filt_count * LANE), BF16)],
        compiler_params=pltpu.CompilerParams(vmem_limit_bytes=VMEM_LIMIT),
        cost_estimate=SMALL_COST,
        name="input_shares",
    )(pos, after, *corrs, projection)


GROUPS = 2


def per_device(inputs, grad_out, filters, projection):
    tp, ctx = lax.axis_index("tp"), lax.axis_index("ctx")
    pos = jnp.stack([tp, ctx]).astype(jnp.int32)

    def later(value, steps):
        return lax.ppermute(value, "ctx", from_later_chip(steps))

    def sibling(value):
        return lax.ppermute(value, "ctx", CORE_SWAP)

    def y_swapped(value, crossed):
        return lax.ppermute(value, "ctx", y_swap(crossed))

    def z_swapped(value, bit):
        return lax.ppermute(value, "ctx", z_swap(bit))

    def x_swapped(value, crossed):
        return lax.ppermute(value, "tp", x_swap(crossed))

    count = filters.shape[0] // GROUPS
    pair = jnp.stack([inputs, lax.ppermute(inputs, "tp", Z_HI_SWAP)])
    gathered = [pair] + [lax.ppermute(pair, "tp", along_x(s)) for s in range(1, NX)]
    table = near_table(pair, filters)
    halo = [grad_out] + [later(grad_out, steps) for steps in range(1, 5)]
    beside = sibling(for_sibling(pos, table, *halo))
    accs = near_conv(gathered[1:1], table, halo[:3], beside, GROUPS)

    def conv(group, after):
        return far_conv(group * count, count, after, filters, accs[group], halo[2:], beside)

    corr_0 = conv(0, table)
    corr_1 = conv(1, corr_0)
    near, near_send, far, far_send = input_shares(
        pos, corr_1, [corr_0, corr_1], projection.transpose(1, 0, 2)
    )
    x_far, x_near = x_swapped(far_send, False), x_swapped(near_send, True)
    keep_0, send_0 = product(False, pos, near_send, corr_0, gathered)
    keep_1, send_1 = product(True, pos, send_0, corr_1, gathered)
    stay_0, leave_0 = halve(send_1, keep_0, sibling(send_0))
    y_0 = y_swapped(leave_0, False)
    stay_1, leave_1 = halve(leave_0, keep_1, sibling(send_1))
    y_1 = y_swapped(leave_1, True)
    far, leave = halve(leave_1, far, x_far)
    x_far = x_swapped(leave, True)
    near, leave = halve(leave, near, x_near)
    x_near = x_swapped(leave, False)
    stay_0, leave_0 = halve(leave, stay_0, y_0)
    y_0 = y_swapped(leave_0, True)
    stay_1, leave_1 = halve(leave_0, stay_1, y_1)
    y_1 = y_swapped(leave_1, False)
    stay_0, leave_0 = halve(leave_1, stay_0[0], y_0[0])
    z_0 = z_swapped(leave_0, 1)
    far = add(leave_0, far, x_far)
    opposite = lax.ppermute(far, "tp", Z_HI_SWAP)
    stay_1, leave_1 = halve(far, stay_1[0], y_1[0])
    z_1 = z_swapped(leave_1, 1)
    stay_0, leave_0 = halve(leave_1, stay_0, z_0)
    z_0 = z_swapped(leave_0, 2)
    stay_1, leave_1 = halve(leave_0, stay_1, z_1)
    z_1 = z_swapped(leave_1, 2)
    parts = [stay_0[0] + z_0[0].astype(F32), stay_1[0] + z_1[0].astype(F32)]
    grad_proj = jnp.concatenate(parts, axis=0).transpose(1, 0, 2)
    total = near[0] + x_near[0].astype(F32) + opposite[0].astype(F32)
    return total.astype(BF16), grad_proj


def solution(mesh):
    return jax.shard_map(
        per_device,
        mesh=mesh,
        in_specs=(P("ctx", "tp"), P("ctx", "tp"), P(), P(None, None, "tp")),
        out_specs=(P("ctx", "tp"), P("ctx", None, "tp")),
        check_vma=False,
    )
```

```python
import functools

import jax
import jax.numpy as jnp
from jax import lax
from jax.experimental import pallas as pl
from jax.experimental.pallas import tpu as pltpu
from jax.sharding import PartitionSpec as P

BF16, F32 = jnp.bfloat16, jnp.float32
ROWS = 64
LANE = 128
NX, NZ_HI, NY, NZ_LO, NCORE = 4, 2, 4, 4, 2
CHIPS = NY * NZ_LO
VMEM_LIMIT = 20 * 1024 * 1024
LARGE_COST = pl.CostEstimate(flops=4_000_000_000, bytes_accessed=8_000_000, transcendentals=0)
SMALL_COST = pl.CostEstimate(flops=1000, bytes_accessed=1000, transcendentals=0)


def ctx_of(y, z, core):
    return (y * NZ_LO + z) * NCORE + core


CTX = [(y, z, core) for y in range(NY) for z in range(NZ_LO) for core in range(NCORE)]
TP = [(x, z) for x in range(NX) for z in range(NZ_HI)]
CORE_SWAP = [(ctx_of(y, z, c), ctx_of(y, z, 1 - c)) for y, z, c in CTX]
Z_HI_SWAP = [(x * NZ_HI + z, x * NZ_HI + 1 - z) for x, z in TP]


def ring_partner(at, crossed):
    return NX - 1 - at if crossed else at ^ 1


def ring_slots(at, crossed):
    near, far = ring_partner(at, crossed), ring_partner(at, not crossed)
    return at, far, near, ring_partner(near, not crossed)


def y_swap(crossed):
    return [(ctx_of(y, z, c), ctx_of(ring_partner(y, crossed), z, c)) for y, z, c in CTX]


def x_swap(crossed):
    return [(x * NZ_HI + z, ring_partner(x, crossed) * NZ_HI + z) for x, z in TP]


def z_swap(bit):
    return [(ctx_of(y, z, c), ctx_of(y, z ^ bit, c)) for y, z, c in CTX]


def along_x(steps):
    return [(x * NZ_HI + z, (x + steps) % NX * NZ_HI + z) for x, z in TP]


def from_later_chip(steps):
    return [
        (NCORE * (chip + steps) + core, NCORE * chip + core)
        for chip in range(CHIPS - steps)
        for core in range(NCORE)
    ]


def shifted_rows(line, rows):
    block = jnp.broadcast_to(line, (rows, line.shape[1]))
    return pltpu.roll(block, 0, 1, stride=1, stride_axis=0).astype(BF16)


def table_kernel(_, filters_ref, near_ref):
    filt_count, rows, near = near_ref.shape
    edge = jnp.zeros((1, LANE), F32)
    for k in range(filt_count):
        line = filters_ref[k : k + 1, :near].astype(F32)
        near_ref[k] = shifted_rows(jnp.concatenate([line, edge], axis=1), rows)[:, :near]


def near_table(after, filters):
    filt_count, taps = filters.shape
    vmem = pl.BlockSpec(memory_space=pltpu.VMEM)
    return pl.pallas_call(
        table_kernel,
        out_shape=jax.ShapeDtypeStruct((filt_count, ROWS, taps // 2), BF16),
        in_specs=[pl.BlockSpec(memory_space=pl.ANY), vmem],
        out_specs=vmem,
        compiler_params=pltpu.CompilerParams(vmem_limit_bytes=VMEM_LIMIT),
        cost_estimate=SMALL_COST,
        name="near_table",
    )(after, filters)


def prep_kernel(pos_ref, _, own_ref, r1_ref, r2_ref, r3_ref, r4_ref, stack_ref, held_ref, arrived):
    copy = pltpu.make_async_copy(own_ref, held_ref, arrived)
    copy.start()
    parts = r1_ref, r2_ref, r3_ref, r4_ref
    core = lax.rem(pos_ref[1], NCORE)
    for s in range(1, stack_ref.shape[0]):
        stack_ref[s] = jnp.where(core == 0, parts[s][...], parts[s - 1][...])
    copy.wait()
    stack_ref[0] = jnp.where(core == 0, r1_ref[...], held_ref[...])


def for_sibling(pos, after, *parts):
    block = parts[0].shape
    vmem = pl.BlockSpec(memory_space=pltpu.VMEM)
    return pl.pallas_call(
        prep_kernel,
        out_shape=jax.ShapeDtypeStruct((4,) + block, BF16),
        in_specs=[pl.BlockSpec(memory_space=pltpu.SMEM)]
        + [pl.BlockSpec(memory_space=pl.ANY)] * 2
        + [vmem] * 4,
        out_specs=vmem,
        scratch_shapes=[pltpu.VMEM(block, BF16), pltpu.SemaphoreType.DMA],
        compiler_params=pltpu.CompilerParams(vmem_limit_bytes=VMEM_LIMIT),
        cost_estimate=SMALL_COST,
        name="for_sibling",
    )(pos, after, *parts)


def pair_of_blocks(grad_ref, start, rows, width):
    first = grad_ref[pl.ds(start, width), :]
    second = grad_ref[pl.ds(start + rows, width), :]
    return jnp.concatenate([first, second], axis=1)


def coords(pos_ref):
    x, z_hi = pos_ref[0] // NZ_HI, lax.rem(pos_ref[0], NZ_HI)
    chip, core = pos_ref[1] // NCORE, lax.rem(pos_ref[1], NCORE)
    return x, z_hi, chip // NZ_LO, lax.rem(chip, NZ_LO), core


def lay_out(grad_ref, refs):
    tok = refs[0].shape[0]
    for s, part in enumerate(refs):
        grad_ref[s * tok : (s + 1) * tok, :] = part[...]


def near_kernel(table_ref, own_ref, r1_ref, r2_ref, sib_ref, *refs):
    acc_refs, grad_ref = refs[:-1], refs[-1]
    filt_count, rows, width = table_ref.shape
    tok = own_ref.shape[0]
    lay_out(grad_ref, (own_ref, sib_ref.at[0], r1_ref, sib_ref.at[1], r2_ref))
    table = table_ref[...].reshape(filt_count * rows, width)

    @pl.loop(0, tok // (2 * rows), unroll=True)
    def _(pair):
        start = pl.multiple_of(pair * (2 * rows), 2 * rows)
        both = pair_of_blocks(grad_ref, start, rows, width)
        result = jnp.dot(table, both, preferred_element_type=F32)
        part = acc_refs[0].shape[1]
        for group, acc_ref in enumerate(acc_refs):
            acc_ref[pair] = result[group * part : (group + 1) * part]


def near_conv(after, table, halo, sibling, groups):
    filt_count, rows, width = table.shape
    tok = halo[0].shape[0]
    vmem = pl.BlockSpec(memory_space=pltpu.VMEM)
    acc = jax.ShapeDtypeStruct((tok // (2 * rows), filt_count // groups * rows, 2 * LANE), F32)
    return pl.pallas_call(
        near_kernel,
        out_shape=[acc] * groups,
        in_specs=[pl.BlockSpec(memory_space=pl.ANY)] * len(after) + [vmem] * 5,
        out_specs=[vmem] * groups,
        scratch_shapes=[pltpu.VMEM((5 * tok, LANE), BF16)],
        compiler_params=pltpu.CompilerParams(vmem_limit_bytes=VMEM_LIMIT),
        cost_estimate=LARGE_COST,
        name="near_conv",
    )(*after, table, *halo, sibling)


def far_kernel(
    first, _, filters_ref, acc_ref, r2_ref, r3_ref, r4_ref, sib_ref,
    corr_ref, grad_ref, table_ref,
):
    filt_count, rows, width = table_ref.shape
    tok = r2_ref.shape[0]
    edge = jnp.zeros((1, LANE), F32)
    start = filters_ref.shape[1] + LANE - width - LANE
    for k in range(filt_count):
        line = filters_ref[first + k : first + k + 1, start:].astype(F32)
        table_ref[k] = shifted_rows(jnp.concatenate([line, edge], axis=1), rows)[:, LANE:]
    lay_out(grad_ref, (r2_ref, sib_ref.at[2], r3_ref, sib_ref.at[3], r4_ref))
    grad_ref[5 * tok :, :] = jnp.zeros((grad_ref.shape[0] - 5 * tok, LANE), BF16)

    @pl.loop(0, tok // (2 * rows), unroll=True)
    def _(pair):
        start = pl.multiple_of(pair * (2 * rows), 2 * rows)
        both = pair_of_blocks(grad_ref, start, rows, width)
        table = table_ref[...].reshape(filt_count * rows, width)
        result = jnp.dot(table, both, preferred_element_type=F32)
        result = (result + acc_ref[pair]).astype(BF16)
        for k in range(filt_count):
            for half in range(2):
                corr_ref[pl.ds(start + half * rows, rows), k * LANE : (k + 1) * LANE] = result[
                    k * rows : (k + 1) * rows, half * LANE : (half + 1) * LANE
                ]


def far_conv(first, count, after, filters, acc, halo, sibling):
    tok = halo[0].shape[0]
    width = filters.shape[1] // 2 + LANE
    vmem = pl.BlockSpec(memory_space=pltpu.VMEM)
    return pl.pallas_call(
        functools.partial(far_kernel, first),
        out_shape=jax.ShapeDtypeStruct((tok, count * LANE), BF16),
        in_specs=[pl.BlockSpec(memory_space=pl.ANY)] + [vmem] * 6,
        out_specs=vmem,
        scratch_shapes=[
            pltpu.VMEM((5 * tok + ROWS, LANE), BF16),
            pltpu.VMEM((count, ROWS, width), BF16),
        ],
        compiler_params=pltpu.CompilerParams(vmem_limit_bytes=VMEM_LIMIT),
        cost_estimate=SMALL_COST,
        name="far_conv",
    )(after, filters, acc, *halo, sibling)


def product_kernel(
    crossed, pos_ref, _, corr_ref, x0_ref, x1_ref, x2_ref, x3_ref, keep_ref, send_ref, full_ref
):
    x, z_hi, y, z_lo, core = coords(pos_ref)
    for s, part in enumerate((x0_ref, x1_ref, x2_ref, x3_ref)):
        for h in range(NZ_HI):
            at = lax.rem(x + NX - s, NX) * NZ_HI + lax.rem(z_hi + h, NZ_HI)
            full_ref[:, pl.ds(pl.multiple_of(at * LANE, LANE), LANE)] = part[h]

    deep = NZ_LO * NCORE * 32
    for s, at in enumerate(ring_slots(y, crossed)):
        part = full_ref[:, pl.ds(pl.multiple_of(at * deep, deep), deep)]
        result = lax.dot_general(
            part, corr_ref[...], (((0,), (0,)), ((), ())), preferred_element_type=F32
        ).astype(BF16)
        for z in range(NZ_LO):
            shift = z ^ z_lo
            slot = lax.rem(shift, 2) * 2 + shift // 2
            for k in range(keep_ref.shape[2]):
                columns = slice(k * LANE, (k + 1) * LANE)
                even = result[z * 64 : z * 64 + 32, columns]
                odd = result[z * 64 + 32 : z * 64 + 64, columns]
                keep_ref[s, slot, k] = jnp.where(core == 0, even, odd)
                send_ref[s, slot, k] = jnp.where(core == 0, odd, even)


def product(crossed, pos, after, corr, gathered):
    tok, width = corr.shape
    part = jax.ShapeDtypeStruct((NY, NZ_LO, width // LANE, 32, LANE), BF16)
    vmem = pl.BlockSpec(memory_space=pltpu.VMEM)
    return pl.pallas_call(
        functools.partial(product_kernel, crossed),
        out_shape=(part, part),
        in_specs=[pl.BlockSpec(memory_space=pltpu.SMEM), pl.BlockSpec(memory_space=pl.ANY)]
        + [vmem] * 5,
        out_specs=(vmem,) * 2,
        scratch_shapes=[pltpu.VMEM((tok, 1024), BF16)],
        compiler_params=pltpu.CompilerParams(vmem_limit_bytes=VMEM_LIMIT),
        cost_estimate=SMALL_COST,
        name="product",
    )(pos, after, corr, *gathered)


def halve_kernel(_, mine_ref, other_ref, stay_ref, leave_ref):
    half = leave_ref.shape[0]
    stay_ref[...] = mine_ref[:half].astype(F32) + other_ref[:half].astype(F32)
    leave_ref[...] = (mine_ref[half:].astype(F32) + other_ref[half:].astype(F32)).astype(BF16)


def halve(after, mine, other, cost=SMALL_COST):
    half = (mine.shape[0] // 2,) + mine.shape[1:]
    vmem = pl.BlockSpec(memory_space=pltpu.VMEM)
    return pl.pallas_call(
        halve_kernel,
        out_shape=(jax.ShapeDtypeStruct(half, F32), jax.ShapeDtypeStruct(half, BF16)),
        in_specs=[pl.BlockSpec(memory_space=pl.ANY), vmem, vmem],
        out_specs=(vmem, vmem),
        compiler_params=pltpu.CompilerParams(vmem_limit_bytes=VMEM_LIMIT),
        cost_estimate=cost,
        name="halve",
    )(after, mine, other)


def add_kernel(_, mine_ref, other_ref, sum_ref):
    sum_ref[...] = (mine_ref[...] + other_ref[...].astype(F32)).astype(BF16)


def add(after, mine, other):
    vmem = pl.BlockSpec(memory_space=pltpu.VMEM)
    return pl.pallas_call(
        add_kernel,
        out_shape=jax.ShapeDtypeStruct(mine.shape, BF16),
        in_specs=[pl.BlockSpec(memory_space=pl.ANY), vmem, vmem],
        out_specs=vmem,
        compiler_params=pltpu.CompilerParams(vmem_limit_bytes=VMEM_LIMIT),
        cost_estimate=LARGE_COST,
        name="add",
    )(after, mine, other)


def join_kernel(_, *refs):
    at, sum_ref = 0, refs[-1]
    for mine_ref, other_ref in zip(refs[0:-1:2], refs[1:-1:2]):
        count = mine_ref.shape[1]
        sum_ref[at : at + count] = mine_ref[0] + other_ref[0].astype(F32)
        at += count


def join(after, *pairs):
    counts = [mine.shape[1] for mine, _ in pairs]
    rest = pairs[0][0].shape[2:]
    vmem = pl.BlockSpec(memory_space=pltpu.VMEM)
    return pl.pallas_call(
        join_kernel,
        out_shape=jax.ShapeDtypeStruct((sum(counts),) + rest, F32),
        in_specs=[pl.BlockSpec(memory_space=pl.ANY)] + [vmem] * (2 * len(pairs)),
        out_specs=vmem,
        compiler_params=pltpu.CompilerParams(vmem_limit_bytes=VMEM_LIMIT),
        cost_estimate=SMALL_COST,
        name="join",
    )(after, *[part for pair in pairs for part in pair])


def share_kernel(pos_ref, _, *refs):
    corr_refs, proj_ref = refs[:-6], refs[-6]
    near_keep, near_send, far_keep, far_send, all_ref = refs[-5:]
    filt_count = proj_ref.shape[0]
    x, z_hi = coords(pos_ref)[:2]
    at = 0
    for part in corr_refs:
        all_ref[:, at : at + part.shape[1]] = part[...]
        at += part.shape[1]
    wide = NZ_HI * LANE
    near_slots = (near_keep, 0), (near_send, 0), (near_keep, 1), (near_send, 1)
    far_slots = (far_keep, 0), (far_keep, 1), (far_send, 0), (far_send, 1)
    for at, near, far in zip(ring_slots(x, False), near_slots, far_slots):
        base = pl.multiple_of(at * wide, wide)
        weights = jnp.concatenate(
            [proj_ref[k, pl.ds(base, wide), :] for k in range(filt_count)], axis=1
        )
        result = lax.dot_general(
            all_ref[...], weights, (((1,), (1,)), ((), ())), preferred_element_type=F32
        )
        low, high = result[:, :LANE], result[:, LANE:]
        near[0][near[1]] = jnp.where(z_hi == 0, low, high).astype(near[0].dtype)
        far[0][far[1]] = jnp.where(z_hi == 0, high, low).astype(far[0].dtype)


def input_shares(pos, after, corrs, projection):
    tok = corrs[0].shape[0]
    filt_count = projection.shape[0]
    vmem = pl.BlockSpec(memory_space=pltpu.VMEM)
    keep = jax.ShapeDtypeStruct((2, tok, LANE), F32)
    send = jax.ShapeDtypeStruct((2, tok, LANE), BF16)
    return pl.pallas_call(
        share_kernel,
        out_shape=(keep, send, keep, send),
        in_specs=[pl.BlockSpec(memory_space=pltpu.SMEM), pl.BlockSpec(memory_space=pl.ANY)]
        + [vmem] * (len(corrs) + 1),
        out_specs=(vmem,) * 4,
        scratch_shapes=[pltpu.VMEM((tok, filt_count * LANE), BF16)],
        compiler_params=pltpu.CompilerParams(vmem_limit_bytes=VMEM_LIMIT),
        cost_estimate=SMALL_COST,
        name="input_shares",
    )(pos, after, *corrs, projection)


GROUPS = 2


def per_device(inputs, grad_out, filters, projection):
    tp, ctx = lax.axis_index("tp"), lax.axis_index("ctx")
    pos = jnp.stack([tp, ctx]).astype(jnp.int32)

    def later(value, steps):
        return lax.ppermute(value, "ctx", from_later_chip(steps))

    def sibling(value):
        return lax.ppermute(value, "ctx", CORE_SWAP)

    def y_swapped(value, crossed):
        return lax.ppermute(value, "ctx", y_swap(crossed))

    def z_swapped(value, bit):
        return lax.ppermute(value, "ctx", z_swap(bit))

    def x_swapped(value, crossed):
        return lax.ppermute(value, "tp", x_swap(crossed))

    count = filters.shape[0] // GROUPS
    pair = jnp.stack([inputs, lax.ppermute(inputs, "tp", Z_HI_SWAP)])
    gathered = [pair] + [lax.ppermute(pair, "tp", along_x(s)) for s in range(1, NX)]
    table = near_table(pair, filters)
    halo = [grad_out] + [later(grad_out, steps) for steps in range(1, 5)]
    beside = sibling(for_sibling(pos, table, *halo))
    accs = near_conv(gathered[1:1], table, halo[:3], beside, GROUPS)

    def conv(group, after):
        return far_conv(group * count, count, after, filters, accs[group], halo[2:], beside)

    corr_0 = conv(0, table)
    corr_1 = conv(1, corr_0)
    near, near_send, far, far_send = input_shares(
        pos, corr_1, [corr_0, corr_1], projection.transpose(1, 0, 2)
    )
    x_far, x_near = x_swapped(far_send, False), x_swapped(near_send, True)
    keep_0, send_0 = product(False, pos, near_send, corr_0, gathered)
    keep_1, send_1 = product(True, pos, send_0, corr_1, gathered)
    stay_0, leave_0 = halve(send_1, keep_0, sibling(send_0))
    y_0 = y_swapped(leave_0, False)
    stay_1, leave_1 = halve(leave_0, keep_1, sibling(send_1))
    y_1 = y_swapped(leave_1, True)
    far, leave = halve(leave_1, far, x_far, LARGE_COST)
    x_far = x_swapped(leave, True)
    near, leave = halve(leave, near, x_near)
    x_near = x_swapped(leave, False)
    stay_0, leave_0 = halve(leave, stay_0, y_0)
    y_0 = y_swapped(leave_0, True)
    stay_1, leave_1 = halve(leave_0, stay_1, y_1)
    y_1 = y_swapped(leave_1, False)
    far = add(leave_1, far, x_far)
    opposite = lax.ppermute(far, "tp", Z_HI_SWAP)
    stay_0, leave_0 = halve(far, stay_0[0], y_0[0])
    z_0 = z_swapped(leave_0, 1)
    stay_1, leave_1 = halve(leave_0, stay_1[0], y_1[0])
    z_1 = z_swapped(leave_1, 1)
    stay_0, leave_0 = halve(leave_1, stay_0, z_0)
    z_0 = z_swapped(leave_0, 2)
    stay_1, leave_1 = halve(leave_0, stay_1, z_1)
    z_1 = z_swapped(leave_1, 2)
    grad_proj = join(near, (stay_0, z_0), (stay_1, z_1)).transpose(1, 0, 2)
    total = near[0] + x_near[0].astype(F32) + opposite[0].astype(F32)
    return total.astype(BF16), grad_proj


def solution(mesh):
    return jax.shard_map(
        per_device,
        mesh=mesh,
        in_specs=(P("ctx", "tp"), P("ctx", "tp"), P(), P(None, None, "tp")),
        out_specs=(P("ctx", "tp"), P("ctx", None, "tp")),
        check_vma=False,
    )
```

```python
import functools

import jax
import jax.numpy as jnp
from jax import lax
from jax.experimental import pallas as pl
from jax.experimental.pallas import tpu as pltpu
from jax.sharding import PartitionSpec as P

BF16, F32 = jnp.bfloat16, jnp.float32
ROWS = 64
LANE = 128
NX, NZ_HI, NY, NZ_LO, NCORE = 4, 2, 4, 4, 2
CHIPS = NY * NZ_LO
VMEM_LIMIT = 20 * 1024 * 1024
LARGE_COST = pl.CostEstimate(flops=4_000_000_000, bytes_accessed=8_000_000, transcendentals=0)
SMALL_COST = pl.CostEstimate(flops=1000, bytes_accessed=1000, transcendentals=0)


def ctx_of(y, z, core):
    return (y * NZ_LO + z) * NCORE + core


CTX = [(y, z, core) for y in range(NY) for z in range(NZ_LO) for core in range(NCORE)]
TP = [(x, z) for x in range(NX) for z in range(NZ_HI)]
CORE_SWAP = [(ctx_of(y, z, c), ctx_of(y, z, 1 - c)) for y, z, c in CTX]
Z_HI_SWAP = [(x * NZ_HI + z, x * NZ_HI + 1 - z) for x, z in TP]


def ring_partner(at, crossed):
    return NX - 1 - at if crossed else at ^ 1


def ring_slots(at, crossed):
    near, far = ring_partner(at, crossed), ring_partner(at, not crossed)
    return at, far, near, ring_partner(near, not crossed)


def y_swap(crossed):
    return [(ctx_of(y, z, c), ctx_of(ring_partner(y, crossed), z, c)) for y, z, c in CTX]


def x_swap(crossed):
    return [(x * NZ_HI + z, ring_partner(x, crossed) * NZ_HI + z) for x, z in TP]


def z_swap(bit):
    return [(ctx_of(y, z, c), ctx_of(y, z ^ bit, c)) for y, z, c in CTX]


def along_x(steps):
    return [(x * NZ_HI + z, (x + steps) % NX * NZ_HI + z) for x, z in TP]


def from_later_chip(steps):
    return [
        (NCORE * (chip + steps) + core, NCORE * chip + core)
        for chip in range(CHIPS - steps)
        for core in range(NCORE)
    ]


def shifted_rows(line, rows):
    block = jnp.broadcast_to(line, (rows, line.shape[1]))
    return pltpu.roll(block, 0, 1, stride=1, stride_axis=0).astype(BF16)


def table_kernel(_, filters_ref, near_ref):
    filt_count, rows, near = near_ref.shape
    edge = jnp.zeros((1, LANE), F32)
    for k in range(filt_count):
        line = filters_ref[k : k + 1, :near].astype(F32)
        near_ref[k] = shifted_rows(jnp.concatenate([line, edge], axis=1), rows)[:, :near]


def near_table(after, filters):
    filt_count, taps = filters.shape
    vmem = pl.BlockSpec(memory_space=pltpu.VMEM)
    return pl.pallas_call(
        table_kernel,
        out_shape=jax.ShapeDtypeStruct((filt_count, ROWS, taps // 2), BF16),
        in_specs=[pl.BlockSpec(memory_space=pl.ANY), vmem],
        out_specs=vmem,
        compiler_params=pltpu.CompilerParams(vmem_limit_bytes=VMEM_LIMIT),
        cost_estimate=SMALL_COST,
        name="near_table",
    )(after, filters)


def pair_of_blocks(grad_ref, start, rows, width):
    first = grad_ref[pl.ds(start, width), :]
    second = grad_ref[pl.ds(start + rows, width), :]
    return jnp.concatenate([first, second], axis=1)


def coords(pos_ref):
    x, z_hi = pos_ref[0] // NZ_HI, lax.rem(pos_ref[0], NZ_HI)
    chip, core = pos_ref[1] // NCORE, lax.rem(pos_ref[1], NCORE)
    return x, z_hi, chip // NZ_LO, lax.rem(chip, NZ_LO), core


def lay_out(core, grad_ref, even_refs, odd_refs):
    tok = even_refs[0].shape[0]
    for s, part in enumerate(even_refs):
        grad_ref[2 * s * tok : (2 * s + 1) * tok, :] = part[...]
    for s in range(len(even_refs) - 1):
        grad_ref[(2 * s + 1) * tok : (2 * s + 2) * tok, :] = jnp.where(
            core == 0, odd_refs[s][...], odd_refs[s + 1][...]
        )


def near_kernel(pos_ref, table_ref, own_ref, r1_ref, r2_ref, s0_ref, s1_ref, s2_ref, *refs):
    acc_refs, grad_ref = refs[:-1], refs[-1]
    filt_count, rows, width = table_ref.shape
    tok = own_ref.shape[0]
    core = lax.rem(pos_ref[1], NCORE)
    lay_out(core, grad_ref, (own_ref, r1_ref, r2_ref), (s0_ref, s1_ref, s2_ref))
    table = table_ref[...].reshape(filt_count * rows, width)

    @pl.loop(0, tok // (2 * rows), unroll=True)
    def _(pair):
        start = pl.multiple_of(pair * (2 * rows), 2 * rows)
        both = pair_of_blocks(grad_ref, start, rows, width)
        result = jnp.dot(table, both, preferred_element_type=F32)
        part = acc_refs[0].shape[1]
        for group, acc_ref in enumerate(acc_refs):
            acc_ref[pair] = result[group * part : (group + 1) * part]


def near_conv(pos, table, halo, sibling, groups):
    filt_count, rows, width = table.shape
    tok = halo[0].shape[0]
    vmem = pl.BlockSpec(memory_space=pltpu.VMEM)
    acc = jax.ShapeDtypeStruct((tok // (2 * rows), filt_count // groups * rows, 2 * LANE), F32)
    return pl.pallas_call(
        near_kernel,
        out_shape=[acc] * groups,
        in_specs=[pl.BlockSpec(memory_space=pltpu.SMEM)] + [vmem] * 7,
        out_specs=[vmem] * groups,
        scratch_shapes=[pltpu.VMEM((5 * tok, LANE), BF16)],
        compiler_params=pltpu.CompilerParams(vmem_limit_bytes=VMEM_LIMIT),
        cost_estimate=LARGE_COST,
        name="near_conv",
    )(pos, table, *halo, *sibling)


def far_kernel(
    first, pos_ref, _, filters_ref, acc_ref, r2_ref, r3_ref, r4_ref, s2_ref, s3_ref, s4_ref,
    corr_ref, grad_ref, table_ref,
):
    filt_count, rows, width = table_ref.shape
    tok = r2_ref.shape[0]
    edge = jnp.zeros((1, LANE), F32)
    start = filters_ref.shape[1] + LANE - width - LANE
    for k in range(filt_count):
        line = filters_ref[first + k : first + k + 1, start:].astype(F32)
        table_ref[k] = shifted_rows(jnp.concatenate([line, edge], axis=1), rows)[:, LANE:]
    core = lax.rem(pos_ref[1], NCORE)
    lay_out(core, grad_ref, (r2_ref, r3_ref, r4_ref), (s2_ref, s3_ref, s4_ref))
    grad_ref[5 * tok :, :] = jnp.zeros((grad_ref.shape[0] - 5 * tok, LANE), BF16)

    @pl.loop(0, tok // (2 * rows), unroll=True)
    def _(pair):
        start = pl.multiple_of(pair * (2 * rows), 2 * rows)
        both = pair_of_blocks(grad_ref, start, rows, width)
        table = table_ref[...].reshape(filt_count * rows, width)
        result = jnp.dot(table, both, preferred_element_type=F32)
        result = (result + acc_ref[pair]).astype(BF16)
        for k in range(filt_count):
            for half in range(2):
                corr_ref[pl.ds(start + half * rows, rows), k * LANE : (k + 1) * LANE] = result[
                    k * rows : (k + 1) * rows, half * LANE : (half + 1) * LANE
                ]


def far_conv(first, count, pos, after, filters, acc, halo, sibling):
    tok = halo[0].shape[0]
    width = filters.shape[1] // 2 + LANE
    vmem = pl.BlockSpec(memory_space=pltpu.VMEM)
    return pl.pallas_call(
        functools.partial(far_kernel, first),
        out_shape=jax.ShapeDtypeStruct((tok, count * LANE), BF16),
        in_specs=[pl.BlockSpec(memory_space=pltpu.SMEM), pl.BlockSpec(memory_space=pl.ANY)]
        + [vmem] * 8,
        out_specs=vmem,
        scratch_shapes=[
            pltpu.VMEM((5 * tok + ROWS, LANE), BF16),
            pltpu.VMEM((count, ROWS, width), BF16),
        ],
        compiler_params=pltpu.CompilerParams(vmem_limit_bytes=VMEM_LIMIT),
        cost_estimate=SMALL_COST,
        name="far_conv",
    )(pos, after, filters, acc, *halo, *sibling)


def product_kernel(
    crossed, pos_ref, _, corr_ref, x0_ref, x1_ref, x2_ref, x3_ref, keep_ref, send_ref, full_ref
):
    x, z_hi, y, z_lo, core = coords(pos_ref)
    for s, part in enumerate((x0_ref, x1_ref, x2_ref, x3_ref)):
        for h in range(NZ_HI):
            at = lax.rem(x + NX - s, NX) * NZ_HI + lax.rem(z_hi + h, NZ_HI)
            full_ref[:, pl.ds(pl.multiple_of(at * LANE, LANE), LANE)] = part[h]

    deep = NZ_LO * NCORE * 32
    for s, at in enumerate(ring_slots(y, crossed)):
        part = full_ref[:, pl.ds(pl.multiple_of(at * deep, deep), deep)]
        result = lax.dot_general(
            part, corr_ref[...], (((0,), (0,)), ((), ())), preferred_element_type=F32
        ).astype(BF16)
        for z in range(NZ_LO):
            shift = z ^ z_lo
            slot = lax.rem(shift, 2) * 2 + shift // 2
            for k in range(keep_ref.shape[2]):
                columns = slice(k * LANE, (k + 1) * LANE)
                even = result[z * 64 : z * 64 + 32, columns]
                odd = result[z * 64 + 32 : z * 64 + 64, columns]
                keep_ref[s, slot, k] = jnp.where(core == 0, even, odd)
                send_ref[s, slot, k] = jnp.where(core == 0, odd, even)


def product(crossed, pos, after, corr, gathered):
    tok, width = corr.shape
    part = jax.ShapeDtypeStruct((NY, NZ_LO, width // LANE, 32, LANE), BF16)
    vmem = pl.BlockSpec(memory_space=pltpu.VMEM)
    return pl.pallas_call(
        functools.partial(product_kernel, crossed),
        out_shape=(part, part),
        in_specs=[pl.BlockSpec(memory_space=pltpu.SMEM), pl.BlockSpec(memory_space=pl.ANY)]
        + [vmem] * 5,
        out_specs=(vmem,) * 2,
        scratch_shapes=[pltpu.VMEM((tok, 1024), BF16)],
        compiler_params=pltpu.CompilerParams(vmem_limit_bytes=VMEM_LIMIT),
        cost_estimate=SMALL_COST,
        name="product",
    )(pos, after, corr, *gathered)


def halve_kernel(_, mine_ref, other_ref, stay_ref, leave_ref):
    half = leave_ref.shape[0]
    stay_ref[...] = mine_ref[:half].astype(F32) + other_ref[:half].astype(F32)
    leave_ref[...] = (mine_ref[half:].astype(F32) + other_ref[half:].astype(F32)).astype(BF16)


def halve(after, mine, other, cost=SMALL_COST):
    half = (mine.shape[0] // 2,) + mine.shape[1:]
    vmem = pl.BlockSpec(memory_space=pltpu.VMEM)
    return pl.pallas_call(
        halve_kernel,
        out_shape=(jax.ShapeDtypeStruct(half, F32), jax.ShapeDtypeStruct(half, BF16)),
        in_specs=[pl.BlockSpec(memory_space=pl.ANY), vmem, vmem],
        out_specs=(vmem, vmem),
        compiler_params=pltpu.CompilerParams(vmem_limit_bytes=VMEM_LIMIT),
        cost_estimate=cost,
        name="halve",
    )(after, mine, other)


def add_kernel(_, mine_ref, other_ref, sum_ref):
    sum_ref[...] = (mine_ref[...] + other_ref[...].astype(F32)).astype(BF16)


def add(after, mine, other):
    vmem = pl.BlockSpec(memory_space=pltpu.VMEM)
    return pl.pallas_call(
        add_kernel,
        out_shape=jax.ShapeDtypeStruct(mine.shape, BF16),
        in_specs=[pl.BlockSpec(memory_space=pl.ANY), vmem, vmem],
        out_specs=vmem,
        compiler_params=pltpu.CompilerParams(vmem_limit_bytes=VMEM_LIMIT),
        cost_estimate=LARGE_COST,
        name="add",
    )(after, mine, other)


def join_kernel(_, *refs):
    at, sum_ref = 0, refs[-1]
    for mine_ref, other_ref in zip(refs[0:-1:2], refs[1:-1:2]):
        count = mine_ref.shape[1]
        sum_ref[at : at + count] = mine_ref[0] + other_ref[0].astype(F32)
        at += count


def join(after, *pairs):
    counts = [mine.shape[1] for mine, _ in pairs]
    rest = pairs[0][0].shape[2:]
    vmem = pl.BlockSpec(memory_space=pltpu.VMEM)
    return pl.pallas_call(
        join_kernel,
        out_shape=jax.ShapeDtypeStruct((sum(counts),) + rest, F32),
        in_specs=[pl.BlockSpec(memory_space=pl.ANY)] + [vmem] * (2 * len(pairs)),
        out_specs=vmem,
        compiler_params=pltpu.CompilerParams(vmem_limit_bytes=VMEM_LIMIT),
        cost_estimate=SMALL_COST,
        name="join",
    )(after, *[part for pair in pairs for part in pair])


def share_kernel(pos_ref, _, *refs):
    corr_refs, proj_ref = refs[:-6], refs[-6]
    near_keep, near_send, far_keep, far_send, all_ref = refs[-5:]
    filt_count = proj_ref.shape[0]
    x, z_hi = coords(pos_ref)[:2]
    at = 0
    for part in corr_refs:
        all_ref[:, at : at + part.shape[1]] = part[...]
        at += part.shape[1]
    wide = NZ_HI * LANE
    near_slots = (near_keep, 0), (near_send, 0), (near_keep, 1), (near_send, 1)
    far_slots = (far_keep, 0), (far_keep, 1), (far_send, 0), (far_send, 1)
    for at, near, far in zip(ring_slots(x, False), near_slots, far_slots):
        base = pl.multiple_of(at * wide, wide)
        weights = jnp.concatenate(
            [proj_ref[k, pl.ds(base, wide), :] for k in range(filt_count)], axis=1
        )
        result = lax.dot_general(
            all_ref[...], weights, (((1,), (1,)), ((), ())), preferred_element_type=F32
        )
        low, high = result[:, :LANE], result[:, LANE:]
        near[0][near[1]] = jnp.where(z_hi == 0, low, high).astype(near[0].dtype)
        far[0][far[1]] = jnp.where(z_hi == 0, high, low).astype(far[0].dtype)


def input_shares(pos, after, corrs, projection):
    tok = corrs[0].shape[0]
    filt_count = projection.shape[0]
    vmem = pl.BlockSpec(memory_space=pltpu.VMEM)
    keep = jax.ShapeDtypeStruct((2, tok, LANE), F32)
    send = jax.ShapeDtypeStruct((2, tok, LANE), BF16)
    return pl.pallas_call(
        share_kernel,
        out_shape=(keep, send, keep, send),
        in_specs=[pl.BlockSpec(memory_space=pltpu.SMEM), pl.BlockSpec(memory_space=pl.ANY)]
        + [vmem] * (len(corrs) + 1),
        out_specs=(vmem,) * 4,
        scratch_shapes=[pltpu.VMEM((tok, filt_count * LANE), BF16)],
        compiler_params=pltpu.CompilerParams(vmem_limit_bytes=VMEM_LIMIT),
        cost_estimate=SMALL_COST,
        name="input_shares",
    )(pos, after, *corrs, projection)


GROUPS = 2


def per_device(inputs, grad_out, filters, projection):
    tp, ctx = lax.axis_index("tp"), lax.axis_index("ctx")
    pos = jnp.stack([tp, ctx]).astype(jnp.int32)

    def later(value, steps):
        return lax.ppermute(value, "ctx", from_later_chip(steps))

    def sibling(value):
        return lax.ppermute(value, "ctx", CORE_SWAP)

    def y_swapped(value, crossed):
        return lax.ppermute(value, "ctx", y_swap(crossed))

    def z_swapped(value, bit):
        return lax.ppermute(value, "ctx", z_swap(bit))

    def x_swapped(value, crossed):
        return lax.ppermute(value, "tp", x_swap(crossed))

    count = filters.shape[0] // GROUPS
    pair = jnp.stack([inputs, lax.ppermute(inputs, "tp", Z_HI_SWAP)])
    gathered = [pair] + [lax.ppermute(pair, "tp", along_x(s)) for s in range(1, NX)]
    table = near_table(pair, filters)
    halo = [grad_out] + [later(grad_out, steps) for steps in range(1, 5)]
    beside = [sibling(part) for part in halo]
    accs = near_conv(pos, table, halo[:3], beside[:3], GROUPS)

    def conv(group, after):
        return far_conv(
            group * count, count, pos, after, filters, accs[group], halo[2:], beside[2:]
        )

    corr_0 = conv(0, table)
    corr_1 = conv(1, corr_0)
    near, near_send, far, far_send = input_shares(
        pos, corr_1, [corr_0, corr_1], projection.transpose(1, 0, 2)
    )
    x_far, x_near = x_swapped(far_send, False), x_swapped(near_send, True)
    keep_0, send_0 = product(False, pos, near_send, corr_0, gathered)
    keep_1, send_1 = product(True, pos, send_0, corr_1, gathered)
    stay_0, leave_0 = halve(send_1, keep_0, sibling(send_0))
    y_0 = y_swapped(leave_0, False)
    stay_1, leave_1 = halve(leave_0, keep_1, sibling(send_1))
    y_1 = y_swapped(leave_1, True)
    far, leave = halve(leave_1, far, x_far, LARGE_COST)
    x_far = x_swapped(leave, True)
    near, leave = halve(leave, near, x_near)
    x_near = x_swapped(leave, False)
    stay_0, leave_0 = halve(leave, stay_0, y_0)
    y_0 = y_swapped(leave_0, True)
    stay_1, leave_1 = halve(leave_0, stay_1, y_1)
    y_1 = y_swapped(leave_1, False)
    far = add(leave_1, far, x_far)
    opposite = lax.ppermute(far, "tp", Z_HI_SWAP)
    stay_0, leave_0 = halve(far, stay_0[0], y_0[0])
    z_0 = z_swapped(leave_0, 1)
    stay_1, leave_1 = halve(leave_0, stay_1[0], y_1[0])
    z_1 = z_swapped(leave_1, 1)
    stay_0, leave_0 = halve(leave_1, stay_0, z_0)
    z_0 = z_swapped(leave_0, 2)
    stay_1, leave_1 = halve(leave_0, stay_1, z_1)
    z_1 = z_swapped(leave_1, 2)
    grad_proj = join(near, (stay_0, z_0), (stay_1, z_1)).transpose(1, 0, 2)
    total = near[0] + x_near[0].astype(F32) + opposite[0].astype(F32)
    return total.astype(BF16), grad_proj


def solution(mesh):
    return jax.shard_map(
        per_device,
        mesh=mesh,
        in_specs=(P("ctx", "tp"), P("ctx", "tp"), P(), P(None, None, "tp")),
        out_specs=(P("ctx", "tp"), P("ctx", None, "tp")),
        check_vma=False,
    )
```

```python
import functools

import jax
import jax.numpy as jnp
from jax import lax
from jax.experimental import pallas as pl
from jax.experimental.pallas import tpu as pltpu
from jax.sharding import PartitionSpec as P

BF16, F32 = jnp.bfloat16, jnp.float32
ROWS = 64
LANE = 128
NX, NZ_HI, NY, NZ_LO, NCORE = 4, 2, 4, 4, 2
CHIPS = NY * NZ_LO
VMEM_LIMIT = 20 * 1024 * 1024
LARGE_COST = pl.CostEstimate(flops=4_000_000_000, bytes_accessed=8_000_000, transcendentals=0)
SMALL_COST = pl.CostEstimate(flops=1000, bytes_accessed=1000, transcendentals=0)


def ctx_of(y, z, core):
    return (y * NZ_LO + z) * NCORE + core


CTX = [(y, z, core) for y in range(NY) for z in range(NZ_LO) for core in range(NCORE)]
TP = [(x, z) for x in range(NX) for z in range(NZ_HI)]
CORE_SWAP = [(ctx_of(y, z, c), ctx_of(y, z, 1 - c)) for y, z, c in CTX]
Z_HI_SWAP = [(x * NZ_HI + z, x * NZ_HI + 1 - z) for x, z in TP]


def ring_partner(at, crossed):
    return NX - 1 - at if crossed else at ^ 1


def ring_slots(at, crossed):
    near, far = ring_partner(at, crossed), ring_partner(at, not crossed)
    return at, far, near, ring_partner(near, not crossed)


def y_swap(crossed):
    return [(ctx_of(y, z, c), ctx_of(ring_partner(y, crossed), z, c)) for y, z, c in CTX]


def x_swap(crossed):
    return [(x * NZ_HI + z, ring_partner(x, crossed) * NZ_HI + z) for x, z in TP]


def z_swap(bit):
    return [(ctx_of(y, z, c), ctx_of(y, z ^ bit, c)) for y, z, c in CTX]


def along_x(steps):
    return [(x * NZ_HI + z, (x + steps) % NX * NZ_HI + z) for x, z in TP]


def from_later_chip(steps):
    return [
        (NCORE * (chip + steps) + core, NCORE * chip + core)
        for chip in range(CHIPS - steps)
        for core in range(NCORE)
    ]


def shifted_rows(line, rows):
    block = jnp.broadcast_to(line, (rows, line.shape[1]))
    return pltpu.roll(block, 0, 1, stride=1, stride_axis=0).astype(BF16)


def table_kernel(_, filters_ref, near_ref):
    filt_count, rows, near = near_ref.shape
    edge = jnp.zeros((1, LANE), F32)
    for k in range(filt_count):
        line = filters_ref[k : k + 1, :near].astype(F32)
        near_ref[k] = shifted_rows(jnp.concatenate([line, edge], axis=1), rows)[:, :near]


def near_table(after, filters):
    filt_count, taps = filters.shape
    vmem = pl.BlockSpec(memory_space=pltpu.VMEM)
    return pl.pallas_call(
        table_kernel,
        out_shape=jax.ShapeDtypeStruct((filt_count, ROWS, taps // 2), BF16),
        in_specs=[pl.BlockSpec(memory_space=pl.ANY), vmem],
        out_specs=vmem,
        compiler_params=pltpu.CompilerParams(vmem_limit_bytes=VMEM_LIMIT),
        cost_estimate=SMALL_COST,
        name="near_table",
    )(after, filters)


def prep_kernel(pos_ref, _, own_ref, r1_ref, r2_ref, r3_ref, r4_ref, stack_ref, held_ref, arrived):
    copy = pltpu.make_async_copy(own_ref, held_ref, arrived)
    copy.start()
    parts = r1_ref, r2_ref, r3_ref, r4_ref
    core = lax.rem(pos_ref[1], NCORE)
    for s in range(1, stack_ref.shape[0]):
        stack_ref[s] = jnp.where(core == 0, parts[s][...], parts[s - 1][...])
    copy.wait()
    stack_ref[0] = jnp.where(core == 0, r1_ref[...], held_ref[...])


def for_sibling(pos, after, *parts):
    block = parts[0].shape
    vmem = pl.BlockSpec(memory_space=pltpu.VMEM)
    return pl.pallas_call(
        prep_kernel,
        out_shape=jax.ShapeDtypeStruct((4,) + block, BF16),
        in_specs=[pl.BlockSpec(memory_space=pltpu.SMEM)]
        + [pl.BlockSpec(memory_space=pl.ANY)] * 2
        + [vmem] * 4,
        out_specs=vmem,
        scratch_shapes=[pltpu.VMEM(block, BF16), pltpu.SemaphoreType.DMA],
        compiler_params=pltpu.CompilerParams(vmem_limit_bytes=VMEM_LIMIT),
        cost_estimate=SMALL_COST,
        name="for_sibling",
    )(pos, after, *parts)


def pair_of_blocks(grad_ref, start, rows, width):
    first = grad_ref[pl.ds(start, width), :]
    second = grad_ref[pl.ds(start + rows, width), :]
    return jnp.concatenate([first, second], axis=1)


def coords(pos_ref):
    x, z_hi = pos_ref[0] // NZ_HI, lax.rem(pos_ref[0], NZ_HI)
    chip, core = pos_ref[1] // NCORE, lax.rem(pos_ref[1], NCORE)
    return x, z_hi, chip // NZ_LO, lax.rem(chip, NZ_LO), core


def lay_out(grad_ref, refs):
    tok = refs[0].shape[0]
    for s, part in enumerate(refs):
        grad_ref[s * tok : (s + 1) * tok, :] = part[...]


def near_kernel(table_ref, own_ref, r1_ref, r2_ref, sib_ref, *refs):
    acc_refs, grad_ref = refs[:-1], refs[-1]
    filt_count, rows, width = table_ref.shape
    tok = own_ref.shape[0]
    lay_out(grad_ref, (own_ref, sib_ref.at[0], r1_ref, sib_ref.at[1], r2_ref))
    table = table_ref[...].reshape(filt_count * rows, width)

    @pl.loop(0, tok // (2 * rows), unroll=True)
    def _(pair):
        start = pl.multiple_of(pair * (2 * rows), 2 * rows)
        both = pair_of_blocks(grad_ref, start, rows, width)
        result = jnp.dot(table, both, preferred_element_type=F32)
        part = acc_refs[0].shape[1]
        for group, acc_ref in enumerate(acc_refs):
            acc_ref[pair] = result[group * part : (group + 1) * part]


def near_conv(after, table, halo, sibling, groups):
    filt_count, rows, width = table.shape
    tok = halo[0].shape[0]
    vmem = pl.BlockSpec(memory_space=pltpu.VMEM)
    acc = jax.ShapeDtypeStruct((tok // (2 * rows), filt_count // groups * rows, 2 * LANE), F32)
    return pl.pallas_call(
        near_kernel,
        out_shape=[acc] * groups,
        in_specs=[pl.BlockSpec(memory_space=pl.ANY)] * len(after) + [vmem] * 5,
        out_specs=[vmem] * groups,
        scratch_shapes=[pltpu.VMEM((5 * tok, LANE), BF16)],
        compiler_params=pltpu.CompilerParams(vmem_limit_bytes=VMEM_LIMIT),
        cost_estimate=LARGE_COST,
        name="near_conv",
    )(*after, table, *halo, sibling)


def far_kernel(
    first, _, filters_ref, acc_ref, r2_ref, r3_ref, r4_ref, sib_ref,
    corr_ref, grad_ref, table_ref,
):
    filt_count, rows, width = table_ref.shape
    tok = r2_ref.shape[0]
    edge = jnp.zeros((1, LANE), F32)
    start = filters_ref.shape[1] + LANE - width - LANE
    for k in range(filt_count):
        line = filters_ref[first + k : first + k + 1, start:].astype(F32)
        table_ref[k] = shifted_rows(jnp.concatenate([line, edge], axis=1), rows)[:, LANE:]
    lay_out(grad_ref, (r2_ref, sib_ref.at[2], r3_ref, sib_ref.at[3], r4_ref))
    grad_ref[5 * tok :, :] = jnp.zeros((grad_ref.shape[0] - 5 * tok, LANE), BF16)

    @pl.loop(0, tok // (2 * rows), unroll=True)
    def _(pair):
        start = pl.multiple_of(pair * (2 * rows), 2 * rows)
        both = pair_of_blocks(grad_ref, start, rows, width)
        table = table_ref[...].reshape(filt_count * rows, width)
        result = jnp.dot(table, both, preferred_element_type=F32)
        result = (result + acc_ref[pair]).astype(BF16)
        for k in range(filt_count):
            for half in range(2):
                corr_ref[pl.ds(start + half * rows, rows), k * LANE : (k + 1) * LANE] = result[
                    k * rows : (k + 1) * rows, half * LANE : (half + 1) * LANE
                ]


def far_conv(first, count, after, filters, acc, halo, sibling):
    tok = halo[0].shape[0]
    width = filters.shape[1] // 2 + LANE
    vmem = pl.BlockSpec(memory_space=pltpu.VMEM)
    return pl.pallas_call(
        functools.partial(far_kernel, first),
        out_shape=jax.ShapeDtypeStruct((tok, count * LANE), BF16),
        in_specs=[pl.BlockSpec(memory_space=pl.ANY)] + [vmem] * 6,
        out_specs=vmem,
        scratch_shapes=[
            pltpu.VMEM((5 * tok + ROWS, LANE), BF16),
            pltpu.VMEM((count, ROWS, width), BF16),
        ],
        compiler_params=pltpu.CompilerParams(vmem_limit_bytes=VMEM_LIMIT),
        cost_estimate=SMALL_COST,
        name="far_conv",
    )(after, filters, acc, *halo, sibling)


def gathered_columns(pos_ref, part_refs, full_ref):
    x, z_hi = coords(pos_ref)[:2]
    for s, part in enumerate(part_refs):
        for h in range(NZ_HI):
            at = lax.rem(x + NX - s, NX) * NZ_HI + lax.rem(z_hi + h, NZ_HI)
            full_ref[:, pl.ds(pl.multiple_of(at * LANE, LANE), LANE)] = part[h]


def products(crossed, pos_ref, corr_ref, full_ref, out_refs):
    y, z_lo, core = coords(pos_ref)[2:]
    stay_ref, leave_ref, send_stay_ref, send_leave_ref = out_refs
    deep = NZ_LO * NCORE * 32
    for s, at in enumerate(ring_slots(y, crossed)):
        part = full_ref[:, pl.ds(pl.multiple_of(at * deep, deep), deep)]
        result = lax.dot_general(
            part, corr_ref[...], (((0,), (0,)), ((), ())), preferred_element_type=F32
        ).astype(BF16)
        keep_ref, send_ref = (stay_ref, send_stay_ref) if s < 2 else (leave_ref, send_leave_ref)
        for z in range(NZ_LO):
            shift = z ^ z_lo
            slot = lax.rem(shift, 2) * 2 + shift // 2
            for k in range(keep_ref.shape[2]):
                columns = slice(k * LANE, (k + 1) * LANE)
                even = result[z * 64 : z * 64 + 32, columns]
                odd = result[z * 64 + 32 : z * 64 + 64, columns]
                keep_ref[s % 2, slot, k] = jnp.where(core == 0, even, odd)
                send_ref[s % 2, slot, k] = jnp.where(core == 0, odd, even)


def first_product_kernel(crossed, pos_ref, _, corr_ref, x0_ref, x1_ref, x2_ref, x3_ref, full_ref, *out_refs):
    gathered_columns(pos_ref, (x0_ref, x1_ref, x2_ref, x3_ref), full_ref)
    products(crossed, pos_ref, corr_ref, full_ref, out_refs)


def next_product_kernel(crossed, pos_ref, _, corr_ref, full_ref, *out_refs):
    products(crossed, pos_ref, corr_ref, full_ref, out_refs)


def product(kernel, crossed, pos, after, corr, sources, keep_full):
    tok, width = corr.shape
    part = jax.ShapeDtypeStruct((2, NZ_LO, width // LANE, 32, LANE), BF16)
    vmem = pl.BlockSpec(memory_space=pltpu.VMEM)
    full = [jax.ShapeDtypeStruct((tok, 1024), BF16)] if keep_full else []
    outs = full + [part] * 4
    return pl.pallas_call(
        functools.partial(kernel, crossed),
        out_shape=outs,
        in_specs=[pl.BlockSpec(memory_space=pltpu.SMEM), pl.BlockSpec(memory_space=pl.ANY)]
        + [vmem] * (1 + len(sources)),
        out_specs=[vmem] * len(outs),
        compiler_params=pltpu.CompilerParams(vmem_limit_bytes=VMEM_LIMIT),
        cost_estimate=SMALL_COST,
        name="product",
    )(pos, after, corr, *sources)


def halve_three_kernel(_, mine_ref, beside_ref, other_ref, stay_ref, leave_ref):
    half = leave_ref.shape[0]
    for out_ref, rows in ((stay_ref, slice(0, half)), (leave_ref, slice(half, 2 * half))):
        total = mine_ref[rows].astype(F32) + beside_ref[rows].astype(F32)
        out_ref[...] = (total + other_ref[rows].astype(F32)).astype(out_ref.dtype)


def halve_three(after, mine, beside, other):
    half = (mine.shape[0] // 2,) + mine.shape[1:]
    vmem = pl.BlockSpec(memory_space=pltpu.VMEM)
    return pl.pallas_call(
        halve_three_kernel,
        out_shape=(jax.ShapeDtypeStruct(half, F32), jax.ShapeDtypeStruct(half, BF16)),
        in_specs=[pl.BlockSpec(memory_space=pl.ANY), vmem, vmem, vmem],
        out_specs=(vmem, vmem),
        compiler_params=pltpu.CompilerParams(vmem_limit_bytes=VMEM_LIMIT),
        cost_estimate=SMALL_COST,
        name="halve_three",
    )(after, mine, beside, other)


def halve_kernel(_, mine_ref, other_ref, stay_ref, leave_ref):
    half = leave_ref.shape[0]
    stay_ref[...] = mine_ref[:half].astype(F32) + other_ref[:half].astype(F32)
    leave_ref[...] = (mine_ref[half:].astype(F32) + other_ref[half:].astype(F32)).astype(BF16)


def halve(after, mine, other, cost=SMALL_COST):
    half = (mine.shape[0] // 2,) + mine.shape[1:]
    vmem = pl.BlockSpec(memory_space=pltpu.VMEM)
    return pl.pallas_call(
        halve_kernel,
        out_shape=(jax.ShapeDtypeStruct(half, F32), jax.ShapeDtypeStruct(half, BF16)),
        in_specs=[pl.BlockSpec(memory_space=pl.ANY), vmem, vmem],
        out_specs=(vmem, vmem),
        compiler_params=pltpu.CompilerParams(vmem_limit_bytes=VMEM_LIMIT),
        cost_estimate=cost,
        name="halve",
    )(after, mine, other)


def add_kernel(_, mine_ref, other_ref, sum_ref):
    sum_ref[...] = (mine_ref[...].astype(F32) + other_ref[...].astype(F32)).astype(BF16)


def add(after, mine, other, cost=SMALL_COST):
    vmem = pl.BlockSpec(memory_space=pltpu.VMEM)
    return pl.pallas_call(
        add_kernel,
        out_shape=jax.ShapeDtypeStruct(mine.shape, BF16),
        in_specs=[pl.BlockSpec(memory_space=pl.ANY), vmem, vmem],
        out_specs=vmem,
        compiler_params=pltpu.CompilerParams(vmem_limit_bytes=VMEM_LIMIT),
        cost_estimate=cost,
        name="add",
    )(after, mine, other)


def join_kernel(_, *refs):
    at, sum_ref = 0, refs[-1]
    for mine_ref, other_ref in zip(refs[0:-1:2], refs[1:-1:2]):
        count = mine_ref.shape[1]
        sum_ref[at : at + count] = mine_ref[0] + other_ref[0].astype(F32)
        at += count


def join(after, *pairs):
    counts = [mine.shape[1] for mine, _ in pairs]
    rest = pairs[0][0].shape[2:]
    vmem = pl.BlockSpec(memory_space=pltpu.VMEM)
    return pl.pallas_call(
        join_kernel,
        out_shape=jax.ShapeDtypeStruct((sum(counts),) + rest, F32),
        in_specs=[pl.BlockSpec(memory_space=pl.ANY)] + [vmem] * (2 * len(pairs)),
        out_specs=vmem,
        compiler_params=pltpu.CompilerParams(vmem_limit_bytes=VMEM_LIMIT),
        cost_estimate=SMALL_COST,
        name="join",
    )(after, *[part for pair in pairs for part in pair])


def share_kernel(pos_ref, _, *refs):
    corr_refs, proj_ref = refs[:-6], refs[-6]
    near_keep, near_send, far_keep, far_send, all_ref = refs[-5:]
    filt_count = proj_ref.shape[0]
    x, z_hi = coords(pos_ref)[:2]
    at = 0
    for part in corr_refs:
        all_ref[:, at : at + part.shape[1]] = part[...]
        at += part.shape[1]
    wide = NZ_HI * LANE
    near_slots = (near_keep, 0), (near_send, 0), (near_keep, 1), (near_send, 1)
    far_slots = (far_keep, 0), (far_keep, 1), (far_send, 0), (far_send, 1)
    for at, near, far in zip(ring_slots(x, False), near_slots, far_slots):
        base = pl.multiple_of(at * wide, wide)
        weights = jnp.concatenate(
            [proj_ref[k, pl.ds(base, wide), :] for k in range(filt_count)], axis=1
        )
        result = lax.dot_general(
            all_ref[...], weights, (((1,), (1,)), ((), ())), preferred_element_type=F32
        )
        low, high = result[:, :LANE], result[:, LANE:]
        near[0][near[1]] = jnp.where(z_hi == 0, low, high).astype(near[0].dtype)
        far[0][far[1]] = jnp.where(z_hi == 0, high, low).astype(far[0].dtype)


def input_shares(pos, after, corrs, projection):
    tok = corrs[0].shape[0]
    filt_count = projection.shape[0]
    vmem = pl.BlockSpec(memory_space=pltpu.VMEM)
    keep = jax.ShapeDtypeStruct((2, tok, LANE), F32)
    send = jax.ShapeDtypeStruct((2, tok, LANE), BF16)
    return pl.pallas_call(
        share_kernel,
        out_shape=(keep, send, keep, send),
        in_specs=[pl.BlockSpec(memory_space=pltpu.SMEM), pl.BlockSpec(memory_space=pl.ANY)]
        + [vmem] * (len(corrs) + 1),
        out_specs=(vmem,) * 4,
        scratch_shapes=[pltpu.VMEM((tok, filt_count * LANE), BF16)],
        compiler_params=pltpu.CompilerParams(vmem_limit_bytes=VMEM_LIMIT),
        cost_estimate=SMALL_COST,
        name="input_shares",
    )(pos, after, *corrs, projection)


GROUPS = 2


def per_device(inputs, grad_out, filters, projection):
    tp, ctx = lax.axis_index("tp"), lax.axis_index("ctx")
    pos = jnp.stack([tp, ctx]).astype(jnp.int32)

    def later(value, steps):
        return lax.ppermute(value, "ctx", from_later_chip(steps))

    def sibling(value):
        return lax.ppermute(value, "ctx", CORE_SWAP)

    def y_swapped(value, crossed):
        return lax.ppermute(value, "ctx", y_swap(crossed))

    def z_swapped(value, bit):
        return lax.ppermute(value, "ctx", z_swap(bit))

    def x_swapped(value, crossed):
        return lax.ppermute(value, "tp", x_swap(crossed))

    count = filters.shape[0] // GROUPS
    pair = jnp.stack([inputs, lax.ppermute(inputs, "tp", Z_HI_SWAP)])
    gathered = [pair] + [lax.ppermute(pair, "tp", along_x(s)) for s in range(1, NX)]
    table = near_table(pair, filters)
    halo = [grad_out] + [later(grad_out, steps) for steps in range(1, 5)]
    beside = sibling(for_sibling(pos, table, *halo))
    accs = near_conv(gathered[1:1], table, halo[:3], beside, GROUPS)

    def conv(group, after):
        return far_conv(group * count, count, after, filters, accs[group], halo[2:], beside)

    corr_0 = conv(0, table)
    corr_1 = conv(1, corr_0)
    near, near_send, far, far_send = input_shares(
        pos, corr_1, [corr_0, corr_1], projection.transpose(1, 0, 2)
    )
    x_far, x_near = x_swapped(far_send, False), x_swapped(near_send, True)
    full, stay_0, leave_0, send_stay_0, send_leave_0 = product(
        first_product_kernel, False, pos, near_send, corr_0, gathered, True
    )
    stay_1, leave_1, send_stay_1, send_leave_1 = product(
        next_product_kernel, True, pos, send_leave_0, corr_1, [full], False
    )
    leave_0 = add(send_leave_1, leave_0, sibling(send_leave_0))
    y_0 = y_swapped(leave_0, False)
    leave_1 = add(leave_0, leave_1, sibling(send_leave_1))
    y_1 = y_swapped(leave_1, True)
    beside_0, beside_1 = sibling(send_stay_0), sibling(send_stay_1)
    far, leave = halve(leave_1, far, x_far, LARGE_COST)
    x_far = x_swapped(leave, True)
    stay_0, leave_0 = halve_three(leave, stay_0, beside_0, y_0)
    y_0 = y_swapped(leave_0, True)
    stay_1, leave_1 = halve_three(leave_0, stay_1, beside_1, y_1)
    y_1 = y_swapped(leave_1, False)
    far = add(leave_1, far, x_far, LARGE_COST)
    opposite = lax.ppermute(far, "tp", Z_HI_SWAP)
    near, leave = halve(far, near, x_near)
    x_near = x_swapped(leave, False)
    stay_0, leave_0 = halve(leave, stay_0[0], y_0[0])
    z_0 = z_swapped(leave_0, 1)
    stay_1, leave_1 = halve(leave_0, stay_1[0], y_1[0])
    z_1 = z_swapped(leave_1, 1)
    stay_0, leave_0 = halve(leave_1, stay_0, z_0)
    z_0 = z_swapped(leave_0, 2)
    stay_1, leave_1 = halve(leave_0, stay_1, z_1)
    z_1 = z_swapped(leave_1, 2)
    grad_proj = join(near, (stay_0, z_0), (stay_1, z_1)).transpose(1, 0, 2)
    total = near[0] + x_near[0].astype(F32) + opposite[0].astype(F32)
    return total.astype(BF16), grad_proj


def solution(mesh):
    return jax.shard_map(
        per_device,
        mesh=mesh,
        in_specs=(P("ctx", "tp"), P("ctx", "tp"), P(), P(None, None, "tp")),
        out_specs=(P("ctx", "tp"), P("ctx", None, "tp")),
        check_vma=False,
    )
```

```python
import functools

import jax
import jax.numpy as jnp
from jax import lax
from jax.experimental import pallas as pl
from jax.experimental.pallas import tpu as pltpu
from jax.sharding import PartitionSpec as P

BF16, F32 = jnp.bfloat16, jnp.float32
ROWS = 64
LANE = 128
NX, NZ_HI, NY, NZ_LO, NCORE = 4, 2, 4, 4, 2
CHIPS = NY * NZ_LO
VMEM_LIMIT = 20 * 1024 * 1024
LARGE_COST = pl.CostEstimate(flops=4_000_000_000, bytes_accessed=8_000_000, transcendentals=0)
SMALL_COST = pl.CostEstimate(flops=1000, bytes_accessed=1000, transcendentals=0)


def ctx_of(y, z, core):
    return (y * NZ_LO + z) * NCORE + core


CTX = [(y, z, core) for y in range(NY) for z in range(NZ_LO) for core in range(NCORE)]
TP = [(x, z) for x in range(NX) for z in range(NZ_HI)]
CORE_SWAP = [(ctx_of(y, z, c), ctx_of(y, z, 1 - c)) for y, z, c in CTX]
Z_HI_SWAP = [(x * NZ_HI + z, x * NZ_HI + 1 - z) for x, z in TP]


def ring_partner(at, crossed):
    return NX - 1 - at if crossed else at ^ 1


def ring_slots(at, crossed):
    near, far = ring_partner(at, crossed), ring_partner(at, not crossed)
    return at, far, near, ring_partner(near, not crossed)


def y_swap(crossed):
    return [(ctx_of(y, z, c), ctx_of(ring_partner(y, crossed), z, c)) for y, z, c in CTX]


def x_swap(crossed):
    return [(x * NZ_HI + z, ring_partner(x, crossed) * NZ_HI + z) for x, z in TP]


def z_swap(bit):
    return [(ctx_of(y, z, c), ctx_of(y, z ^ bit, c)) for y, z, c in CTX]


def along_x(steps):
    return [(x * NZ_HI + z, (x + steps) % NX * NZ_HI + z) for x, z in TP]


def from_later_chip(steps):
    return [
        (NCORE * (chip + steps) + core, NCORE * chip + core)
        for chip in range(CHIPS - steps)
        for core in range(NCORE)
    ]


def shifted_rows(line, rows):
    block = jnp.broadcast_to(line, (rows, line.shape[1]))
    return pltpu.roll(block, 0, 1, stride=1, stride_axis=0).astype(BF16)


def table_kernel(_, filters_ref, near_ref):
    filt_count, rows, near = near_ref.shape
    edge = jnp.zeros((1, LANE), F32)
    for k in range(filt_count):
        line = filters_ref[k : k + 1, :near].astype(F32)
        near_ref[k] = shifted_rows(jnp.concatenate([line, edge], axis=1), rows)[:, :near]


def near_table(after, filters):
    filt_count, taps = filters.shape
    vmem = pl.BlockSpec(memory_space=pltpu.VMEM)
    return pl.pallas_call(
        table_kernel,
        out_shape=jax.ShapeDtypeStruct((filt_count, ROWS, taps // 2), BF16),
        in_specs=[pl.BlockSpec(memory_space=pl.ANY), vmem],
        out_specs=vmem,
        compiler_params=pltpu.CompilerParams(vmem_limit_bytes=VMEM_LIMIT),
        cost_estimate=SMALL_COST,
        name="near_table",
    )(after, filters)


def prep_kernel(pos_ref, _, own_ref, r1_ref, r2_ref, r3_ref, r4_ref, stack_ref, held_ref, arrived):
    copy = pltpu.make_async_copy(own_ref, held_ref, arrived)
    copy.start()
    parts = r1_ref, r2_ref, r3_ref, r4_ref
    core = lax.rem(pos_ref[1], NCORE)
    for s in range(1, stack_ref.shape[0]):
        stack_ref[s] = jnp.where(core == 0, parts[s][...], parts[s - 1][...])
    copy.wait()
    stack_ref[0] = jnp.where(core == 0, r1_ref[...], held_ref[...])


def for_sibling(pos, after, *parts):
    block = parts[0].shape
    vmem = pl.BlockSpec(memory_space=pltpu.VMEM)
    return pl.pallas_call(
        prep_kernel,
        out_shape=jax.ShapeDtypeStruct((4,) + block, BF16),
        in_specs=[pl.BlockSpec(memory_space=pltpu.SMEM)]
        + [pl.BlockSpec(memory_space=pl.ANY)] * 2
        + [vmem] * 4,
        out_specs=vmem,
        scratch_shapes=[pltpu.VMEM(block, BF16), pltpu.SemaphoreType.DMA],
        compiler_params=pltpu.CompilerParams(vmem_limit_bytes=VMEM_LIMIT),
        cost_estimate=SMALL_COST,
        name="for_sibling",
    )(pos, after, *parts)


def pair_of_blocks(grad_ref, start, rows, width):
    first = grad_ref[pl.ds(start, width), :]
    second = grad_ref[pl.ds(start + rows, width), :]
    return jnp.concatenate([first, second], axis=1)


def coords(pos_ref):
    x, z_hi = pos_ref[0] // NZ_HI, lax.rem(pos_ref[0], NZ_HI)
    chip, core = pos_ref[1] // NCORE, lax.rem(pos_ref[1], NCORE)
    return x, z_hi, chip // NZ_LO, lax.rem(chip, NZ_LO), core


def lay_out(grad_ref, refs):
    tok = refs[0].shape[0]
    for s, part in enumerate(refs):
        grad_ref[s * tok : (s + 1) * tok, :] = part[...]


def near_kernel(table_ref, own_ref, r1_ref, r2_ref, sib_ref, *refs):
    acc_refs, grad_ref = refs[:-1], refs[-1]
    filt_count, rows, width = table_ref.shape
    tok = own_ref.shape[0]
    lay_out(grad_ref, (own_ref, sib_ref.at[0], r1_ref, sib_ref.at[1], r2_ref))
    table = table_ref[...].reshape(filt_count * rows, width)

    @pl.loop(0, tok // (2 * rows), unroll=True)
    def _(pair):
        start = pl.multiple_of(pair * (2 * rows), 2 * rows)
        both = pair_of_blocks(grad_ref, start, rows, width)
        result = jnp.dot(table, both, preferred_element_type=F32)
        part = acc_refs[0].shape[1]
        for group, acc_ref in enumerate(acc_refs):
            acc_ref[pair] = result[group * part : (group + 1) * part]


def near_conv(after, table, halo, sibling, groups):
    filt_count, rows, width = table.shape
    tok = halo[0].shape[0]
    vmem = pl.BlockSpec(memory_space=pltpu.VMEM)
    acc = jax.ShapeDtypeStruct((tok // (2 * rows), filt_count // groups * rows, 2 * LANE), F32)
    return pl.pallas_call(
        near_kernel,
        out_shape=[acc] * groups,
        in_specs=[pl.BlockSpec(memory_space=pl.ANY)] * len(after) + [vmem] * 5,
        out_specs=[vmem] * groups,
        scratch_shapes=[pltpu.VMEM((5 * tok, LANE), BF16)],
        compiler_params=pltpu.CompilerParams(vmem_limit_bytes=VMEM_LIMIT),
        cost_estimate=LARGE_COST,
        name="near_conv",
    )(*after, table, *halo, sibling)


def far_kernel(
    first, _, filters_ref, acc_ref, r2_ref, r3_ref, r4_ref, sib_ref,
    corr_ref, grad_ref, table_ref,
):
    filt_count, rows, width = table_ref.shape
    tok = r2_ref.shape[0]
    edge = jnp.zeros((1, LANE), F32)
    start = filters_ref.shape[1] + LANE - width - LANE
    for k in range(filt_count):
        line = filters_ref[first + k : first + k + 1, start:].astype(F32)
        table_ref[k] = shifted_rows(jnp.concatenate([line, edge], axis=1), rows)[:, LANE:]
    lay_out(grad_ref, (r2_ref, sib_ref.at[2], r3_ref, sib_ref.at[3], r4_ref))
    grad_ref[5 * tok :, :] = jnp.zeros((grad_ref.shape[0] - 5 * tok, LANE), BF16)

    @pl.loop(0, tok // (2 * rows), unroll=True)
    def _(pair):
        start = pl.multiple_of(pair * (2 * rows), 2 * rows)
        both = pair_of_blocks(grad_ref, start, rows, width)
        table = table_ref[...].reshape(filt_count * rows, width)
        result = jnp.dot(table, both, preferred_element_type=F32)
        result = (result + acc_ref[pair]).astype(BF16)
        for k in range(filt_count):
            for half in range(2):
                corr_ref[pl.ds(start + half * rows, rows), k * LANE : (k + 1) * LANE] = result[
                    k * rows : (k + 1) * rows, half * LANE : (half + 1) * LANE
                ]


def far_conv(first, count, after, filters, acc, halo, sibling):
    tok = halo[0].shape[0]
    width = filters.shape[1] // 2 + LANE
    vmem = pl.BlockSpec(memory_space=pltpu.VMEM)
    return pl.pallas_call(
        functools.partial(far_kernel, first),
        out_shape=jax.ShapeDtypeStruct((tok, count * LANE), BF16),
        in_specs=[pl.BlockSpec(memory_space=pl.ANY)] + [vmem] * 6,
        out_specs=vmem,
        scratch_shapes=[
            pltpu.VMEM((5 * tok + ROWS, LANE), BF16),
            pltpu.VMEM((count, ROWS, width), BF16),
        ],
        compiler_params=pltpu.CompilerParams(vmem_limit_bytes=VMEM_LIMIT),
        cost_estimate=SMALL_COST,
        name="far_conv",
    )(after, filters, acc, *halo, sibling)


def gathered_columns(pos_ref, part_refs, full_ref):
    x, z_hi = coords(pos_ref)[:2]
    for s, part in enumerate(part_refs):
        for h in range(NZ_HI):
            at = lax.rem(x + NX - s, NX) * NZ_HI + lax.rem(z_hi + h, NZ_HI)
            full_ref[:, pl.ds(pl.multiple_of(at * LANE, LANE), LANE)] = part[h]


def products(crossed, pos_ref, corr_ref, full_ref, slots):
    y, z_lo, core = coords(pos_ref)[2:]
    deep = NZ_LO * NCORE * 32
    for at, (keep_ref, send_ref, s) in zip(ring_slots(y, crossed), slots):
        part = full_ref[:, pl.ds(pl.multiple_of(at * deep, deep), deep)]
        result = lax.dot_general(
            part, corr_ref[...], (((0,), (0,)), ((), ())), preferred_element_type=F32
        ).astype(BF16)
        for z in range(NZ_LO):
            shift = z ^ z_lo
            slot = lax.rem(shift, 2) * 2 + shift // 2
            for k in range(keep_ref.shape[2]):
                columns = slice(k * LANE, (k + 1) * LANE)
                even = result[z * 64 : z * 64 + 32, columns]
                odd = result[z * 64 + 32 : z * 64 + 64, columns]
                keep_ref[s, slot, k] = jnp.where(core == 0, even, odd)
                send_ref[s, slot, k] = jnp.where(core == 0, odd, even)


def first_product_kernel(
    crossed, pos_ref, _, corr_ref, x0_ref, x1_ref, x2_ref, x3_ref, full_ref, keep_ref, send_ref
):
    gathered_columns(pos_ref, (x0_ref, x1_ref, x2_ref, x3_ref), full_ref)
    products(crossed, pos_ref, corr_ref, full_ref, [(keep_ref, send_ref, s) for s in range(NY)])


def last_product_kernel(
    crossed, pos_ref, _, corr_ref, full_ref, stay_ref, leave_ref, send_stay_ref, send_leave_ref
):
    slots = [(stay_ref, send_stay_ref, s) for s in range(2)]
    slots += [(leave_ref, send_leave_ref, s) for s in range(2)]
    products(crossed, pos_ref, corr_ref, full_ref, slots)


def product(kernel, crossed, pos, after, corr, sources, first):
    tok, width = corr.shape
    rest = (NZ_LO, width // LANE, 32, LANE)
    vmem = pl.BlockSpec(memory_space=pltpu.VMEM)
    outs = [jax.ShapeDtypeStruct((2,) + rest, BF16)] * 4
    if first:
        outs = [jax.ShapeDtypeStruct((tok, 1024), BF16)]
        outs += [jax.ShapeDtypeStruct((NY,) + rest, BF16)] * 2
    return pl.pallas_call(
        functools.partial(kernel, crossed),
        out_shape=outs,
        in_specs=[pl.BlockSpec(memory_space=pltpu.SMEM), pl.BlockSpec(memory_space=pl.ANY)]
        + [vmem] * (1 + len(sources)),
        out_specs=[vmem] * len(outs),
        compiler_params=pltpu.CompilerParams(vmem_limit_bytes=VMEM_LIMIT),
        cost_estimate=SMALL_COST,
        name="product",
    )(pos, after, corr, *sources)


def halve_three_kernel(_, mine_ref, beside_ref, other_ref, stay_ref, leave_ref):
    half = leave_ref.shape[0]
    for out_ref, rows in ((stay_ref, slice(0, half)), (leave_ref, slice(half, 2 * half))):
        total = mine_ref[rows].astype(F32) + beside_ref[rows].astype(F32)
        out_ref[...] = (total + other_ref[rows].astype(F32)).astype(out_ref.dtype)


def halve_three(after, mine, beside, other):
    half = (mine.shape[0] // 2,) + mine.shape[1:]
    vmem = pl.BlockSpec(memory_space=pltpu.VMEM)
    return pl.pallas_call(
        halve_three_kernel,
        out_shape=(jax.ShapeDtypeStruct(half, F32), jax.ShapeDtypeStruct(half, BF16)),
        in_specs=[pl.BlockSpec(memory_space=pl.ANY), vmem, vmem, vmem],
        out_specs=(vmem, vmem),
        compiler_params=pltpu.CompilerParams(vmem_limit_bytes=VMEM_LIMIT),
        cost_estimate=SMALL_COST,
        name="halve_three",
    )(after, mine, beside, other)


def halve_kernel(_, mine_ref, other_ref, stay_ref, leave_ref):
    half = leave_ref.shape[0]
    stay_ref[...] = mine_ref[:half].astype(F32) + other_ref[:half].astype(F32)
    leave_ref[...] = (mine_ref[half:].astype(F32) + other_ref[half:].astype(F32)).astype(BF16)


def halve(after, mine, other, cost=SMALL_COST):
    half = (mine.shape[0] // 2,) + mine.shape[1:]
    vmem = pl.BlockSpec(memory_space=pltpu.VMEM)
    return pl.pallas_call(
        halve_kernel,
        out_shape=(jax.ShapeDtypeStruct(half, F32), jax.ShapeDtypeStruct(half, BF16)),
        in_specs=[pl.BlockSpec(memory_space=pl.ANY), vmem, vmem],
        out_specs=(vmem, vmem),
        compiler_params=pltpu.CompilerParams(vmem_limit_bytes=VMEM_LIMIT),
        cost_estimate=cost,
        name="halve",
    )(after, mine, other)


def add_kernel(_, mine_ref, other_ref, sum_ref):
    sum_ref[...] = (mine_ref[...].astype(F32) + other_ref[...].astype(F32)).astype(BF16)


def add(after, mine, other, cost=SMALL_COST):
    vmem = pl.BlockSpec(memory_space=pltpu.VMEM)
    return pl.pallas_call(
        add_kernel,
        out_shape=jax.ShapeDtypeStruct(mine.shape, BF16),
        in_specs=[pl.BlockSpec(memory_space=pl.ANY), vmem, vmem],
        out_specs=vmem,
        compiler_params=pltpu.CompilerParams(vmem_limit_bytes=VMEM_LIMIT),
        cost_estimate=cost,
        name="add",
    )(after, mine, other)


def join_kernel(_, *refs):
    at, sum_ref = 0, refs[-1]
    for mine_ref, other_ref in zip(refs[0:-1:2], refs[1:-1:2]):
        count = mine_ref.shape[1]
        sum_ref[at : at + count] = mine_ref[0] + other_ref[0].astype(F32)
        at += count


def join(after, *pairs):
    counts = [mine.shape[1] for mine, _ in pairs]
    rest = pairs[0][0].shape[2:]
    vmem = pl.BlockSpec(memory_space=pltpu.VMEM)
    return pl.pallas_call(
        join_kernel,
        out_shape=jax.ShapeDtypeStruct((sum(counts),) + rest, F32),
        in_specs=[pl.BlockSpec(memory_space=pl.ANY)] + [vmem] * (2 * len(pairs)),
        out_specs=vmem,
        compiler_params=pltpu.CompilerParams(vmem_limit_bytes=VMEM_LIMIT),
        cost_estimate=SMALL_COST,
        name="join",
    )(after, *[part for pair in pairs for part in pair])


def share_kernel(pos_ref, _, *refs):
    corr_refs, proj_ref = refs[:-6], refs[-6]
    near_keep, near_send, far_keep, far_send, all_ref = refs[-5:]
    filt_count = proj_ref.shape[0]
    x, z_hi = coords(pos_ref)[:2]
    at = 0
    for part in corr_refs:
        all_ref[:, at : at + part.shape[1]] = part[...]
        at += part.shape[1]
    wide = NZ_HI * LANE
    near_slots = (near_keep, 0), (near_send, 0), (near_keep, 1), (near_send, 1)
    far_slots = (far_keep, 0), (far_keep, 1), (far_send, 0), (far_send, 1)
    for at, near, far in zip(ring_slots(x, False), near_slots, far_slots):
        base = pl.multiple_of(at * wide, wide)
        weights = jnp.concatenate(
            [proj_ref[k, pl.ds(base, wide), :] for k in range(filt_count)], axis=1
        )
        result = lax.dot_general(
            all_ref[...], weights, (((1,), (1,)), ((), ())), preferred_element_type=F32
        )
        low, high = result[:, :LANE], result[:, LANE:]
        near[0][near[1]] = jnp.where(z_hi == 0, low, high).astype(near[0].dtype)
        far[0][far[1]] = jnp.where(z_hi == 0, high, low).astype(far[0].dtype)


def input_shares(pos, after, corrs, projection):
    tok = corrs[0].shape[0]
    filt_count = projection.shape[0]
    vmem = pl.BlockSpec(memory_space=pltpu.VMEM)
    keep = jax.ShapeDtypeStruct((2, tok, LANE), F32)
    send = jax.ShapeDtypeStruct((2, tok, LANE), BF16)
    return pl.pallas_call(
        share_kernel,
        out_shape=(keep, send, keep, send),
        in_specs=[pl.BlockSpec(memory_space=pltpu.SMEM), pl.BlockSpec(memory_space=pl.ANY)]
        + [vmem] * (len(corrs) + 1),
        out_specs=(vmem,) * 4,
        scratch_shapes=[pltpu.VMEM((tok, filt_count * LANE), BF16)],
        compiler_params=pltpu.CompilerParams(vmem_limit_bytes=VMEM_LIMIT),
        cost_estimate=SMALL_COST,
        name="input_shares",
    )(pos, after, *corrs, projection)


GROUPS = 2


def per_device(inputs, grad_out, filters, projection):
    tp, ctx = lax.axis_index("tp"), lax.axis_index("ctx")
    pos = jnp.stack([tp, ctx]).astype(jnp.int32)

    def later(value, steps):
        return lax.ppermute(value, "ctx", from_later_chip(steps))

    def sibling(value):
        return lax.ppermute(value, "ctx", CORE_SWAP)

    def y_swapped(value, crossed):
        return lax.ppermute(value, "ctx", y_swap(crossed))

    def z_swapped(value, bit):
        return lax.ppermute(value, "ctx", z_swap(bit))

    def x_swapped(value, crossed):
        return lax.ppermute(value, "tp", x_swap(crossed))

    count = filters.shape[0] // GROUPS
    pair = jnp.stack([inputs, lax.ppermute(inputs, "tp", Z_HI_SWAP)])
    gathered = [pair] + [lax.ppermute(pair, "tp", along_x(s)) for s in range(1, NX)]
    table = near_table(pair, filters)
    halo = [grad_out] + [later(grad_out, steps) for steps in range(1, 5)]
    beside = sibling(for_sibling(pos, table, *halo))
    accs = near_conv(gathered[1:1], table, halo[:3], beside, GROUPS)

    def conv(group, after):
        return far_conv(group * count, count, after, filters, accs[group], halo[2:], beside)

    corr_0 = conv(0, table)
    corr_1 = conv(1, corr_0)
    near, near_send, far, far_send = input_shares(
        pos, corr_1, [corr_0, corr_1], projection.transpose(1, 0, 2)
    )
    x_far, x_near = x_swapped(far_send, False), x_swapped(near_send, True)
    full, keep_0, send_0 = product(
        first_product_kernel, False, pos, near_send, corr_0, gathered, True
    )
    stay_1, leave_1, send_stay_1, send_leave_1 = product(
        last_product_kernel, True, pos, send_0, corr_1, [full], False
    )
    stay_0, leave_0 = halve(send_leave_1, keep_0, sibling(send_0))
    y_0 = y_swapped(leave_0, False)
    leave_1 = add(leave_0, leave_1, sibling(send_leave_1))
    y_1 = y_swapped(leave_1, True)
    beside_1 = sibling(send_stay_1)
    far, leave = halve(leave_1, far, x_far, LARGE_COST)
    x_far = x_swapped(leave, True)
    near, leave = halve(leave, near, x_near)
    x_near = x_swapped(leave, False)
    stay_0, leave_0 = halve(leave, stay_0, y_0)
    y_0 = y_swapped(leave_0, True)
    stay_1, leave_1 = halve_three(leave_0, stay_1, beside_1, y_1)
    y_1 = y_swapped(leave_1, False)
    far = add(leave_1, far, x_far, LARGE_COST)
    opposite = lax.ppermute(far, "tp", Z_HI_SWAP)
    stay_0, leave_0 = halve(far, stay_0[0], y_0[0])
    z_0 = z_swapped(leave_0, 1)
    stay_1, leave_1 = halve(leave_0, stay_1[0], y_1[0])
    z_1 = z_swapped(leave_1, 1)
    stay_0, leave_0 = halve(leave_1, stay_0, z_0)
    z_0 = z_swapped(leave_0, 2)
    stay_1, leave_1 = halve(leave_0, stay_1, z_1)
    z_1 = z_swapped(leave_1, 2)
    grad_proj = join(near, (stay_0, z_0), (stay_1, z_1)).transpose(1, 0, 2)
    total = near[0] + x_near[0].astype(F32) + opposite[0].astype(F32)
    return total.astype(BF16), grad_proj


def solution(mesh):
    return jax.shard_map(
        per_device,
        mesh=mesh,
        in_specs=(P("ctx", "tp"), P("ctx", "tp"), P(), P(None, None, "tp")),
        out_specs=(P("ctx", "tp"), P("ctx", None, "tp")),
        check_vma=False,
    )
```
